32 devices in a mesh: section: 2 (over core), dp: 4 (over y, x), seq: 4 (over z).
Axes of the slice: x: 2, y: 2, z: 4, core: 2. Of those that a mesh axis runs over, the one named last changes fastest.
Arguments:
- layer_input: bfloat16 [2, 4, 1024, 768], P(None, 'dp', 'seq'), may hold values from -6 to 6
- out_cot: bfloat16 [2, 4, 1024, 768], P(None, 'dp', 'seq'), may hold values from -6 to 6
- doc_lengths: int32 [2, 4, 3], P(None, 'dp'), may hold values from 1 to 769, 1024 in all within a row
- norm_gains: bfloat16 [2, 2, 768], P('section'), may hold values from 0.5 to 1.5
- biases: bfloat16 [2, 4, 768], P('section'), may hold values from -1.796875 to 1.796875
- in_weight: bfloat16 [2, 768, 2304], P('section'), may hold values from -0.21875 to 0.21875
- mix_vecs: bfloat16 [2, 5, 2304], P('section'), may hold values from -3 to 3
- filt_first: bfloat16 [2, 33, 64], P('section'), may hold values from -1.5 to 1.5
- filt_inner_bias: bfloat16 [2, 2, 64], P('section'), may hold values from -3 to 3
- filt_second: bfloat16 [2, 64, 64], P('section'), may hold values from -1 to 1
- filt_last: bfloat16 [2, 64, 768], P('section'), may hold values from -0.059814453 to 0.059814453
- filt_skip: bfloat16 [2, 1, 768], P('section'), may hold values from -3 to 3
- out_weight: bfloat16 [2, 768, 768], P('section'), may hold values from -0.21875 to 0.21875
- up_weight: bfloat16 [2, 768, 3072], P('section'), may hold values from -0.21875 to 0.21875
- up_bias: bfloat16 [2, 1, 3072], P('section'), may hold values from -1.796875 to 1.796875
- down_weight: bfloat16 [2, 3072, 768], P('section'), may hold values from -0.109375 to 0.109375
Outputs:
- layer_output: float32 [2, 2, 4, 1024, 768], P('section', None, 'dp', 'seq')
- input_grad: float32 [2, 2, 4, 1024, 768], P('section', None, 'dp', 'seq')
- norm_gains_grad: float32 [2, 2, 768], P('section', None, ('dp', 'seq'))
- biases_grad: float32 [2, 4, 768], P('section', None, ('dp', 'seq'))
- in_weight_grad: float32 [2, 768, 2304], P('section', None, ('dp', 'seq'))
- mix_vecs_grad: float32 [2, 5, 2304], P('section', None, ('dp', 'seq'))
- filt_first_grad: float32 [2, 33, 64], P('section')
- filt_inner_bias_grad: float32 [2, 2, 64], P('section')
- filt_second_grad: float32 [2, 64, 64], P('section')
- filt_last_grad: float32 [2, 64, 768], P('section', None, ('dp', 'seq'))
- filt_skip_grad: float32 [2, 1, 768], P('section', None, ('dp', 'seq'))
- out_weight_grad: float32 [2, 768, 768], P('section', None, ('dp', 'seq'))
- up_weight_grad: float32 [2, 768, 3072], P('section', None, ('dp', 'seq'))
- up_bias_grad: float32 [2, 1, 3072], P('section', None, ('dp', 'seq'))
- down_weight_grad: float32 [2, 3072, 768], P('section', None, ('dp', 'seq'))
- penalty: float32 [], replicated
The draws below stay inside these ranges and needn't reach their ends.
Inputs may be any that keep to these rules, and one draw needn't show every extreme that they name: `doc_lengths`: each row's 3 lengths are positive and sum to 1024; one of them is exactly 769.
All inputs are finite; a program needn't handle non-finite values.
Results may differ from the reference program's by a relative error of at most 0.015.
Values may be sent and summed in bfloat16 or wider, within the bound.
No kernel may reach another device: no remote copies, remote signals or barrier semaphores. Data moves between devices by JAX's collectives and lax.ppermute only.
A program may use at most 384 MiB of HBM per device.

```python
import math
import jax
import jax.numpy as jnp
import numpy as np
from jax import lax

D = 768
FF = 3072
EMB = 33
FILT = 64
SEQ = 1024
MICRO = 2
NDOCS = 3
LAYERS = 2
BATCH = 4
SHARD = 256
CHAN = 192
LONG_LAG = 32


def level_of(rng, dims, split, least, largest):
    def one(axis_at, blocks):
        steps = jax.random.uniform(jax.random.fold_in(jax.random.fold_in(rng, 6), axis_at), (blocks,), jnp.float32, least / len(split), largest / len(split))
        return jnp.repeat(jnp.exp(steps), dims[axis_at] // blocks).reshape((-1,) + (1,) * (len(dims) - axis_at - 1))

    gain = one(*split[0])
    for cut in split[1:]:
        gain = gain * one(*cut)
    return gain


def length_profile(number_of, total, limit, slope):
    loads = [(1 << 20) // math.isqrt(grade ** slope) + 1 for grade in range(2, number_of + 1)]
    surplus, given = total - limit - (number_of - 1), [1] * (number_of - 1)
    while surplus > 0:
        candidates = [i for i in range(number_of - 1) if given[i] < limit]
        whole, remaining = sum([loads[i] for i in candidates]), surplus
        for i in candidates:
            more = min(limit - given[i], max(1, remaining * loads[i] // whole), surplus)
            given[i] = given[i] + more
            surplus = surplus - more
    return np.array([limit] + given)


def uneven(stream_key, amount, total, most, slope):
    if amount == 2:
        one = jax.random.randint(stream_key, (), max(1, total - most), min(most, total - 1) + 1)
        return jnp.stack([one, total - one])
    tallies = jnp.asarray(length_profile(amount, total, most, slope), jnp.int32)
    twos = (amount - 1) // 2
    donor, receiver = tallies[1:1 + 2 * twos:2], tallies[2:2 + 2 * twos:2]
    slack = jnp.minimum(donor - 1, most - receiver)
    passed = jax.random.randint(jax.random.fold_in(stream_key, 1), (twos,), 0, 1 << 20) % (slack + 1)
    tallies = tallies.at[1:1 + 2 * twos:2].set(donor - passed).at[2:2 + 2 * twos:2].set(receiver + passed)
    return tallies[jax.random.permutation(jax.random.fold_in(stream_key, 2), amount)]


def bell_draw(own_key, extent, width, most, cuts=(), held_as=jnp.bfloat16):
    drawn = width * jax.random.normal(own_key, extent, jnp.float32)
    if cuts:
        drawn = drawn * level_of(own_key, extent, cuts, -0.22, 0.18)
    return jnp.clip(drawn, -most, most).astype(held_as)


def setup_inputs(seed: int = 0) -> dict:
    seeds = jax.random.split(jax.random.key(seed), 17)
    return {
        "layer_input": bell_draw(seeds[0], (MICRO, BATCH, SEQ, D), 1.0, 6.0, ((1, 4), (2, 4))),
        "out_cot": bell_draw(seeds[1], (MICRO, BATCH, SEQ, D), 1.0, 6.0, ((1, 4), (2, 4))),
        "doc_lengths": jax.vmap(lambda own: uneven(own, NDOCS, SEQ, SEQ - SHARD + 1, 2))(jax.random.split(seeds[2], MICRO * BATCH)).reshape((MICRO, BATCH, NDOCS)).astype(jnp.int32),
        "norm_gains": jnp.clip(1.0 + 0.1 * jax.random.normal(seeds[3], (LAYERS, 2, D), jnp.float32), 0.5, 1.5).astype(jnp.bfloat16),
        "biases": bell_draw(seeds[4], (LAYERS, 4, D), 0.3, 1.796875, ((0, 2),)),
        "in_weight": bell_draw(seeds[5], (LAYERS, D, 3 * D), D ** -0.5, 0.21875, ((0, 2),)),
        "mix_vecs": bell_draw(seeds[6], (LAYERS, 5, 3 * D), 0.5, 3.0, ((0, 2),)),
        "filt_first": jnp.clip(jax.random.uniform(seeds[7], (LAYERS, EMB, FILT), jnp.float32, -1.5, 1.5) * level_of(seeds[7], (LAYERS, EMB, FILT), ((0, 2),), -0.4, 0.0), -1.5, 1.5).astype(jnp.bfloat16),
        "filt_inner_bias": bell_draw(seeds[8], (LAYERS, 2, FILT), 0.5, 3.0, ((0, 2),)),
        "filt_second": jnp.clip(jax.random.uniform(seeds[9], (LAYERS, FILT, FILT), jnp.float32, -1.0, 1.0) * level_of(seeds[9], (LAYERS, FILT, FILT), ((0, 2),), -0.4, 0.0), -1.0, 1.0).astype(jnp.bfloat16),
        "filt_last": bell_draw(seeds[10], (LAYERS, FILT, D), 0.01, 0.059814453, ((0, 2),)),
        "filt_skip": bell_draw(seeds[11], (LAYERS, 1, D), 0.5, 3.0, ((0, 2),)),
        "out_weight": bell_draw(seeds[12], (LAYERS, D, D), D ** -0.5, 0.21875, ((0, 2),)),
        "up_weight": bell_draw(seeds[13], (LAYERS, D, FF), D ** -0.5, 0.21875, ((0, 2),)),
        "up_bias": bell_draw(seeds[14], (LAYERS, 1, FF), 0.3, 1.796875, ((0, 2),)),
        "down_weight": bell_draw(seeds[15], (LAYERS, FF, D), FF ** -0.5, 0.109375, ((0, 2),)),
    }


@jax.custom_vjp
def low(v):
    return lax.optimization_barrier(v.astype(jnp.bfloat16)).astype(jnp.float32)

@jax.custom_vjp
def low_back(v):
    return v

def low_keep(v):
    return (low(v), None)

def low_pass(kept, grad):
    return (grad,)

def back_keep(v):
    return (v, None)

def back_low(kept, grad):
    return (low(grad),)
low.defvjp(low_keep, low_pass)
low_back.defvjp(back_keep, back_low)
eps = 1e-05

def matmul(left_op, right_op):
    return jnp.dot(left_op, right_op, precision=lax.Precision.HIGHEST)

def layer_norm(values, gain_vec, shift_vec):
    centre = lax.optimization_barrier(jnp.mean(values, axis=-1, keepdims=True))
    centred = values - centre
    variance = lax.optimization_barrier(jnp.mean(centred * centred, axis=-1, keepdims=True))
    return centred * lax.rsqrt(variance + eps) * gain_vec + shift_vec

def position_table():
    positions = jnp.arange(SEQ, dtype=jnp.float32)
    band_count = (EMB - 1) // 2
    band_freq = 0.0001 + jnp.arange(band_count, dtype=jnp.float32) * ((band_count - 1 - 0.0001) / (band_count - 1))
    angles = 2.0 * jnp.pi / SEQ * positions[:, None] * band_freq[None, :]
    return jnp.concatenate([(positions / SEQ)[:, None], jnp.cos(angles), jnp.sin(angles)], axis=1)

def decay_table(channels, offset):
    times = jnp.arange(SEQ, dtype=jnp.float32)[:, None] / SEQ
    chan_ids = (jnp.arange(channels, dtype=jnp.int32) + offset).astype(jnp.float32)
    rates = 3.0 + 12.0 * chan_ids / (D - 1)
    return jnp.exp(-times * rates[None, :])

def filter_taps(first_w, inner_b, second_w, last_w, decay_vals):
    pos_table = position_table()
    hidden = jnp.sin(matmul(pos_table, first_w) + inner_b[0])
    hidden = jnp.sin(matmul(hidden, second_w) + inner_b[1])
    return matmul(hidden, last_w) * decay_vals

def doc_masks(lengths):
    doc_ends = jnp.cumsum(lengths, axis=-1)
    doc_starts = doc_ends - lengths
    positions = jnp.arange(SEQ, dtype=jnp.int32)
    inside = (positions >= doc_starts[..., None]) & (positions < doc_ends[..., None])
    own_start = lax.optimization_barrier(jnp.sum(jnp.where(inside, doc_starts[..., None], 0), axis=-2)).astype(jnp.int32)
    return (inside.astype(jnp.float32), positions - own_start)

def long_conv(filt_vals, signal, row_mask):
    fft_len = 2 * SEQ
    filt_spec = jnp.fft.rfft(filt_vals, n=fft_len, axis=0)
    pieces = row_mask[:, :, None] * signal[None]
    piece_spec = jnp.fft.rfft(pieces, n=fft_len, axis=1)
    joined = jnp.fft.irfft(piece_spec * filt_spec[None], n=fft_len, axis=1)[:, :SEQ]
    return lax.optimization_barrier(jnp.sum(joined * row_mask[:, :, None], axis=0))

def layer_taps(weights, decay_vals):
    return filter_taps(weights[4], weights[5], weights[6], weights[7], decay_vals)

def hyena_layer(weights, filt_vals, row_in, row_mask, row_place):
    gain_vecs, bias_vecs, weight_in, vec_rows = (weights[0], weights[1], weights[2], weights[3])
    skip_vec = weights[8][0]
    weight_out, weight_up, hidden_bias, weight_down = (weights[9], weights[10], weights[11][0], weights[12])
    normed = low(layer_norm(row_in, gain_vecs[0], bias_vecs[0]))
    streams = low_back(low(matmul(normed, weight_in) + vec_rows[0]))
    mixed_in = vec_rows[4] + vec_rows[1] * streams
    for step_back in (1, 2):
        earlier = jnp.pad(streams, ((step_back, 0), (0, 0)))[:SEQ]
        mixed_in = mixed_in + vec_rows[1 + step_back] * earlier * (row_place >= step_back).astype(jnp.float32)[:, None]
    gate_out = mixed_in[:, :D]
    inner_gate = mixed_in[:, D:2 * D]
    value_part = mixed_in[:, 2 * D:]
    signal = value_part * inner_gate
    conv_out = long_conv(filt_vals, signal, row_mask)
    gated = low_back(low((conv_out + skip_vec * signal) * gate_out))
    residual = row_in + low_back(matmul(gated, weight_out) + bias_vecs[1])
    normed_two = low(layer_norm(residual, gain_vecs[1], bias_vecs[2]))
    pre_act = low_back(matmul(normed_two, weight_up) + hidden_bias)
    hidden = low(jax.nn.gelu(pre_act, approximate=True))
    return residual + low_back(matmul(hidden, weight_down) + bias_vecs[3])

def long_share(filt_vals):
    energy = filt_vals * filt_vals
    return jnp.sum(lax.optimization_barrier(jnp.sum(energy[LONG_LAG:], axis=0)) / (lax.optimization_barrier(jnp.sum(energy, axis=0)) + 1e-06))

def reference(layer_input, out_cot, doc_lengths, norm_gains, biases, in_weight, mix_vecs, filt_first, filt_inner_bias, filt_second, filt_last, filt_skip, out_weight, up_weight, up_bias, down_weight):
    params = tuple((tensor.astype(jnp.float32) for tensor in (norm_gains, biases, in_weight, mix_vecs, filt_first, filt_inner_bias, filt_second, filt_last, filt_skip, out_weight, up_weight, up_bias, down_weight)))
    row_total = MICRO * BATCH
    inputs = layer_input.astype(jnp.float32).reshape(row_total, SEQ, D)
    cot_rows = out_cot.astype(jnp.float32).reshape(row_total, SEQ, D)
    masks_all, place_all = doc_masks(doc_lengths.reshape(row_total, NDOCS))
    decay_vals = decay_table(D, 0)
    mid_bump = jnp.zeros_like(inputs)

    def network(weights, start_rows, extra_rows):
        layer_zero = tuple((member[0] for member in weights))
        layer_one = tuple((member[1] for member in weights))
        taps_zero = layer_taps(layer_zero, decay_vals)
        taps_one = layer_taps(layer_one, decay_vals)

        def per_row(carry_val, row_items):
            row_in, row_extra, row_mask, row_place = row_items
            mid_out = hyena_layer(layer_zero, taps_zero, row_in, row_mask, row_place)
            top_out = hyena_layer(layer_one, taps_one, mid_out + row_extra, row_mask, row_place)
            return (carry_val, (mid_out, top_out))
        _, (mids, tops) = lax.scan(jax.checkpoint(per_row), jnp.zeros((), jnp.float32), (start_rows, extra_rows, masks_all, place_all))
        return (mids, tops)
    (mids, tops), pull_back = jax.vjp(network, params, inputs, mid_bump)
    param_grads, first_grad, mid_grad = pull_back((jnp.zeros_like(mids), cot_rows))
    layer_output = jnp.stack([mids, tops]).reshape(LAYERS, MICRO, BATCH, SEQ, D)
    input_grad = jnp.stack([first_grad, mid_grad]).reshape(LAYERS, MICRO, BATCH, SEQ, D)
    shares = long_share(layer_taps(tuple((member[0] for member in params)), decay_vals)) + 4.0 * long_share(layer_taps(tuple((member[1] for member in params)), decay_vals))
    penalty = shares / CHAN
    return (layer_output, input_grad, param_grads[0], param_grads[1], param_grads[2], param_grads[3], param_grads[4], param_grads[5], param_grads[6], param_grads[7], param_grads[8], param_grads[9], param_grads[10], param_grads[11], param_grads[12], penalty)
```

```python
import functools

import jax
import jax.numpy as jnp
import ml_dtypes
import numpy as np
from jax import lax
from jax.experimental import pallas as pl
from jax.experimental.pallas import tpu as pltpu
from jax.sharding import PartitionSpec as P

D = 768
FF = 3072
EMB = 33
FILT = 64
SEQ = 1024
NDOCS = 3
LONG_LAG = 32
BLK = 128
NB = SEQ // BLK
FREQ = 2 * BLK
PIECES = NB + NDOCS - 1
HALO = 16
TILE = 48
FF_TILE = 512

eps = 1e-05
highest = lax.Precision.HIGHEST
f32 = jnp.float32
bf16 = jnp.bfloat16
VMEM_LIMIT = 56 * 1024 * 1024


def split_table(table):
    high = table.astype(ml_dtypes.bfloat16)
    low = (table - high.astype(np.float64)).astype(ml_dtypes.bfloat16)
    return high, low


def ring_table(offsets):
    theta = 2.0 * np.pi * (np.arange(BLK) + 0.5) / FREQ
    angles = offsets[:, None] * theta[None, :]
    return np.concatenate([np.cos(angles), -np.sin(angles)], axis=1)


def block_tables():
    fwd = ring_table(np.arange(BLK, dtype=np.float64))
    fwd_hi, fwd_lo = split_table(fwd)
    inv_hi, inv_lo = split_table(fwd.T / BLK)
    window = ring_table(np.arange(FREQ, dtype=np.float64) - BLK)
    window[0] = 0.0
    return fwd_hi, fwd_lo, inv_hi, inv_lo, window.astype(np.float32)


def position_table():
    positions = np.arange(SEQ, dtype=np.float32)
    band_count = (EMB - 1) // 2
    band_freq = np.float32(0.0001) + np.arange(band_count, dtype=np.float32) * np.float32(
        (band_count - 1 - 0.0001) / (band_count - 1)
    )
    angles = np.float32(2.0 * np.pi / SEQ) * positions[:, None] * band_freq[None, :]
    return np.concatenate(
        [(positions / SEQ)[:, None], np.cos(angles), np.sin(angles)], axis=1
    ).T.astype(np.float32)


def dot(left, right, dims=((1,), (0,))):
    return lax.dot_general(left, right, (dims, ((), ())), preferred_element_type=f32)


NT = ((1,), (1,))
TN = ((0,), (0,))


def norm_stats(values):
    centre = jnp.mean(values, axis=-1, keepdims=True)
    centred = values - centre
    variance = jnp.mean(centred * centred, axis=-1, keepdims=True)
    scale = lax.rsqrt(variance + eps)
    return centred * scale, scale


def norm_back(grad, gain, unit, scale):
    scaled = grad * gain
    return scale * (
        scaled
        - jnp.mean(scaled, axis=-1, keepdims=True)
        - unit * jnp.mean(scaled * unit, axis=-1, keepdims=True)
    )


def col_sum(values):
    return jnp.sum(values, axis=0, keepdims=True)


def place_masks(sc, rows, shard_len):
    pos = sc[1] * shard_len + lax.broadcasted_iota(jnp.int32, (rows, 1), 0)
    starts = pos == sc[2]
    after = pos == sc[2] + 1
    for doc in range(1, NDOCS):
        starts = starts | (pos == sc[2 + doc])
        after = after | (pos == sc[2 + doc] + 1)
    one = jnp.where(starts, 0.0, 1.0)
    two = jnp.where(starts | after, 0.0, 1.0)
    return one, two


def shifted(stream_ext):
    ext = stream_ext.astype(f32)
    return (
        ext[HALO:],
        pltpu.roll(ext, 1, 0)[HALO:],
        pltpu.roll(ext, 2, 0)[HALO:],
    )


def mix_row(p_ref, which, stream):
    row = 6 + 3 * which + stream
    return p_ref[row : row + 1, :]


def short_conv(st_ref, p_ref, stream, masks):
    zero, one, two = shifted(st_ref[:, stream * D : (stream + 1) * D])
    return (
        mix_row(p_ref, 4, stream)
        + mix_row(p_ref, 1, stream) * zero
        + mix_row(p_ref, 2, stream) * (one * masks[0])
        + mix_row(p_ref, 3, stream) * (two * masks[1])
    )


def fetch(own_first, own, rcv, dst, sem):
    @pl.when(own_first)
    def _():
        pltpu.make_async_copy(own, dst, sem).start()

    @pl.when(jnp.logical_not(own_first))
    def _():
        pltpu.make_async_copy(rcv, dst, sem).start()


def rows_at(start, size):
    return pl.ds(pl.multiple_of(start, 16), size)


def fetch_in(own_first, own, rcv, weight, sems):
    def part(ref, stream):
        return ref.at[0, :, pl.ds(stream * D, D)]

    def dest(stream):
        return weight.at[:, pl.ds(stream * D, D)]

    for stream in range(3):
        fetch(own_first, part(own, stream), part(rcv, stream), dest(stream), sems.at[stream])

    def wait(stream):
        pltpu.make_async_copy(part(own, stream), dest(stream), sems.at[stream]).wait()

    return wait


SMEM = pl.BlockSpec(memory_space=pltpu.SMEM)
VMEM = pl.BlockSpec(memory_space=pltpu.VMEM)
ANY = pl.BlockSpec(memory_space=pl.ANY)


def run(body, outs, ins, specs, scratch, name, flops=0, bytes_accessed=0):
    return pl.pallas_call(
        body,
        out_shape=[jax.ShapeDtypeStruct(shape, dtype) for shape, dtype in outs],
        in_specs=specs,
        out_specs=[VMEM] * len(outs),
        scratch_shapes=scratch,
        compiler_params=pltpu.CompilerParams(vmem_limit_bytes=VMEM_LIMIT),
        cost_estimate=pl.CostEstimate(
            flops=flops, bytes_accessed=bytes_accessed, transcendentals=0
        ),
        name=name,
    )(*ins)


def in_part(block, shard_len, count):
    chan = D // count

    def body(sc, x_ref, halo_ref, p_ref, own, rcv, normed_ref, st_ref, *rest):
        outs = rest[:count]
        weight, sig_t, sems = rest[count:]
        wait = fetch_in(sc[0] == block, own, rcv, weight, sems)
        ext = jnp.concatenate([halo_ref[...].astype(f32), x_ref[...].astype(f32)], axis=0)
        unit, _ = norm_stats(ext)
        normed = (unit * p_ref[0:1, :] + p_ref[2:3, :]).astype(bf16)
        normed_ref[...] = normed[HALO:]
        for stream in range(3):
            wait(stream)
            cols = slice(stream * D, (stream + 1) * D)
            st_ref[:, cols] = (dot(normed, weight[:, cols]) + mix_row(p_ref, 0, stream)).astype(bf16)
        masks = place_masks(sc, shard_len, shard_len)
        signal = short_conv(st_ref, p_ref, 2, masks) * short_conv(st_ref, p_ref, 1, masks)
        sig_t[...] = signal.T.astype(bf16)
        for step in range(count):
            outs[step][...] = sig_t[rows_at((sc[1] ^ step) * chan, chan), :]

    def call(sc, x, halo, params, own, rcv):
        return run(
            body,
            [((shard_len, D), bf16), ((shard_len + HALO, 3 * D), bf16)]
            + [((chan, shard_len), bf16)] * count,
            (sc, x, halo, params, own, rcv),
            [SMEM, VMEM, VMEM, VMEM, ANY, ANY],
            [
                pltpu.VMEM((D, 3 * D), bf16),
                pltpu.VMEM((D, shard_len), bf16),
                pltpu.SemaphoreType.DMA((3,)),
            ],
            f"in_part_{block}",
            2 * shard_len * D * 3 * D,
            D * 3 * D * 2,
        )

    return call


def piece_scalars(sc):
    starts = [sc[2 + doc] for doc in range(NDOCS)] + [SEQ]
    lows, offsets = [], [0]
    for doc in range(NDOCS):
        low, high = starts[doc] // BLK, (starts[doc + 1] - 1) // BLK
        lows.append(low)
        offsets.append(offsets[-1] + high - low + 1)
    pieces = []
    for piece in range(PIECES):
        begin, stop, low, first, last = starts[0], starts[1], lows[0], offsets[0], offsets[1]
        for doc in range(1, NDOCS):
            here = piece >= offsets[doc]
            begin = jnp.where(here, starts[doc], begin)
            stop = jnp.where(here, starts[doc + 1], stop)
            low = jnp.where(here, lows[doc], low)
            first = jnp.where(here, offsets[doc], first)
            last = jnp.where(here, offsets[doc + 1], last)
        live = piece < offsets[NDOCS]
        blk = jnp.minimum(low + piece - first, NB - 1)
        begin = jnp.where(live, begin, 0)
        stop = jnp.where(live, stop, 0)
        first = jnp.where(live, first, piece + 1)
        last = jnp.where(live, last, piece)
        pieces.append((blk, begin, stop, first, last))
    return pieces


def piece_mask(piece):
    pos = piece[0] * BLK + lax.broadcasted_iota(jnp.int32, (1, BLK), 1)
    return (pos >= piece[1]) & (pos < piece[2])


def gather_blocks(sc, ins, blocks, per_shard):
    for step, ref in enumerate(ins):
        source = sc[1] ^ step
        for part in range(per_shard):
            blocks[source * per_shard + part] = ref[:, part * BLK : (part + 1) * BLK]


def to_freq(pieces, blocks, masked, freq, tables, chan):
    for index, piece in enumerate(pieces):
        keep = jnp.where(piece_mask(piece), 1.0, 0.0)
        masked[index * chan : (index + 1) * chan, :] = (
            blocks[piece[0]].astype(f32) * keep
        ).astype(bf16)
    values = masked[...]
    freq[...] = dot(values, tables[0][...]) + dot(values, tables[1][...])


def from_freq(pieces, freq, out_blocks, tables, chan):
    values = freq[...]
    high = values.astype(bf16)
    low = (values - high.astype(f32)).astype(bf16)
    back = dot(high, tables[2][...]) + dot(low, tables[2][...]) + dot(high, tables[3][...])
    for index, piece in enumerate(pieces):
        mine = back[index * chan : (index + 1) * chan, :]
        before = out_blocks[piece[0]]
        out_blocks[piece[0]] = jnp.where(piece_mask(piece), mine, before)


def scatter_blocks(sc, outs, out_blocks, per_shard):
    for step, ref in enumerate(outs):
        target = sc[1] ^ step
        for part in range(per_shard):
            ref[:, part * BLK : (part + 1) * BLK] = out_blocks[target * per_shard + part].astype(bf16)


def conv_part(block, shard_len, count):
    chan = D // count
    per_shard = shard_len // BLK
    tiles = chan // TILE

    def body(sc, filt, *rest):
        ins, tables, rest = rest[:count], rest[count : count + 4], rest[count + 4 :]
        outs, blocks = rest[:count], rest[count]
        masked, freq, total, out_blocks = rest[count + 1 :]
        gather_blocks(sc, ins, blocks, per_shard)
        pieces = piece_scalars(sc)
        to_freq(pieces, blocks, masked, freq, tables, chan)
        for index, piece in enumerate(pieces):
            for tile in range(tiles):

                def step(other, carry, index=index, piece=piece, tile=tile):
                    sum_re, sum_im = carry
                    rows = rows_at(other * chan + tile * TILE, TILE)
                    sig_re, sig_im = freq[rows, :BLK], freq[rows, BLK:]
                    lag = index - other
                    here = slice(tile * TILE, (tile + 1) * TILE)
                    fil_re, fil_im = filt[lag, here, :BLK], filt[lag, here, BLK:]
                    return (
                        sum_re + fil_re * sig_re - fil_im * sig_im,
                        sum_im + fil_re * sig_im + fil_im * sig_re,
                    )

                zero = jnp.zeros((TILE, BLK), f32)
                sum_re, sum_im = lax.fori_loop(piece[3], index + 1, step, (zero, zero))
                here = slice(index * chan + tile * TILE, index * chan + (tile + 1) * TILE)
                total[here, :BLK] = sum_re
                total[here, BLK:] = sum_im
        out_blocks[...] = jnp.zeros_like(out_blocks)
        from_freq(pieces, total, out_blocks, tables, chan)
        scatter_blocks(sc, outs, out_blocks, per_shard)

    def call(sc, filt, ins, tables):
        return run(
            body,
            [((chan, shard_len), bf16)] * count + [((NB, chan, BLK), bf16)],
            (sc, filt, *ins, *tables),
            [SMEM] + [VMEM] * (count + 5),
            [
                pltpu.VMEM((PIECES * chan, BLK), bf16),
                pltpu.VMEM((PIECES * chan, FREQ), f32),
                pltpu.VMEM((PIECES * chan, FREQ), f32),
                pltpu.VMEM((NB, chan, BLK), f32),
            ],
            f"conv_part_{block}",
            10 * PIECES * chan * BLK * FREQ,
            NB * chan * FREQ * 4,
        )

    return call


def conv_back(block, shard_len, count):
    chan = D // count
    per_shard = shard_len // BLK
    tiles = chan // TILE

    def body(sc, filt, blocks, *rest):
        ins, tables, rest = rest[:count], rest[count : count + 4], rest[count + 4 :]
        outs, d_filt = rest[:count], rest[count]
        d_blocks, masked, freq, d_freq, total, out_blocks = rest[count + 1 :]
        gather_blocks(sc, ins, d_blocks, per_shard)
        pieces = piece_scalars(sc)
        to_freq(pieces, blocks, masked, freq, tables, chan)
        to_freq(pieces, d_blocks, masked, d_freq, tables, chan)
        d_filt[...] = jnp.zeros_like(d_filt)
        for index, piece in enumerate(pieces):
            for tile in range(tiles):
                rows = slice(index * chan + tile * TILE, index * chan + (tile + 1) * TILE)
                here = slice(tile * TILE, (tile + 1) * TILE)

                def step(other, carry, index=index, here=here, rows=rows, tile=tile):
                    sum_re, sum_im = carry
                    sig_re, sig_im = freq[rows, :BLK], freq[rows, BLK:]
                    there = rows_at(other * chan + tile * TILE, TILE)
                    der_re, der_im = d_freq[there, :BLK], d_freq[there, BLK:]
                    lag = other - index
                    fil_re, fil_im = filt[lag, here, :BLK], filt[lag, here, BLK:]
                    d_filt[lag, here, :BLK] += sig_re * der_re + sig_im * der_im
                    d_filt[lag, here, BLK:] += sig_re * der_im - sig_im * der_re
                    return (
                        sum_re + fil_re * der_re + fil_im * der_im,
                        sum_im + fil_re * der_im - fil_im * der_re,
                    )

                zero = jnp.zeros((TILE, BLK), f32)
                sum_re, sum_im = lax.fori_loop(index, piece[4], step, (zero, zero))
                total[rows, :BLK] = sum_re
                total[rows, BLK:] = sum_im
        out_blocks[...] = jnp.zeros_like(out_blocks)
        from_freq(pieces, total, out_blocks, tables, chan)
        scatter_blocks(sc, outs, out_blocks, per_shard)

    def call(sc, filt, blocks, ins, tables):
        return run(
            body,
            [((chan, shard_len), bf16)] * count + [((NB, chan, FREQ), f32)],
            (sc, filt, blocks, *ins, *tables),
            [SMEM] + [VMEM] * (count + 6),
            [
                pltpu.VMEM((NB, chan, BLK), bf16),
                pltpu.VMEM((PIECES * chan, BLK), bf16),
                pltpu.VMEM((PIECES * chan, FREQ), f32),
                pltpu.VMEM((PIECES * chan, FREQ), f32),
                pltpu.VMEM((PIECES * chan, FREQ), f32),
                pltpu.VMEM((NB, chan, BLK), f32),
            ],
            f"conv_back_{block}",
            14 * PIECES * chan * BLK * FREQ,
            NB * chan * FREQ * 8,
        )

    return call


def token_major(sc, ins, turned, chan):
    for step, ref in enumerate(ins):
        turned[rows_at((sc[1] ^ step) * chan, chan), :] = ref[...]
    return turned[...].astype(f32).T


def weight_scratch():
    return [
        pltpu.VMEM((D, D), bf16),
        pltpu.VMEM((D, FF), bf16),
        pltpu.VMEM((FF, D), bf16),
        pltpu.SemaphoreType.DMA((1 + 2 * (FF // FF_TILE),)),
    ]


def fetch_mlp(own_first, pairs, dsts, sems, out_first):
    tiles = FF // FF_TILE
    (out_own, out_rcv), (up_own, up_rcv), (down_own, down_rcv) = pairs
    w_out, w_up, w_down = dsts

    def start_out():
        fetch(own_first, out_own.at[0], out_rcv.at[0], w_out, sems.at[0])

    def start_up(tile):
        cols = pl.ds(tile * FF_TILE, FF_TILE)
        fetch(
            own_first,
            up_own.at[0, :, cols],
            up_rcv.at[0, :, cols],
            w_up.at[:, cols],
            sems.at[1 + tile],
        )

    def start_down(tile):
        rows = pl.ds(tile * FF_TILE, FF_TILE)
        fetch(
            own_first,
            down_own.at[0, rows],
            down_rcv.at[0, rows],
            w_down.at[rows],
            sems.at[1 + tiles + tile],
        )

    if out_first:
        start_out()
    for tile in range(tiles):
        if out_first:
            start_up(tile)
            start_down(tile)
        else:
            start_down(tile)
            start_up(tile)
    if not out_first:
        start_out()

    def wait_out():
        pltpu.make_async_copy(out_own.at[0], w_out, sems.at[0]).wait()

    def wait_up(tile):
        cols = pl.ds(pl.multiple_of(tile * FF_TILE, FF_TILE), FF_TILE)
        pltpu.make_async_copy(up_own.at[0, :, cols], w_up.at[:, cols], sems.at[1 + tile]).wait()
        return cols

    def wait_down(tile):
        rows = pl.ds(pl.multiple_of(tile * FF_TILE, FF_TILE), FF_TILE)
        pltpu.make_async_copy(
            down_own.at[0, rows], w_down.at[rows], sems.at[1 + tiles + tile]
        ).wait()
        return rows

    return wait_out, wait_up, wait_down


GELU_SCALE = 0.7978845608028654
GELU_CUBE = 0.044715


def out_part(block, shard_len, count):
    chan = D // count

    def body(sc, x_ref, st_ref, p_ref, bias_ref, *rest):
        ins, rest = rest[:count], rest[count:]
        pairs = (rest[0:2], rest[2:4], rest[4:6])
        result_ref, residual_ref, gated_ref, normed_ref, hidden_ref, slope_ref, cmix_ref = rest[6:13]
        turned, w_out, w_up, w_down, sems = rest[13:]
        wait_out, wait_up, wait_down = fetch_mlp(
            sc[0] == block, pairs, (w_out, w_up, w_down), sems, True
        )
        masks = place_masks(sc, shard_len, shard_len)
        conv = token_major(sc, ins, turned, chan)
        signal = short_conv(st_ref, p_ref, 2, masks) * short_conv(st_ref, p_ref, 1, masks)
        cmix = conv + p_ref[21:22, :] * signal
        cmix_ref[...] = cmix
        gated = (cmix * short_conv(st_ref, p_ref, 0, masks)).astype(bf16)
        gated_ref[...] = gated
        wait_out()
        residual = x_ref[...].astype(f32) + dot(gated, w_out[...]) + p_ref[3:4, :]
        residual_ref[...] = residual
        unit, _ = norm_stats(residual)
        normed_ref[...] = (unit * p_ref[1:2, :] + p_ref[4:5, :]).astype(bf16)
        result_ref[...] = residual + p_ref[5:6, :]

        @pl.loop(0, FF // FF_TILE)
        def _(tile):
            cols = wait_up(tile)
            pre = dot(normed_ref[...], w_up[:, cols]) + bias_ref[:, cols]
            square = pre * pre
            bent = jnp.tanh(GELU_SCALE * pre * (1.0 + GELU_CUBE * square))
            half = 0.5 * (1.0 + bent)
            slope = half + (0.5 * GELU_SCALE) * pre * (1.0 - bent * bent) * (
                1.0 + 3.0 * GELU_CUBE * square
            )
            hidden = (pre * half).astype(bf16)
            hidden_ref[:, cols] = hidden
            slope_ref[:, cols] = slope.astype(bf16)
            rows = wait_down(tile)
            result_ref[...] += dot(hidden, w_down[rows, :])

    def call(sc, x, st, params, up_bias, ins, weights):
        return run(
            body,
            [
                ((shard_len, D), f32),
                ((shard_len, D), f32),
                ((shard_len, D), bf16),
                ((shard_len, D), bf16),
                ((shard_len, FF), bf16),
                ((shard_len, FF), bf16),
                ((shard_len, D), f32),
            ],
            (sc, x, st, params, up_bias, *ins, *weights),
            [SMEM] + [VMEM] * (4 + count) + [ANY] * 6,
            [pltpu.VMEM((D, shard_len), bf16)] + weight_scratch(),
            f"out_part_{block}",
            2 * shard_len * D * (D + 2 * FF),
            D * (D + 2 * FF) * 2,
        )

    return call


def out_back(block, shard_len, count):
    chan = D // count

    def body(sc, grad_ref, residual_ref, slope_ref, st_ref, cmix_ref, p_ref, *rest):
        pairs = (rest[0:2], rest[2:4], rest[4:6])
        d_pre_ref, gm_ref, dres_ref, gb_ref, dg_ref, vec_ref, dub_ref = rest[6:13]
        outs, rest = rest[13 : 13 + count], rest[13 + count :]
        turned, w_out, w_up, w_down, sems, total = rest
        wait_out, wait_up, wait_down = fetch_mlp(
            sc[0] == block, pairs, (w_out, w_up, w_down), sems, False
        )
        grad = grad_ref[...].astype(f32)
        gm = grad.astype(bf16)
        gm_ref[...] = gm
        total[...] = jnp.zeros_like(total)

        @pl.loop(0, FF // FF_TILE)
        def _(tile):
            rows = wait_down(tile)
            d_hidden = dot(gm_ref[...], w_down[rows, :], NT)
            d_pre = (d_hidden * slope_ref[:, rows].astype(f32)).astype(bf16)
            d_pre_ref[:, rows] = d_pre
            dub_ref[:, rows] = jnp.broadcast_to(col_sum(d_pre.astype(f32)), (8, FF_TILE))
            cols = wait_up(tile)
            total[...] += dot(d_pre, w_up[:, cols], NT)

        d_normed = total[...]
        unit, scale = norm_stats(residual_ref[...])
        d_res = grad + norm_back(d_normed, p_ref[1:2, :], unit, scale)
        dres_ref[...] = d_res
        gb = d_res.astype(bf16)
        gb_ref[...] = gb
        wait_out()
        dg = dot(gb, w_out[...], NT).astype(bf16)
        dg_ref[...] = dg
        masks = place_masks(sc, shard_len, shard_len)
        d_conv = dg.astype(f32) * short_conv(st_ref, p_ref, 0, masks)
        turned[...] = d_conv.T.astype(bf16)
        for step in range(count):
            outs[step][...] = turned[rows_at((sc[1] ^ step) * chan, chan), :]
        vec_ref[...] = jnp.concatenate(
            [
                col_sum(d_normed * unit),
                col_sum(d_normed),
                col_sum(gb.astype(f32)),
                col_sum(gm.astype(f32)),
                jnp.zeros((4, D), f32),
            ],
            axis=0,
        )

    def call(sc, grad, residual, slope, st, cmix, params, weights):
        return run(
            body,
            [
                ((shard_len, FF), bf16),
                ((shard_len, D), bf16),
                ((shard_len, D), f32),
                ((shard_len, D), bf16),
                ((shard_len, D), bf16),
                ((8, D), f32),
                ((8, FF), f32),
            ]
            + [((chan, shard_len), bf16)] * count,
            (sc, grad, residual, slope, st, cmix, params, *weights),
            [SMEM] + [VMEM] * 6 + [ANY] * 6,
            [pltpu.VMEM((D, shard_len), bf16)]
            + weight_scratch()
            + [pltpu.VMEM((shard_len, D), f32)],
            f"out_back_{block}",
            2 * shard_len * D * (D + 2 * FF),
            D * (D + 2 * FF) * 2,
        )

    return call


def short_back(block, shard_len, count):
    chan = D // count

    def body(sc, st_ref, dg_ref, cmix_ref, p_ref, *rest):
        ins = rest[:count]
        ds_ref, head_ref, vec_ref, turned = rest[count:]
        masks = place_masks(sc, shard_len, shard_len)
        d_signal = token_major(sc, ins, turned, chan)
        dg = dg_ref[...].astype(f32)
        d_conv = dg * short_conv(st_ref, p_ref, 0, masks)
        inner = short_conv(st_ref, p_ref, 1, masks)
        value = short_conv(st_ref, p_ref, 2, masks)
        d_signal = d_signal + p_ref[21:22, :] * d_conv
        rows = [None] * 16
        rows[12] = col_sum(d_conv * value * inner)
        for stream, d_short in enumerate((dg * cmix_ref[...], d_signal * value, d_signal * inner)):
            cols = slice(stream * D, (stream + 1) * D)
            ds_ref[:, cols] = d_short
            head_ref[:, cols] = d_short[:HALO]
            zero, one, two = shifted(st_ref[:, cols])
            rows[stream] = col_sum(d_short * zero)
            rows[3 + stream] = col_sum(d_short * (one * masks[0]))
            rows[6 + stream] = col_sum(d_short * (two * masks[1]))
            rows[9 + stream] = col_sum(d_short)
        for index in range(13, 16):
            rows[index] = jnp.zeros((1, D), f32)
        vec_ref[...] = jnp.concatenate(rows, axis=0)

    def call(sc, st, dg, cmix, params, ins):
        return run(
            body,
            [((shard_len, 3 * D), f32), ((HALO, 3 * D), f32), ((16, D), f32)],
            (sc, st, dg, cmix, params, *ins),
            [SMEM] + [VMEM] * (4 + count),
            [pltpu.VMEM((D, shard_len), bf16)],
            f"short_back_{block}",
            40 * shard_len * D,
            shard_len * D * 20,
        )

    return call


def in_back(block, shard_len):
    def body(sc, ds_ref, halo_ref, x_ref, dres_ref, p_ref, own, rcv, dst_ref, dx_ref, vec_ref, weight, sems):
        wait = fetch_in(sc[0] == block, own, rcv, weight, sems)
        long = shard_len + HALO
        one, two = place_masks(sc, long, shard_len)
        d_normed = jnp.zeros((shard_len, D), f32)
        rows = []
        for stream in range(3):
            cols = slice(stream * D, (stream + 1) * D)
            ext = jnp.concatenate([ds_ref[:, cols], halo_ref[:, cols]], axis=0)
            d_stream = (
                mix_row(p_ref, 1, stream) * ext[:shard_len]
                + mix_row(p_ref, 2, stream) * pltpu.roll(ext * one, long - 1, 0)[:shard_len]
                + mix_row(p_ref, 3, stream) * pltpu.roll(ext * two, long - 2, 0)[:shard_len]
            ).astype(bf16)
            dst_ref[:, cols] = d_stream
            rows.append(col_sum(d_stream.astype(f32)))
            wait(stream)
            d_normed = d_normed + dot(d_stream, weight[:, cols], NT)
        unit, scale = norm_stats(x_ref[...].astype(f32))
        dx_ref[...] = dres_ref[...] + norm_back(d_normed, p_ref[0:1, :], unit, scale)
        vec_ref[...] = jnp.concatenate(
            [col_sum(d_normed * unit), col_sum(d_normed)] + rows + [jnp.zeros((3, D), f32)], axis=0
        )

    def call(sc, d_short, halo, x, d_res, params, own, rcv):
        return run(
            body,
            [((shard_len, 3 * D), bf16), ((shard_len, D), f32), ((8, D), f32)],
            (sc, d_short, halo, x, d_res, params, own, rcv),
            [SMEM] + [VMEM] * 5 + [ANY] * 2,
            [pltpu.VMEM((D, 3 * D), bf16), pltpu.SemaphoreType.DMA((3,))],
            f"in_back_{block}",
            2 * shard_len * D * 3 * D,
            D * 3 * D * 2,
        )

    return call


def weight_grad(name, rows, cols, shard_len):
    chunk = 384 if rows % 384 == 0 else rows

    def body(g_own, g_rcv, a_own, a_rcv, out_ref):
        @pl.loop(0, rows // chunk)
        def _(step):
            here = pl.ds(pl.multiple_of(step * chunk, chunk), chunk)
            out_ref[here, :] = (
                dot(g_own[:, here], a_own[...], TN) + dot(g_rcv[:, here], a_rcv[...], TN)
            ).astype(bf16)

    def call(*ins):
        return run(
            body,
            [((rows, cols), bf16)],
            ins,
            [VMEM] * 4,
            [],
            name,
            4 * shard_len * rows * cols,
            rows * cols * 2,
        )[0]

    return call


def pairs(count, step):
    return [(index, index ^ step) for index in range(count)]


def swap(value):
    return lax.ppermute(value, "section", pairs(2, 1))


def exchange(chunks):
    count = len(chunks)
    return [chunks[0]] + [
        lax.ppermute(chunks[step], "seq", pairs(count, step)) for step in range(1, count)
    ]


def add_round(first, second):
    return (first.astype(f32) + second.astype(f32)).astype(bf16)


def scatter_sum(value, low_first):
    dp, count = value.shape[0], value.shape[1]
    bits = dp.bit_length() - 1
    index = lax.axis_index("dp")
    value = value.reshape((2,) * bits + value.shape[1:])
    order = list(range(bits))
    if low_first:
        order = order[::-1]
    axes = list(range(bits))
    for bit in order:
        axis = axes.index(bit)
        weight = 1 << (bits - 1 - bit)
        mine = (index // weight) % 2
        send = lax.dynamic_index_in_dim(value, 1 - mine, axis, keepdims=False)
        keep = lax.dynamic_index_in_dim(value, mine, axis, keepdims=False)
        got = lax.ppermute(send, "dp", pairs(dp, weight))
        value = add_round(keep, got)
        axes.remove(bit)
    place = lax.axis_index("seq")
    total = lax.dynamic_index_in_dim(value, place, 0, keepdims=False).astype(f32)
    for step in range(1, count):
        part = lax.dynamic_index_in_dim(value, place ^ step, 0, keepdims=False)
        total = total + lax.ppermute(part, "seq", pairs(count, step)).astype(f32)
    return total


def sum_all(value):
    value = value + swap(value)
    for axis in ("dp", "seq"):
        count = lax.axis_size(axis)
        step = 1
        while step < count:
            value = value + lax.ppermute(value, axis, pairs(count, step))
            step *= 2
    return value


def mat(spec, left, right):
    return jnp.einsum(spec, left, right, precision=highest, preferred_element_type=f32)


def filter_state(net, last, decay, pos, window):
    first_w, inner_b, second_w = net[:EMB], net[EMB : EMB + 2], net[EMB + 2 :]
    pre_a = mat("ef,en->fn", first_w, pos) + inner_b[0][:, None]
    hid_a = jnp.sin(pre_a)
    pre_b = mat("gf,gn->fn", second_w, hid_a) + inner_b[1][:, None]
    hid_b = jnp.sin(pre_b)
    taps = mat("fc,fn->cn", last, hid_b) * decay
    blocks = taps.reshape(taps.shape[0], NB, BLK)
    filt = mat("cmn,nk->mck", blocks, window[BLK:])
    behind = mat("cmn,nk->mck", blocks[:, :-1], window[:BLK])
    filt = filt + jnp.pad(behind, ((1, 0), (0, 0), (0, 0)))
    energy = taps * taps
    share = jnp.sum(jnp.sum(energy[:, LONG_LAG:], axis=1) / (jnp.sum(energy, axis=1) + 1e-06))
    return filt, share, (pre_a, hid_a, pre_b, hid_b, second_w)


def filter_back(d_filt, state, last, decay, pos, window):
    pre_a, hid_a, pre_b, hid_b, second_w = state
    ahead = jnp.pad(d_filt[1:], ((0, 1), (0, 0), (0, 0)))
    d_taps = mat("mck,nk->cmn", d_filt, window[BLK:]) + mat("mck,nk->cmn", ahead, window[:BLK])
    d_out = d_taps.reshape(last.shape[1], SEQ) * (decay / BLK)
    d_last = mat("fn,cn->fc", hid_b, d_out)
    d_b = mat("fc,cn->fn", last, d_out) * jnp.cos(pre_b)
    d_second = mat("gn,fn->gf", hid_a, d_b)
    d_a = mat("gf,fn->gn", second_w, d_b) * jnp.cos(pre_a)
    d_first = mat("en,fn->ef", pos, d_a)
    d_inner = jnp.stack([jnp.sum(d_a, axis=1), jnp.sum(d_b, axis=1)])
    return d_last, jnp.concatenate([d_first, d_inner, d_second], axis=0)


def local(
    layer_input,
    out_cot,
    doc_lengths,
    norm_gains,
    biases,
    in_weight,
    mix_vecs,
    filt_first,
    filt_inner_bias,
    filt_second,
    filt_last,
    filt_skip,
    out_weight,
    up_weight,
    up_bias,
    down_weight,
):
    count = lax.axis_size("seq")
    dp_count = lax.axis_size("dp")
    section = lax.axis_index("section")
    place = lax.axis_index("seq")
    first = section == 0
    shard_len = layer_input.shape[2]
    chan = D // count
    fwd_hi, fwd_lo, inv_hi, inv_lo, window = block_tables()
    tables = tuple(jnp.asarray(t) for t in (fwd_hi, fwd_lo, inv_hi, inv_lo))
    window = jnp.asarray(window)
    pos = jnp.asarray(position_table())

    def own_micro(value):
        return lax.dynamic_index_in_dim(value, section, 0, keepdims=False)[0]

    x_zero = own_micro(layer_input)
    cot = own_micro(out_cot)
    lengths = own_micro(doc_lengths)
    starts = jnp.cumsum(lengths) - lengths
    sc = jnp.concatenate([jnp.stack([section, place]), starts]).astype(jnp.int32)

    def behind(rows):
        return lax.ppermute(rows, "seq", [(index, index + 1) for index in range(count - 1)])

    def ahead(rows):
        return lax.ppermute(rows, "seq", [(index + 1, index) for index in range(count - 1)])

    halo = behind(x_zero[-HALO:])
    small = jnp.concatenate(
        [
            norm_gains[0],
            biases[0],
            mix_vecs[0].reshape(15, D),
            filt_skip[0],
            up_bias[0].reshape(4, D),
            filt_last[0],
        ],
        axis=0,
    )
    net = jnp.concatenate([filt_first[0], filt_inner_bias[0], filt_second[0]], axis=0)
    small_rcv, net_rcv = swap(small), swap(net)
    rcv_in, rcv_out, rcv_up, rcv_down = (
        swap(in_weight),
        swap(out_weight),
        swap(up_weight),
        swap(down_weight),
    )
    mlp_pairs = (out_weight, rcv_out, up_weight, rcv_up, down_weight, rcv_down)
    params, nets = [], []
    for block in range(2):
        mine = section == block
        params.append(jnp.where(mine, small, small_rcv).astype(f32))
        nets.append(jnp.where(mine, net, net_rcv).astype(f32))
    tokens = [p[:24] for p in params]
    up_biases = [p[22:26].reshape(1, FF) for p in params]
    lasts = [lax.dynamic_slice_in_dim(p[26:90], place * chan, chan, 1) for p in params]
    chan_ids = (jnp.arange(chan, dtype=jnp.int32) + place * chan).astype(f32)
    times = jnp.arange(SEQ, dtype=f32) / SEQ
    decay = jnp.exp(-(3.0 + 12.0 * chan_ids / (D - 1))[:, None] * times[None, :])
    filters = [filter_state(nets[b], lasts[b], decay, pos, window) for b in range(2)]

    x = x_zero
    kept = []
    results = []
    for block in range(2):
        normed, st, *chunks = in_part(block, shard_len, count)(
            sc, x, halo, tokens[block], in_weight, rcv_in
        )
        *chunks, blocks = conv_part(block, shard_len, count)(
            sc, filters[block][0], exchange(chunks), tables
        )
        result, residual, gated, normed_two, hidden, slope, cmix = out_part(
            block, shard_len, count
        )(sc, x, st, tokens[block], up_biases[block], exchange(chunks), mlp_pairs)
        kept.append((x, normed, st, blocks, residual, gated, normed_two, hidden, slope, cmix))
        results.append(result)
        x = result
        if block == 0:
            halo = behind(result[-HALO:])

    def half_pair(value):
        half = value.shape[1] // 2
        mine = lax.dynamic_slice_in_dim(value, section * half, half, 1)
        other = lax.dynamic_slice_in_dim(value, (1 - section) * half, half, 1)
        return mine, swap(other)

    def reduced(name, grads, acts, low_first):
        mine, got = half_pair(acts)
        rows, cols = grads.shape[1], mine.shape[1]
        full = weight_grad(name, rows, cols, shard_len)(grads, swap(grads), mine, got)
        blocked = full.reshape(dp_count, count, rows // (dp_count * count), cols)
        return scatter_sum(blocked, low_first)

    grad = cot
    pieces = [None, None]
    packs = [None, None]
    in_grads = [None, None]
    for block in (1, 0):
        x, normed, st, blocks, residual, gated, normed_two, hidden, slope, cmix = kept[block]
        d_pre, gm, d_res, gb, dg, vec_out, d_up_bias, *chunks = out_back(block, shard_len, count)(
            sc, grad, residual, slope, st, cmix, tokens[block], mlp_pairs
        )
        *chunks, d_filt = conv_back(block, shard_len, count)(
            sc, filters[block][0], blocks, exchange(chunks), tables
        )
        d_short, head, vec_short = short_back(block, shard_len, count)(
            sc, st, dg, cmix, tokens[block], exchange(chunks)
        )
        d_st, d_x, vec_in = in_back(block, shard_len)(
            sc, d_short, ahead(head), x, d_res, tokens[block], in_weight, rcv_in
        )
        in_grads[block] = d_x
        grad = d_x
        d_last, d_net = filter_back(d_filt, filters[block][2], lasts[block], decay, pos, window)
        pieces[block] = (
            reduced(f"down_grad_{block}", gm, hidden, True),
            reduced(f"up_grad_{block}", d_pre, normed_two, False),
            reduced(f"out_grad_{block}", gb, gated, True),
            reduced(f"in_grad_{block}", d_st, normed, False),
        )
        last_full = lax.dynamic_update_slice_in_dim(
            jnp.zeros((FILT, D), f32), d_last, place * chan, 1
        )
        extra = filters[0][1] + 4.0 * filters[1][1] if block == 0 else jnp.zeros((), f32)
        extra = extra / (chan * 2 * dp_count)
        flat = jnp.concatenate([d_net.reshape(-1), extra[None]])
        flat = jnp.pad(flat, (0, 9 * D - flat.shape[0])).reshape(9, D)
        packs[block] = sum_all(
            jnp.concatenate(
                [
                    vec_in[0:1],
                    vec_out[0:1],
                    vec_in[1:2],
                    vec_out[2:3],
                    vec_out[1:2],
                    vec_out[3:4],
                    vec_in[2:5],
                    vec_short[0:12],
                    vec_short[12:13],
                    d_up_bias[0:1].reshape(4, D),
                    last_full,
                    flat,
                ],
                axis=0,
            )
        )

    def choose(values):
        return jnp.where(first, values[0], values[1]), jnp.where(first, values[1], values[0])

    def both_micros(values):
        mine, other = choose(values)
        got = swap(other)
        return jnp.stack([jnp.where(first, mine, got), jnp.where(first, got, mine)])[None, :, None]

    def whole_grad(index, turn):
        mine, other = choose([pieces[0][index], pieces[1][index]])
        got = swap(other)
        full = jnp.concatenate(
            [jnp.where(first, mine, got), jnp.where(first, got, mine)], axis=1
        )
        return full.T[None]

    pack, _ = choose(packs)
    shard = lax.axis_index("dp") * count + place
    shards = dp_count * count

    def columns(value):
        width = value.shape[1] // shards
        return lax.dynamic_slice_in_dim(value, shard * width, width, 1)[None]

    flat = pack[90:99].reshape(-1)
    d_net = flat[: 99 * FILT].reshape(99, FILT)
    penalty = packs[0][90:99].reshape(-1)[99 * FILT]
    return (
        both_micros(results),
        both_micros(in_grads),
        columns(pack[0:2]),
        columns(pack[2:6]),
        whole_grad(3, True),
        columns(pack[6:21].reshape(5, 3 * D)),
        d_net[None, :EMB],
        d_net[None, EMB : EMB + 2],
        d_net[None, EMB + 2 :],
        columns(pack[26:90]),
        columns(pack[21:22]),
        whole_grad(2, True),
        whole_grad(1, True),
        columns(pack[22:26].reshape(1, FF)),
        whole_grad(0, True),
        penalty,
    )


def solution(mesh):
    by_section = P("section")
    shard = P("section", None, ("dp", "seq"))
    tokens = P("section", None, "dp", "seq", None)
    return jax.shard_map(
        local,
        mesh=mesh,
        in_specs=(P(None, "dp", "seq", None), P(None, "dp", "seq", None), P(None, "dp", None))
        + (by_section,) * 13,
        out_specs=(tokens, tokens, shard, shard, shard, shard)
        + (by_section,) * 3
        + (shard,) * 6
        + (P(),),
        check_vma=False,
    )
```

```python
import functools

import jax
import jax.numpy as jnp
import ml_dtypes
import numpy as np
from jax import lax
from jax.experimental import pallas as pl
from jax.experimental.pallas import tpu as pltpu
from jax.sharding import PartitionSpec as P

D = 768
FF = 3072
EMB = 33
FILT = 64
SEQ = 1024
NDOCS = 3
LONG_LAG = 32
BLK = 128
NB = SEQ // BLK
FREQ = 2 * BLK
PIECES = NB + NDOCS - 1
HALO = 16
TILE = 48
FF_TILE = 512

eps = 1e-05
highest = lax.Precision.HIGHEST
f32 = jnp.float32
bf16 = jnp.bfloat16
TICK = ((1, 1), f32)
HALF = D // 2
ACT_HIDDEN = 0
ACT_TWO = FF // 2
ACT_GATED = ACT_TWO + HALF
ACT_NORMED = ACT_GATED + HALF
ACT_COLS = ACT_NORMED + HALF
GRAD_PRE = 0
GRAD_MLP = FF
GRAD_BRANCH = FF + D
GRAD_COLS = FF + 2 * D
SPLIT = 80
VMEM_LIMIT = 56 * 1024 * 1024


def split_table(table):
    high = table.astype(ml_dtypes.bfloat16)
    low = (table - high.astype(np.float64)).astype(ml_dtypes.bfloat16)
    return high, low


def ring_table(offsets):
    theta = 2.0 * np.pi * (np.arange(BLK) + 0.5) / FREQ
    angles = offsets[:, None] * theta[None, :]
    return np.concatenate([np.cos(angles), -np.sin(angles)], axis=1)


def block_tables():
    fwd = ring_table(np.arange(BLK, dtype=np.float64))
    fwd_hi, fwd_lo = split_table(fwd)
    inv_hi, inv_lo = split_table(fwd.T / BLK)
    window = ring_table(np.arange(FREQ, dtype=np.float64) - BLK)
    window[0] = 0.0
    return fwd_hi, fwd_lo, inv_hi, inv_lo, window.astype(np.float32)


def position_table():
    positions = np.arange(SEQ, dtype=np.float32)
    band_count = (EMB - 1) // 2
    band_freq = np.float32(0.0001) + np.arange(band_count, dtype=np.float32) * np.float32(
        (band_count - 1 - 0.0001) / (band_count - 1)
    )
    angles = np.float32(2.0 * np.pi / SEQ) * positions[:, None] * band_freq[None, :]
    return np.concatenate(
        [(positions / SEQ)[:, None], np.cos(angles), np.sin(angles)], axis=1
    ).T.astype(np.float32)


def dot(left, right, dims=((1,), (0,))):
    return lax.dot_general(left, right, (dims, ((), ())), preferred_element_type=f32)


NT = ((1,), (1,))
TN = ((0,), (0,))


def norm_stats(values):
    centre = jnp.mean(values, axis=-1, keepdims=True)
    centred = values - centre
    variance = jnp.mean(centred * centred, axis=-1, keepdims=True)
    scale = lax.rsqrt(variance + eps)
    return centred * scale, scale


def norm_back(grad, gain, unit, scale):
    scaled = grad * gain
    return scale * (
        scaled
        - jnp.mean(scaled, axis=-1, keepdims=True)
        - unit * jnp.mean(scaled * unit, axis=-1, keepdims=True)
    )


def col_sum(values):
    return jnp.sum(values, axis=0, keepdims=True)


def place_masks(sc, rows, shard_len):
    pos = sc[1] * shard_len + lax.broadcasted_iota(jnp.int32, (rows, 1), 0)
    starts = pos == sc[2]
    after = pos == sc[2] + 1
    for doc in range(1, NDOCS):
        starts = starts | (pos == sc[2 + doc])
        after = after | (pos == sc[2 + doc] + 1)
    one = jnp.where(starts, 0.0, 1.0)
    two = jnp.where(starts | after, 0.0, 1.0)
    return one, two


def shifted(stream_ext):
    ext = stream_ext.astype(f32)
    return (
        ext[HALO:],
        pltpu.roll(ext, 1, 0)[HALO:],
        pltpu.roll(ext, 2, 0)[HALO:],
    )


def mix_row(p_ref, which, stream):
    row = 6 + 3 * which + stream
    return p_ref[row : row + 1, :]


def short_conv(st_ref, p_ref, stream, masks):
    zero, one, two = shifted(st_ref[:, stream * D : (stream + 1) * D])
    return (
        mix_row(p_ref, 4, stream)
        + mix_row(p_ref, 1, stream) * zero
        + mix_row(p_ref, 2, stream) * (one * masks[0])
        + mix_row(p_ref, 3, stream) * (two * masks[1])
    )


def fetch(own_first, own, rcv, dst, sem):
    @pl.when(own_first)
    def _():
        pltpu.make_async_copy(own, dst, sem).start()

    @pl.when(jnp.logical_not(own_first))
    def _():
        pltpu.make_async_copy(rcv, dst, sem).start()


def rows_at(start, size):
    return pl.ds(pl.multiple_of(start, 16), size)


def fetch_in(own_first, own, rcv, weight, sems):
    def part(ref, stream):
        return ref.at[0, :, pl.ds(stream * D, D)]

    def dest(stream):
        return weight.at[:, pl.ds(stream * D, D)]

    for stream in range(3):
        fetch(own_first, part(own, stream), part(rcv, stream), dest(stream), sems.at[stream])

    def wait(stream):
        pltpu.make_async_copy(part(own, stream), dest(stream), sems.at[stream]).wait()

    return wait


SMEM = pl.BlockSpec(memory_space=pltpu.SMEM)
VMEM = pl.BlockSpec(memory_space=pltpu.VMEM)
ANY = pl.BlockSpec(memory_space=pl.ANY)


def run(body, outs, ins, specs, scratch, name, flops=0, bytes_accessed=0, deps=()):
    taken, skipped = len(ins), len(deps)

    def wrapped(*refs):
        body(*refs[:taken], *refs[taken + skipped :])

    return pl.pallas_call(
        wrapped,
        out_shape=[jax.ShapeDtypeStruct(shape, dtype) for shape, dtype in outs],
        in_specs=specs + [ANY] * skipped,
        out_specs=[SMEM if out == TICK else VMEM for out in outs],
        scratch_shapes=scratch,
        compiler_params=pltpu.CompilerParams(vmem_limit_bytes=VMEM_LIMIT),
        cost_estimate=pl.CostEstimate(
            flops=1, bytes_accessed=1, transcendentals=0
        ),
        name=name,
    )(*ins, *deps)


def in_part(block, shard_len, count):
    chan = D // count

    def body(sc, x_ref, halo_ref, p_ref, own, rcv, normed_ref, st_ref, tick_ref, *rest):
        outs = rest[0]
        tick_ref[0, 0] = 0.0
        weight, sig_t, sems = rest[1:]
        wait = fetch_in(sc[0] == block, own, rcv, weight, sems)
        ext = jnp.concatenate([halo_ref[...].astype(f32), x_ref[...].astype(f32)], axis=0)
        unit, _ = norm_stats(ext)
        normed = (unit * p_ref[0:1, :] + p_ref[2:3, :]).astype(bf16)
        normed_ref[...] = normed[HALO:]
        for stream in range(3):
            wait(stream)
            cols = slice(stream * D, (stream + 1) * D)
            st_ref[:, cols] = (dot(normed, weight[:, cols]) + mix_row(p_ref, 0, stream)).astype(bf16)
        masks = place_masks(sc, shard_len, shard_len)
        signal = short_conv(st_ref, p_ref, 2, masks) * short_conv(st_ref, p_ref, 1, masks)
        sig_t[...] = signal.T.astype(bf16)
        for step in range(count):
            outs[step] = sig_t[step * chan : (step + 1) * chan, :]

    def call(sc, x, halo, params, own, rcv):
        return run(
            body,
            [((shard_len, D), bf16), ((shard_len + HALO, 3 * D), bf16), TICK]
            + [((count, chan, shard_len), bf16)],
            (sc, x, halo, params, own, rcv),
            [SMEM, VMEM, VMEM, VMEM, ANY, ANY],
            [
                pltpu.VMEM((D, 3 * D), bf16),
                pltpu.VMEM((D, shard_len), bf16),
                pltpu.SemaphoreType.DMA((3,)),
            ],
            f"in_part_{block}",
            2 * shard_len * D * 3 * D,
            D * 3 * D * 2,
        )

    return call


def piece_scalars(sc):
    starts = [sc[2 + doc] for doc in range(NDOCS)] + [SEQ]
    lows, offsets = [], [0]
    for doc in range(NDOCS):
        low, high = starts[doc] // BLK, (starts[doc + 1] - 1) // BLK
        lows.append(low)
        offsets.append(offsets[-1] + high - low + 1)
    pieces = []
    for piece in range(PIECES):
        begin, stop, low, first, last = starts[0], starts[1], lows[0], offsets[0], offsets[1]
        for doc in range(1, NDOCS):
            here = piece >= offsets[doc]
            begin = jnp.where(here, starts[doc], begin)
            stop = jnp.where(here, starts[doc + 1], stop)
            low = jnp.where(here, lows[doc], low)
            first = jnp.where(here, offsets[doc], first)
            last = jnp.where(here, offsets[doc + 1], last)
        live = piece < offsets[NDOCS]
        blk = jnp.minimum(low + piece - first, NB - 1)
        begin = jnp.where(live, begin, 0)
        stop = jnp.where(live, stop, 0)
        first = jnp.where(live, first, piece + 1)
        last = jnp.where(live, last, piece)
        pieces.append((blk, begin, stop, first, last))
    return pieces


def piece_mask(piece):
    pos = piece[0] * BLK + lax.broadcasted_iota(jnp.int32, (1, BLK), 1)
    return (pos >= piece[1]) & (pos < piece[2])


def gather_blocks(sc, ins, blocks, per_shard):
    for source in range(NB // per_shard):
        for part in range(per_shard):
            blocks[source * per_shard + part] = ins[source, :, part * BLK : (part + 1) * BLK]


def to_freq(pieces, blocks, masked, freq, tables, chan):
    for index, piece in enumerate(pieces):
        keep = jnp.where(piece_mask(piece), 1.0, 0.0)
        masked[index * chan : (index + 1) * chan, :] = (
            blocks[piece[0]].astype(f32) * keep
        ).astype(bf16)
    values = masked[...]
    freq[...] = dot(values, tables[0][...]) + dot(values, tables[1][...])


def from_freq(pieces, freq, out_blocks, tables, chan):
    values = freq[...]
    high = values.astype(bf16)
    low = (values - high.astype(f32)).astype(bf16)
    back = dot(high, tables[2][...]) + dot(low, tables[2][...]) + dot(high, tables[3][...])
    for index, piece in enumerate(pieces):
        mine = back[index * chan : (index + 1) * chan, :]
        before = out_blocks[piece[0]]
        out_blocks[piece[0]] = jnp.where(piece_mask(piece), mine, before)


def scatter_blocks(sc, outs, out_blocks, per_shard):
    for target in range(NB // per_shard):
        for part in range(per_shard):
            outs[target, :, part * BLK : (part + 1) * BLK] = out_blocks[
                target * per_shard + part
            ].astype(bf16)


def conv_part(block, shard_len, count):
    chan = D // count
    per_shard = shard_len // BLK
    tiles = chan // TILE

    def body(sc, filt, *rest):
        ins, tables, rest = rest[0], rest[1:5], rest[5:]
        outs, blocks, tick_ref = rest[:3]
        masked, freq, total, out_blocks = rest[3:]
        tick_ref[0, 0] = 0.0
        gather_blocks(sc, ins, blocks, per_shard)
        pieces = piece_scalars(sc)
        to_freq(pieces, blocks, masked, freq, tables, chan)
        for index, piece in enumerate(pieces):
            for tile in range(tiles):

                def step(other, carry, index=index, piece=piece, tile=tile):
                    sum_re, sum_im = carry
                    rows = rows_at(other * chan + tile * TILE, TILE)
                    sig_re, sig_im = freq[rows, :BLK], freq[rows, BLK:]
                    lag = index - other
                    here = slice(tile * TILE, (tile + 1) * TILE)
                    fil_re, fil_im = filt[lag, here, :BLK], filt[lag, here, BLK:]
                    return (
                        sum_re + fil_re * sig_re - fil_im * sig_im,
                        sum_im + fil_re * sig_im + fil_im * sig_re,
                    )

                zero = jnp.zeros((TILE, BLK), f32)
                sum_re, sum_im = lax.fori_loop(piece[3], index + 1, step, (zero, zero))
                here = slice(index * chan + tile * TILE, index * chan + (tile + 1) * TILE)
                total[here, :BLK] = sum_re
                total[here, BLK:] = sum_im
        out_blocks[...] = jnp.zeros_like(out_blocks)
        from_freq(pieces, total, out_blocks, tables, chan)
        scatter_blocks(sc, outs, out_blocks, per_shard)

    def call(sc, filt, ins, tables):
        return run(
            body,
            [((count, chan, shard_len), bf16), ((NB, chan, BLK), bf16), TICK],
            (sc, filt, ins, *tables),
            [SMEM] + [VMEM] * 6,
            [
                pltpu.VMEM((PIECES * chan, BLK), bf16),
                pltpu.VMEM((PIECES * chan, FREQ), f32),
                pltpu.VMEM((PIECES * chan, FREQ), f32),
                pltpu.VMEM((NB, chan, BLK), f32),
            ],
            f"conv_part_{block}",
            10 * PIECES * chan * BLK * FREQ,
            NB * chan * FREQ * 4,
        )

    return call


def conv_back(block, shard_len, count):
    chan = D // count
    per_shard = shard_len // BLK
    tiles = chan // TILE

    def body(sc, filt, blocks, *rest):
        ins, tables, rest = rest[0], rest[1:5], rest[5:]
        outs, d_filt, tick_ref = rest[:3]
        d_blocks, masked, freq, d_freq, total, out_blocks = rest[3:]
        tick_ref[0, 0] = 0.0
        gather_blocks(sc, ins, d_blocks, per_shard)
        pieces = piece_scalars(sc)
        to_freq(pieces, blocks, masked, freq, tables, chan)
        to_freq(pieces, d_blocks, masked, d_freq, tables, chan)
        d_filt[...] = jnp.zeros_like(d_filt)
        for index, piece in enumerate(pieces):
            for tile in range(tiles):
                rows = slice(index * chan + tile * TILE, index * chan + (tile + 1) * TILE)
                here = slice(tile * TILE, (tile + 1) * TILE)

                def step(other, carry, index=index, here=here, rows=rows, tile=tile):
                    sum_re, sum_im = carry
                    sig_re, sig_im = freq[rows, :BLK], freq[rows, BLK:]
                    there = rows_at(other * chan + tile * TILE, TILE)
                    der_re, der_im = d_freq[there, :BLK], d_freq[there, BLK:]
                    lag = other - index
                    fil_re, fil_im = filt[lag, here, :BLK], filt[lag, here, BLK:]
                    d_filt[lag, here, :BLK] += sig_re * der_re + sig_im * der_im
                    d_filt[lag, here, BLK:] += sig_re * der_im - sig_im * der_re
                    return (
                        sum_re + fil_re * der_re + fil_im * der_im,
                        sum_im + fil_re * der_im - fil_im * der_re,
                    )

                zero = jnp.zeros((TILE, BLK), f32)
                sum_re, sum_im = lax.fori_loop(index, piece[4], step, (zero, zero))
                total[rows, :BLK] = sum_re
                total[rows, BLK:] = sum_im
        out_blocks[...] = jnp.zeros_like(out_blocks)
        from_freq(pieces, total, out_blocks, tables, chan)
        scatter_blocks(sc, outs, out_blocks, per_shard)

    def call(sc, filt, blocks, ins, tables, deps):
        return run(
            body,
            [((count, chan, shard_len), bf16), ((NB, chan, FREQ), f32), TICK],
            (sc, filt, blocks, ins, *tables),
            [SMEM] + [VMEM] * 7,
            [
                pltpu.VMEM((NB, chan, BLK), bf16),
                pltpu.VMEM((PIECES * chan, BLK), bf16),
                pltpu.VMEM((PIECES * chan, FREQ), f32),
                pltpu.VMEM((PIECES * chan, FREQ), f32),
                pltpu.VMEM((PIECES * chan, FREQ), f32),
                pltpu.VMEM((NB, chan, BLK), f32),
            ],
            f"conv_back_{block}",
            14 * PIECES * chan * BLK * FREQ,
            NB * chan * FREQ * 8,
            deps,
        )

    return call


def token_major(ins):
    return ins[...].reshape(D, ins.shape[2]).astype(f32).T


def weight_scratch():
    return [
        pltpu.VMEM((D, D), bf16),
        pltpu.VMEM((D, FF), bf16),
        pltpu.VMEM((FF, D), bf16),
        pltpu.SemaphoreType.DMA((1 + 2 * (FF // FF_TILE),)),
    ]


def fetch_mlp(own_first, pairs, dsts, sems, out_first):
    tiles = FF // FF_TILE
    (out_own, out_rcv), (up_own, up_rcv), (down_own, down_rcv) = pairs
    w_out, w_up, w_down = dsts

    def start_out():
        fetch(own_first, out_own.at[0], out_rcv.at[0], w_out, sems.at[0])

    def start_up(tile):
        cols = pl.ds(tile * FF_TILE, FF_TILE)
        fetch(
            own_first,
            up_own.at[0, :, cols],
            up_rcv.at[0, :, cols],
            w_up.at[:, cols],
            sems.at[1 + tile],
        )

    def start_down(tile):
        rows = pl.ds(tile * FF_TILE, FF_TILE)
        fetch(
            own_first,
            down_own.at[0, rows],
            down_rcv.at[0, rows],
            w_down.at[rows],
            sems.at[1 + tiles + tile],
        )

    if out_first:
        start_out()
    for tile in range(tiles):
        if out_first:
            start_up(tile)
            start_down(tile)
        else:
            start_down(tile)
            start_up(tile)
    if not out_first:
        start_out()

    def wait_out():
        pltpu.make_async_copy(out_own.at[0], w_out, sems.at[0]).wait()

    def wait_up(tile):
        cols = pl.ds(pl.multiple_of(tile * FF_TILE, FF_TILE), FF_TILE)
        pltpu.make_async_copy(up_own.at[0, :, cols], w_up.at[:, cols], sems.at[1 + tile]).wait()
        return cols

    def wait_down(tile):
        rows = pl.ds(pl.multiple_of(tile * FF_TILE, FF_TILE), FF_TILE)
        pltpu.make_async_copy(
            down_own.at[0, rows], w_down.at[rows], sems.at[1 + tiles + tile]
        ).wait()
        return rows

    return wait_out, wait_up, wait_down


GELU_SCALE = 0.7978845608028654
GELU_CUBE = 0.044715


def out_part(block, shard_len, count):
    chan = D // count

    def body(sc, x_ref, st_ref, normed_one, p_ref, bias_ref, *rest):
        ins, rest = rest[0], rest[1:]
        pairs = (rest[0:2], rest[2:4], rest[4:6])
        result_ref, residual_ref, mine_ref, other_ref, slope_ref, cmix_ref = rest[6:12]
        w_out, w_up, w_down, sems, normed_ref, gated_ref, hidden_ref = rest[12:]

        def keep_halves(ref, start, half):
            for side, target in ((sc[0], mine_ref), (1 - sc[0], other_ref)):
                cols = pl.ds(pl.multiple_of(side * half, half), half)
                target[:, start : start + half] = ref[:, cols]

        wait_out, wait_up, wait_down = fetch_mlp(
            sc[0] == block, pairs, (w_out, w_up, w_down), sems, True
        )
        masks = place_masks(sc, shard_len, shard_len)
        conv = token_major(ins)
        signal = short_conv(st_ref, p_ref, 2, masks) * short_conv(st_ref, p_ref, 1, masks)
        cmix = conv + p_ref[21:22, :] * signal
        cmix_ref[...] = cmix
        gated = (cmix * short_conv(st_ref, p_ref, 0, masks)).astype(bf16)
        gated_ref[...] = gated
        wait_out()
        residual = x_ref[...].astype(f32) + dot(gated, w_out[...]) + p_ref[3:4, :]
        residual_ref[...] = residual
        unit, _ = norm_stats(residual)
        normed_ref[...] = (unit * p_ref[1:2, :] + p_ref[4:5, :]).astype(bf16)
        result_ref[...] = residual + p_ref[5:6, :]

        @pl.loop(0, FF // FF_TILE)
        def _(tile):
            cols = wait_up(tile)
            pre = dot(normed_ref[...], w_up[:, cols]) + bias_ref[:, cols]
            square = pre * pre
            bent = jnp.tanh(GELU_SCALE * pre * (1.0 + GELU_CUBE * square))
            half = 0.5 * (1.0 + bent)
            slope = half + (0.5 * GELU_SCALE) * pre * (1.0 - bent * bent) * (
                1.0 + 3.0 * GELU_CUBE * square
            )
            hidden = (pre * half).astype(bf16)
            hidden_ref[:, cols] = hidden
            slope_ref[:, cols] = slope.astype(bf16)
            rows = wait_down(tile)
            result_ref[...] += dot(hidden, w_down[rows, :])

        keep_halves(hidden_ref, ACT_HIDDEN, FF // 2)
        keep_halves(normed_ref, ACT_TWO, HALF)
        keep_halves(gated_ref, ACT_GATED, HALF)
        keep_halves(normed_one, ACT_NORMED, HALF)

    def call(sc, x, st, normed, params, up_bias, ins, weights):
        return run(
            body,
            [
                ((shard_len, D), f32),
                ((shard_len, D), f32),
                ((shard_len, ACT_COLS), bf16),
                ((shard_len, ACT_COLS), bf16),
                ((shard_len, FF), bf16),
                ((shard_len, D), f32),
            ],
            (sc, x, st, normed, params, up_bias, ins, *weights),
            [SMEM] + [VMEM] * 6 + [ANY] * 6,
            weight_scratch()
            + [
                pltpu.VMEM((shard_len, D), bf16),
                pltpu.VMEM((shard_len, D), bf16),
                pltpu.VMEM((shard_len, FF), bf16),
            ],
            f"out_part_{block}",
            2 * shard_len * D * (D + 2 * FF),
            D * (D + 2 * FF) * 2,
        )

    return call


def out_back(block, shard_len, count):
    chan = D // count

    def body(sc, grad_ref, residual_ref, slope_ref, st_ref, p_ref, *rest):
        pairs = (rest[0:2], rest[2:4], rest[4:6])
        grads_ref, dres_ref, dg_ref, vec_ref, dub_ref, tick_ref = rest[6:12]
        outs, rest = rest[12], rest[13:]
        tick_ref[0, 0] = 0.0
        turned, w_out, w_up, w_down, sems, total = rest
        wait_out, wait_up, wait_down = fetch_mlp(
            sc[0] == block, pairs, (w_out, w_up, w_down), sems, False
        )
        grad = grad_ref[...].astype(f32)
        gm = grad.astype(bf16)
        grads_ref[:, GRAD_MLP : GRAD_MLP + D] = gm
        total[...] = jnp.zeros_like(total)

        @pl.loop(0, FF // FF_TILE)
        def _(tile):
            rows = wait_down(tile)
            d_hidden = dot(grads_ref[:, GRAD_MLP : GRAD_MLP + D], w_down[rows, :], NT)
            d_pre = (d_hidden * slope_ref[:, rows].astype(f32)).astype(bf16)
            grads_ref[:, rows] = d_pre
            dub_ref[:, rows] = jnp.broadcast_to(col_sum(d_pre.astype(f32)), (8, FF_TILE))
            cols = wait_up(tile)
            total[...] += dot(d_pre, w_up[:, cols], NT)

        d_normed = total[...]
        unit, scale = norm_stats(residual_ref[...])
        d_res = grad + norm_back(d_normed, p_ref[1:2, :], unit, scale)
        dres_ref[...] = d_res
        gb = d_res.astype(bf16)
        grads_ref[:, GRAD_BRANCH : GRAD_BRANCH + D] = gb
        wait_out()
        dg = dot(gb, w_out[...], NT).astype(bf16)
        dg_ref[...] = dg
        masks = place_masks(sc, shard_len, shard_len)
        d_conv = dg.astype(f32) * short_conv(st_ref, p_ref, 0, masks)
        turned[...] = d_conv.T.astype(bf16)
        for step in range(count):
            outs[step] = turned[step * chan : (step + 1) * chan, :]
        vec_ref[...] = jnp.concatenate(
            [
                col_sum(d_normed * unit),
                col_sum(d_normed),
                col_sum(gb.astype(f32)),
                col_sum(gm.astype(f32)),
                jnp.zeros((4, D), f32),
            ],
            axis=0,
        )

    def call(sc, grad, residual, slope, st, params, weights, deps):
        return run(
            body,
            [
                ((shard_len, GRAD_COLS), bf16),
                ((shard_len, D), f32),
                ((shard_len, D), bf16),
                ((8, D), f32),
                ((8, FF), f32),
                TICK,
            ]
            + [((count, chan, shard_len), bf16)],
            (sc, grad, residual, slope, st, params, *weights),
            [SMEM] + [VMEM] * 5 + [ANY] * 6,
            [pltpu.VMEM((D, shard_len), bf16)]
            + weight_scratch()
            + [pltpu.VMEM((shard_len, D), f32)],
            f"out_back_{block}",
            2 * shard_len * D * (D + 2 * FF),
            D * (D + 2 * FF) * 2,
            deps,
        )

    return call


def short_back(block, shard_len, count):
    chan = D // count

    def body(sc, st_ref, dg_ref, cmix_ref, p_ref, *rest):
        ins, ds_ref, head_ref, vec_ref, tick_ref = rest
        tick_ref[0, 0] = 0.0
        masks = place_masks(sc, shard_len, shard_len)
        d_signal = token_major(ins)
        dg = dg_ref[...].astype(f32)
        d_conv = dg * short_conv(st_ref, p_ref, 0, masks)
        inner = short_conv(st_ref, p_ref, 1, masks)
        value = short_conv(st_ref, p_ref, 2, masks)
        d_signal = d_signal + p_ref[21:22, :] * d_conv
        rows = [None] * 16
        rows[12] = col_sum(d_conv * value * inner)
        for stream, d_short in enumerate((dg * cmix_ref[...], d_signal * value, d_signal * inner)):
            cols = slice(stream * D, (stream + 1) * D)
            ds_ref[:, cols] = d_short
            head_ref[:, cols] = d_short[:HALO]
            zero, one, two = shifted(st_ref[:, cols])
            rows[stream] = col_sum(d_short * zero)
            rows[3 + stream] = col_sum(d_short * (one * masks[0]))
            rows[6 + stream] = col_sum(d_short * (two * masks[1]))
            rows[9 + stream] = col_sum(d_short)
        for index in range(13, 16):
            rows[index] = jnp.zeros((1, D), f32)
        vec_ref[...] = jnp.concatenate(rows, axis=0)

    def call(sc, st, dg, cmix, params, ins, deps):
        return run(
            body,
            [((shard_len, 3 * D), f32), ((HALO, 3 * D), f32), ((16, D), f32), TICK],
            (sc, st, dg, cmix, params, ins),
            [SMEM] + [VMEM] * 5,
            [],
            f"short_back_{block}",
            40 * shard_len * D,
            shard_len * D * 20,
            deps,
        )

    return call


def in_back(block, shard_len):
    def body(sc, ds_ref, halo_ref, x_ref, dres_ref, p_ref, own, rcv, dst_ref, dx_ref, vec_ref, weight, sems):
        wait = fetch_in(sc[0] == block, own, rcv, weight, sems)
        long = shard_len + HALO
        one, two = place_masks(sc, long, shard_len)
        d_normed = jnp.zeros((shard_len, D), f32)
        rows = []
        for stream in range(3):
            cols = slice(stream * D, (stream + 1) * D)
            ext = jnp.concatenate([ds_ref[:, cols], halo_ref[:, cols]], axis=0)
            d_stream = (
                mix_row(p_ref, 1, stream) * ext[:shard_len]
                + mix_row(p_ref, 2, stream) * pltpu.roll(ext * one, long - 1, 0)[:shard_len]
                + mix_row(p_ref, 3, stream) * pltpu.roll(ext * two, long - 2, 0)[:shard_len]
            ).astype(bf16)
            dst_ref[:, cols] = d_stream
            rows.append(col_sum(d_stream.astype(f32)))
            wait(stream)
            d_normed = d_normed + dot(d_stream, weight[:, cols], NT)
        unit, scale = norm_stats(x_ref[...].astype(f32))
        dx_ref[...] = dres_ref[...] + norm_back(d_normed, p_ref[0:1, :], unit, scale)
        vec_ref[...] = jnp.concatenate(
            [col_sum(d_normed * unit), col_sum(d_normed)] + rows + [jnp.zeros((3, D), f32)], axis=0
        )

    def call(sc, d_short, halo, x, d_res, params, own, rcv, deps):
        return run(
            body,
            [((shard_len, 3 * D), bf16), ((shard_len, D), f32), ((8, D), f32)],
            (sc, d_short, halo, x, d_res, params, own, rcv),
            [SMEM] + [VMEM] * 5 + [ANY] * 2,
            [pltpu.VMEM((D, 3 * D), bf16), pltpu.SemaphoreType.DMA((3,))],
            f"in_back_{block}",
            2 * shard_len * D * 3 * D,
            D * 3 * D * 2,
            deps,
        )

    return call


def weight_grad(name, parts, first_bits, shard_len, shards, count):
    groups = len(first_bits)
    sizes = [0] * groups
    for _, rows, _, cols, splits in parts:
        for group, _, size in splits:
            sizes[group] += size * (cols // HALF)
    shapes, firsts = [], []
    for size, bit in zip(sizes, first_bits):
        firsts.append(len(shapes))
        shapes += [(shards, size, HALF)] if bit is None else [(shards // 2, size, HALF)] * 2

    def body(sc, g_own, g_rcv, a_own, a_rcv, *outs):
        outs[-1][0, 0] = 0.0
        me = sc[2 + NDOCS] * count
        bases = [0] * groups
        for g_start, rows, a_start, cols, splits in parts:
            block = rows // shards
            chunk = 8 * block if block % 32 else 4 * block
            acts = slice(a_start, a_start + cols)
            starts = list(bases)

            @pl.loop(0, rows // chunk)
            def _(step, starts=starts, g_start=g_start, chunk=chunk, block=block, acts=acts, cols=cols, splits=splits):
                here = pl.ds(pl.multiple_of(g_start + step * chunk, 128), chunk)
                full = dot(g_own[:, here], a_own[:, acts], TN) + dot(g_rcv[:, here], a_rcv[:, acts], TN)
                for index in range(chunk // block):
                    device = step * (chunk // block) + index
                    for group, begin, size in splits:
                        bit = first_bits[group]
                        if bit is None:
                            slot = device
                        else:
                            away = device ^ me
                            low = away & ((1 << bit) - 1)
                            slot = ((away >> (bit + 1)) << bit) | low
                            sent = (away >> bit) & 1

                        def store(ref, group=group, begin=begin, size=size, slot=slot, index=index):
                            for part in range(cols // HALF):
                                top = starts[group] + part * size
                                ref[slot, top : top + size, :] = full[
                                    index * block + begin : index * block + begin + size,
                                    part * HALF : (part + 1) * HALF,
                                ].astype(bf16)

                        first = firsts[group]
                        if bit is None:
                            store(outs[first])
                        else:
                            pl.when(sent == 1)(functools.partial(store, outs[first]))
                            pl.when(sent == 0)(functools.partial(store, outs[first + 1]))

            for group, _, size in splits:
                bases[group] += size * (cols // HALF)

    def call(sc, *ins, deps=()):
        flops = sum(4 * shard_len * rows * cols for _, rows, _, cols, _ in parts)
        outs = run(
            body,
            [(shape, bf16) for shape in shapes] + [TICK],
            (sc, *ins),
            [SMEM] + [VMEM] * 4,
            [],
            name,
            flops,
            flops // 256,
            deps,
        )
        return [
            outs[first] if bit is None else outs[first : first + 2]
            for first, bit in zip(firsts, first_bits)
        ], outs[-1]

    return call


def weight_grad_plain(parts, first_bits, shards, me):
    groups = len(first_bits)

    def call(_, g_own, g_rcv, a_own, a_rcv, deps=()):
        gathered = [[] for _ in range(groups)]
        for g_start, rows, a_start, cols, splits in parts:
            block = rows // shards
            full = sum(
                jnp.einsum(
                    "tn,tk->nk",
                    g[:, g_start : g_start + rows],
                    a[:, a_start : a_start + cols],
                    preferred_element_type=f32,
                )
                for g, a in ((g_own, a_own), (g_rcv, a_rcv))
            ).astype(bf16)
            full = full.reshape(shards, block, cols // HALF, HALF).transpose(0, 2, 1, 3)
            for group, begin, size in splits:
                piece = full[:, :, begin : begin + size]
                gathered[group].append(piece.reshape(shards, -1, HALF))
        outs = []
        for group in range(groups):
            whole = jnp.concatenate(gathered[group], axis=1)
            bit = first_bits[group]
            if bit is None:
                outs.append(whole)
                continue
            whole = whole[jnp.arange(shards, dtype=jnp.int32) ^ me]
            whole = whole.reshape((shards >> (bit + 1), 2, 1 << bit) + whole.shape[1:])
            outs.append(
                [whole[:, side].reshape((shards // 2,) + whole.shape[3:]) for side in (1, 0)]
            )
        return outs, jnp.zeros((1, 1), f32)

    return call


def halving(name, shapes, count):
    def body(*refs):
        groups = len(shapes)
        refs[-1][0, 0] = 0.0
        for group in range(groups):
            kept, got = refs[2 * group : 2 * group + 2]
            send, keep = refs[2 * groups + 2 * group : 2 * groups + 2 * group + 2]
            send[0, 0] = (kept[0, 1, 0].astype(f32) + got[0, 1, 0].astype(f32)).astype(bf16)
            keep[0, 0] = (kept[0, 0, 0].astype(f32) + got[0, 0, 0].astype(f32)).astype(bf16)

    def call(terms, spots, deps):
        ins, outs, in_specs, out_specs = [], [], [], []
        steps = None
        for (kept, got), spot in zip(terms, spots):
            blocks, rows, cols = kept.shape
            inner = count << spot
            outer = blocks // (2 * inner)
            steps = outer * inner
            ins += [v.reshape(outer, 2, inner, rows, cols) for v in (kept, got)]
            in_specs += [
                pl.BlockSpec((1, 2, 1, rows, cols), lambda i, inner=inner: (i // inner, 0, i % inner, 0, 0))
            ] * 2
            outs += [jax.ShapeDtypeStruct((outer, inner, rows, cols), bf16)] * 2
            out_specs += [
                pl.BlockSpec((1, 1, rows, cols), lambda i, inner=inner: (i // inner, i % inner, 0, 0))
            ] * 2
        taken = len(ins)

        def wrapped(*refs):
            body(*refs[:taken], *refs[taken + len(deps) :])

        values = pl.pallas_call(
            wrapped,
            grid=(steps,),
            out_shape=outs + [jax.ShapeDtypeStruct(*TICK)],
            in_specs=in_specs + [ANY] * len(deps),
            out_specs=out_specs + [SMEM],
            compiler_params=pltpu.CompilerParams(vmem_limit_bytes=VMEM_LIMIT),
            cost_estimate=pl.CostEstimate(flops=1, bytes_accessed=1, transcendentals=0),
            name=name,
        )(*ins, *deps)
        flat = [v.reshape((-1,) + v.shape[2:]) for v in values[:-1]]
        return [flat[2 * group : 2 * group + 2] for group in range(len(terms))], values[-1]

    return call


def pairs(count, step):
    return [(index, index ^ step) for index in range(count)]


def swap(value):
    return lax.ppermute(value, "section", pairs(2, 1))


def exchange(chunks):
    return lax.all_to_all(chunks, "seq", split_axis=0, concat_axis=0, tiled=True)


def add_round(first, second, tick):
    return (first.astype(f32) + second.astype(f32) + tick[0, 0]).astype(bf16)


class Reduction:
    def __init__(self, groups, dp_count, count):
        self.sizes = (dp_count, count)
        self.terms = []
        for (sent, kept), bits in groups:
            self.terms.append((kept, self.over_dp(sent, bits[0]), list(bits[1:])))

    def over_dp(self, value, bit):
        return lax.ppermute(value, "dp", pairs(self.sizes[0], (1 << bit) // self.sizes[1]))

    def plane(self, name, tick, deps=()):
        for turn in range(len(self.terms[0][2])):
            spots = [sum(1 for other in left[1:] if other < left[0]) for _, _, left in self.terms]
            values, tick = halving(f"{name}_{turn}", self.terms, self.sizes[1])(
                [(kept, got) for kept, got, _ in self.terms], spots, [tick, *deps]
            )
            self.terms = [
                (keep, self.over_dp(send, left[0]), left[1:])
                for (send, keep), (_, _, left) in zip(values, self.terms)
            ]
        return tick

    def rest(self, tick):
        return jnp.concatenate([add_round(kept, got, tick) for kept, got, _ in self.terms], axis=1)


def line_sum(values):
    return jnp.sum(exchange(values).astype(f32), axis=0)


def scatter(value, axis):
    blocks, rows, cols = value.shape
    value = value.reshape(blocks * rows, cols)
    return lax.psum_scatter(value, axis, scatter_dimension=0, tiled=True).reshape(-1, rows, cols)


def mat(spec, left, right):
    return jnp.einsum(spec, left, right, precision=highest, preferred_element_type=f32)


def filter_state(net, last, decay, pos, window):
    first_w, inner_b, second_w = net[:EMB], net[EMB : EMB + 2], net[EMB + 2 :]
    pre_a = mat("ef,en->fn", first_w, pos) + inner_b[0][:, None]
    hid_a = jnp.sin(pre_a)
    pre_b = mat("gf,gn->fn", second_w, hid_a) + inner_b[1][:, None]
    hid_b = jnp.sin(pre_b)
    taps = mat("fc,fn->cn", last, hid_b) * decay
    blocks = taps.reshape(taps.shape[0], NB, BLK)
    filt = mat("cmn,nk->mck", blocks, window[BLK:])
    behind = mat("cmn,nk->mck", blocks[:, :-1], window[:BLK])
    filt = filt + jnp.pad(behind, ((1, 0), (0, 0), (0, 0)))
    energy = taps * taps
    share = jnp.sum(jnp.sum(energy[:, LONG_LAG:], axis=1) / (jnp.sum(energy, axis=1) + 1e-06))
    return filt, share, (pre_a, hid_a, pre_b, hid_b, second_w)


def filter_back(d_filt, state, last, decay, pos, window):
    pre_a, hid_a, pre_b, hid_b, second_w = state
    ahead = jnp.pad(d_filt[1:], ((0, 1), (0, 0), (0, 0)))
    d_taps = mat("mck,nk->cmn", d_filt, window[BLK:]) + mat("mck,nk->cmn", ahead, window[:BLK])
    d_out = d_taps.reshape(last.shape[1], SEQ) * (decay / BLK)
    d_last = mat("fn,cn->fc", hid_b, d_out)
    d_b = mat("fc,cn->fn", last, d_out) * jnp.cos(pre_b)
    d_second = mat("gn,fn->gf", hid_a, d_b)
    d_a = mat("gf,fn->gn", second_w, d_b) * jnp.cos(pre_a)
    d_first = mat("en,fn->ef", pos, d_a)
    d_inner = jnp.stack([jnp.sum(d_a, axis=1), jnp.sum(d_b, axis=1)])
    return d_last, jnp.concatenate([d_first, d_inner, d_second], axis=0)


def local(
    layer_input,
    out_cot,
    doc_lengths,
    norm_gains,
    biases,
    in_weight,
    mix_vecs,
    filt_first,
    filt_inner_bias,
    filt_second,
    filt_last,
    filt_skip,
    out_weight,
    up_weight,
    up_bias,
    down_weight,
):
    count = lax.axis_size("seq")
    dp_count = lax.axis_size("dp")
    section = lax.axis_index("section")
    place = lax.axis_index("seq")
    first = section == 0
    shard_len = layer_input.shape[2]
    chan = D // count
    fwd_hi, fwd_lo, inv_hi, inv_lo, window = block_tables()
    tables = tuple(jnp.asarray(t) for t in (fwd_hi, fwd_lo, inv_hi, inv_lo))
    window = jnp.asarray(window)
    pos = jnp.asarray(position_table())

    def own_micro(value):
        return lax.dynamic_index_in_dim(value, section, 0, keepdims=False)[0]

    x_zero = own_micro(layer_input)
    cot = own_micro(out_cot)
    lengths = own_micro(doc_lengths)
    starts = jnp.cumsum(lengths) - lengths
    sc = jnp.concatenate(
        [jnp.stack([section, place]), starts, lax.axis_index("dp")[None]]
    ).astype(jnp.int32)

    def behind(rows):
        return lax.ppermute(rows, "seq", [(index, index + 1) for index in range(count - 1)])

    def ahead(rows):
        return lax.ppermute(rows, "seq", [(index + 1, index) for index in range(count - 1)])

    halo = behind(x_zero[-HALO:])
    small = jnp.concatenate(
        [
            norm_gains[0],
            biases[0],
            mix_vecs[0].reshape(15, D),
            filt_skip[0],
            up_bias[0].reshape(4, D),
            filt_last[0],
        ],
        axis=0,
    )
    net = jnp.concatenate([filt_first[0], filt_inner_bias[0], filt_second[0]], axis=0)
    small_rcv, net_rcv = swap(small), swap(net)
    rcv_in, rcv_out, rcv_up, rcv_down = (
        swap(in_weight),
        swap(out_weight),
        swap(up_weight),
        swap(down_weight),
    )
    mlp_pairs = (out_weight, rcv_out, up_weight, rcv_up, down_weight, rcv_down)
    params, nets = [], []
    for block in range(2):
        mine = section == block
        params.append(jnp.where(mine, small, small_rcv).astype(f32))
        nets.append(jnp.where(mine, net, net_rcv).astype(f32))
    tokens = [p[:24] for p in params]
    up_biases = [p[22:26].reshape(1, FF) for p in params]
    lasts = [lax.dynamic_slice_in_dim(p[26:90], place * chan, chan, 1) for p in params]
    chan_ids = (jnp.arange(chan, dtype=jnp.int32) + place * chan).astype(f32)
    times = jnp.arange(SEQ, dtype=f32) / SEQ
    decay = jnp.exp(-(3.0 + 12.0 * chan_ids / (D - 1))[:, None] * times[None, :])

    x = x_zero
    kept = []
    results = []
    filters = []
    for block in range(2):
        normed, st, tick, chunks = in_part(block, shard_len, count)(
            sc, x, halo, tokens[block], in_weight, rcv_in
        )
        if block == 0:
            filters.append(filter_state(nets[0] + tick[0, 0], lasts[0], decay, pos, window))
        chunks, blocks, tick = conv_part(block, shard_len, count)(
            sc, filters[block][0], exchange(chunks), tables
        )
        if block == 0:
            filters.append(filter_state(nets[1] + tick[0, 0], lasts[1], decay, pos, window))
        result, residual, acts, acts_other, slope, cmix = out_part(block, shard_len, count)(
            sc, x, st, normed, tokens[block], up_biases[block], exchange(chunks), mlp_pairs
        )
        kept.append((x, st, blocks, residual, acts, swap(acts_other), slope, cmix))
        results.append(result)
        x = result
        if block == 0:
            halo = behind(result[-HALO:])

    def choose(values):
        return jnp.where(first, values[0], values[1]), jnp.where(first, values[1], values[0])

    def swapped(values):
        mine, other = choose(values)
        got = swap(other)
        return jnp.stack([jnp.where(first, mine, got), jnp.where(first, got, mine)]), [got]

    outputs, got_results = swapped(results)
    shards = dp_count * count
    shard = lax.axis_index("dp") * count + place
    low_bit = count.bit_length() - 1
    up_bits = list(range(low_bit, low_bit + dp_count.bit_length() - 1))
    down_bits = up_bits[::-1]
    rows, wide_rows, ff_rows = D // shards, 3 * D // shards, FF // shards
    split = SPLIT if wide_rows > SPLIT else wide_rows // 2
    parts_a = [
        (GRAD_MLP, D, ACT_HIDDEN, FF // 2, [(0, 0, rows)]),
        (GRAD_BRANCH, D, ACT_GATED, HALF, [(0, 0, rows)]),
    ]
    parts_b = [(GRAD_PRE, FF, ACT_TWO, HALF, [(0, 0, ff_rows)])]
    parts_in = [(0, 3 * D, ACT_NORMED, HALF, [(0, 0, split), (1, split, wide_rows - split)])]
    parts_early = parts_a + parts_b
    parts_in_one = [(0, 3 * D, ACT_NORMED, HALF, [(0, 0, wide_rows)])]
    whole_tiles = rows % 16 == 0

    def grads_of(name, parts, first_bits):
        if whole_tiles:
            return weight_grad(name, parts, first_bits, shard_len, shards, count)
        return weight_grad_plain(parts, first_bits, shards, shard - place)

    def back(block, grad, wait_out, wait_conv, wait_short, wait_in):
        x, st, blocks, residual, acts, acts_got, slope, cmix = kept[block]
        grads, d_res, dg, vec_out, d_up_bias, tick, chunks = out_back(block, shard_len, count)(
            sc, grad, residual, slope, st, tokens[block], mlp_pairs, wait_out
        )
        state = dict(grads=(grads, swap(grads), acts, acts_got), acts=(acts, acts_got))
        chunks, d_filt, tick = conv_back(block, shard_len, count)(
            sc, filters[block][0], blocks, exchange(chunks), tables, wait_conv(state, tick)
        )
        state["d_filt"] = d_filt
        d_short, head, vec_short, tick = short_back(block, shard_len, count)(
            sc, st, dg, cmix, tokens[block], exchange(chunks), wait_short(state, tick)
        )
        d_st, d_x, vec_in = in_back(block, shard_len)(
            sc, d_short, ahead(head), x, d_res, tokens[block], in_weight, rcv_in, wait_in(state, tick)
        )
        state["grads_in"] = (d_st, swap(d_st), acts, acts_got)
        state["vecs"] = (vec_in, vec_out, vec_short, d_up_bias)
        return d_x, state

    def grads_a(block, state, tick, bits):
        (value,), _ = grads_of(f"grad_a_{block}", parts_a, bits)(sc, *state["grads"], deps=[tick])
        state["a"] = value
        return list(value) if bits[0] is not None else [value]

    def grads_b(block, state, tick, bits):
        (value,), _ = grads_of(f"grad_b_{block}", parts_b, bits)(sc, *state["grads"], deps=[tick])
        state["b"] = value
        return list(value) if bits[0] is not None else [value]

    def early_one(state, tick):
        (value,), _ = grads_of("grad_early_1", parts_early, [None])(
            sc, *state["grads"], deps=[tick]
        )
        state["early"] = scatter(value, "dp")
        return [value]

    def net_grads(block, state, tick):
        return filter_back(
            state["d_filt"] + tick[0, 0], filters[block][2], lasts[block], decay, pos, window
        )

    d_mid, one = back(
        1, cot, [], lambda state, tick: list(got_results), early_one, lambda state, tick: []
    )

    def in_grads_one(state, tick):
        (value,), _ = grads_of("grad_in_1", parts_in_one, [None])(sc, *one["grads_in"], deps=[tick, one["early"]])
        one["late"] = scatter(value, "dp")
        return [value]

    def line_one(state, tick):
        value = jnp.concatenate([one["early"], one["late"]], axis=1)
        one["all"] = scatter(value, "seq")[0].astype(f32)
        return [value]

    d_start, zero = back(
        0,
        d_mid,
        [],
        lambda state, tick: grads_a(0, state, tick, up_bits[:1]),
        lambda state, tick: in_grads_one(state, tick) + grads_b(0, state, tick, down_bits[:1]),
        line_one,
    )
    in_grads, got_grads = swapped([d_start, d_mid])
    zero["early"] = Reduction([(zero["a"], up_bits), (zero["b"], down_bits)], dp_count, count)
    two, tick = grads_of("grad_in_0", parts_in, [up_bits[0], down_bits[0]])(
        sc, *zero["grads_in"], deps=got_grads
    )
    zero["late"] = Reduction([(two[0], up_bits), (two[1], down_bits)], dp_count, count)
    tick = zero["early"].plane("halve_early", tick)
    zero["net"] = net_grads(0, zero, tick)
    one["net"] = net_grads(1, one, tick)

    def cut(value):
        height, width = value.shape
        return value.reshape(height, shards, width // shards).swapaxes(0, 1).reshape(shards, -1)

    penalty = (filters[0][1] + 4.0 * filters[1][1]) / (chan * dp_count)
    penalty_high = penalty.astype(bf16)
    penalty_low = (penalty - penalty_high.astype(f32)).astype(bf16)
    packs = []
    for block, state in enumerate((zero, one)):
        vec_in, vec_out, vec_short, d_up_bias = state["vecs"]
        d_last, d_net = state["net"]
        vecs = jnp.concatenate(
            [
                vec_in[0:1],
                vec_out[0:1],
                vec_in[1:2],
                vec_out[2:3],
                vec_out[1:2],
                vec_out[3:4],
                vec_short[12:13],
            ],
            axis=0,
        )
        mixes = jnp.concatenate([vec_in[2:5], vec_short[0:12]], axis=0).reshape(5, 3 * D)
        last_full = lax.dynamic_update_slice_in_dim(
            jnp.zeros((FILT, D), f32), d_last, place * chan, 1
        )
        packs.append(
            jnp.concatenate(
                [
                    cut(vecs),
                    cut(mixes),
                    cut(d_up_bias[0:1]),
                    cut(last_full),
                    jnp.broadcast_to(d_net.reshape(1, -1), (shards, d_net.size)),
                ],
                axis=1,
            )
        )

    mine, other = choose(packs)
    got = swap(other.astype(bf16))
    pack = (mine + got.astype(f32)).astype(bf16)
    ends = jnp.broadcast_to(jnp.stack([penalty_high, penalty_low])[None], (shards, 2))
    pack = jnp.concatenate([pack, ends], axis=1)
    width = pack.shape[1]
    pack = jnp.pad(pack, ((0, 0), (0, -width % 1024))).reshape(shards, -1, 128)
    pack = lax.all_to_all(pack, ("dp", "seq"), split_axis=0, concat_axis=0, tiled=True)
    pack = jnp.sum(pack.astype(f32), axis=0).reshape(-1)

    tick = zero["late"].plane("halve_late", tick)
    left = jnp.concatenate([zero["early"].rest(tick), zero["late"].rest(tick)], axis=1)
    zero["all"] = line_sum(left)

    def turned(value):
        return value.swapaxes(-1, -2).reshape(1, -1, value.shape[-2])

    full, _ = swapped([zero["all"], one["all"]])
    down_rows = rows * (FF // D)
    edges = [down_rows, down_rows + rows, down_rows + rows + ff_rows]
    down = full[:, : edges[0]].reshape(2, FF // D, rows, HALF)
    taken = [0]

    def part(height, cols):
        begin = taken[0]
        taken[0] += height * cols
        return pack[begin : begin + height * cols].reshape(1, height, cols)

    vecs = part(7, rows)
    mixes = part(5, wide_rows)
    d_up_bias = part(1, ff_rows)
    d_last = part(FILT, rows)
    d_net = part(EMB + 2 + FILT, FILT)
    penalty = jnp.sum(part(1, 2))
    return (
        outputs[None, :, None],
        in_grads[None, :, None],
        vecs[:, 0:2],
        vecs[:, 2:6],
        turned(full[:, edges[2] :]),
        mixes,
        d_net[:, :EMB],
        d_net[:, EMB : EMB + 2],
        d_net[:, EMB + 2 :],
        d_last,
        vecs[:, 6:7],
        turned(full[:, edges[0] : edges[1]]),
        turned(full[:, edges[1] : edges[2]]),
        d_up_bias,
        turned(down),
        penalty,
    )


def solution(mesh):
    by_section = P("section")
    shard = P("section", None, ("dp", "seq"))
    tokens = P("section", None, "dp", "seq", None)
    return jax.shard_map(
        local,
        mesh=mesh,
        in_specs=(P(None, "dp", "seq", None), P(None, "dp", "seq", None), P(None, "dp", None))
        + (by_section,) * 13,
        out_specs=(tokens, tokens, shard, shard, shard, shard)
        + (by_section,) * 3
        + (shard,) * 6
        + (P(),),
        check_vma=False,
    )
```

```python
import functools

import jax
import jax.numpy as jnp
import ml_dtypes
import numpy as np
from jax import lax
from jax.experimental import pallas as pl
from jax.experimental.pallas import tpu as pltpu
from jax.sharding import PartitionSpec as P

D = 768
FF = 3072
EMB = 33
FILT = 64
SEQ = 1024
NDOCS = 3
LONG_LAG = 32
BLK = 128
NB = SEQ // BLK
FREQ = 2 * BLK
PIECES = NB + NDOCS - 1
HALO = 16
TILE = 48
FF_TILE = 512

eps = 1e-05
highest = lax.Precision.HIGHEST
f32 = jnp.float32
bf16 = jnp.bfloat16
TICK = ((1, 1), f32)
HALF = D // 2
ACT_HIDDEN = 0
ACT_TWO = FF // 2
ACT_GATED = ACT_TWO + HALF
ACT_NORMED = ACT_GATED + HALF
ACT_COLS = ACT_NORMED + HALF
GRAD_PRE = 0
GRAD_MLP = FF
GRAD_BRANCH = FF + D
GRAD_COLS = FF + 2 * D
SPLIT = 80
VMEM_LIMIT = 56 * 1024 * 1024


def split_table(table):
    high = table.astype(ml_dtypes.bfloat16)
    low = (table - high.astype(np.float64)).astype(ml_dtypes.bfloat16)
    return high, low


def ring_table(offsets):
    theta = 2.0 * np.pi * (np.arange(BLK) + 0.5) / FREQ
    angles = offsets[:, None] * theta[None, :]
    return np.concatenate([np.cos(angles), -np.sin(angles)], axis=1)


def block_tables():
    fwd = ring_table(np.arange(BLK, dtype=np.float64))
    fwd_hi, fwd_lo = split_table(fwd)
    inv_hi, inv_lo = split_table(fwd.T / BLK)
    window = ring_table(np.arange(FREQ, dtype=np.float64) - BLK)
    window[0] = 0.0
    return fwd_hi, fwd_lo, inv_hi, inv_lo, window.astype(np.float32)


def position_table():
    positions = np.arange(SEQ, dtype=np.float32)
    band_count = (EMB - 1) // 2
    band_freq = np.float32(0.0001) + np.arange(band_count, dtype=np.float32) * np.float32(
        (band_count - 1 - 0.0001) / (band_count - 1)
    )
    angles = np.float32(2.0 * np.pi / SEQ) * positions[:, None] * band_freq[None, :]
    return np.concatenate(
        [(positions / SEQ)[:, None], np.cos(angles), np.sin(angles)], axis=1
    ).T.astype(np.float32)


def dot(left, right, dims=((1,), (0,))):
    return lax.dot_general(left, right, (dims, ((), ())), preferred_element_type=f32)


NT = ((1,), (1,))
TN = ((0,), (0,))


def norm_stats(values):
    centre = jnp.mean(values, axis=-1, keepdims=True)
    centred = values - centre
    variance = jnp.mean(centred * centred, axis=-1, keepdims=True)
    scale = lax.rsqrt(variance + eps)
    return centred * scale, scale


def norm_back(grad, gain, unit, scale):
    scaled = grad * gain
    return scale * (
        scaled
        - jnp.mean(scaled, axis=-1, keepdims=True)
        - unit * jnp.mean(scaled * unit, axis=-1, keepdims=True)
    )


def col_sum(values):
    return jnp.sum(values, axis=0, keepdims=True)


def place_masks(sc, rows, shard_len):
    pos = sc[1] * shard_len + lax.broadcasted_iota(jnp.int32, (rows, 1), 0)
    starts = pos == sc[2]
    after = pos == sc[2] + 1
    for doc in range(1, NDOCS):
        starts = starts | (pos == sc[2 + doc])
        after = after | (pos == sc[2 + doc] + 1)
    one = jnp.where(starts, 0.0, 1.0)
    two = jnp.where(starts | after, 0.0, 1.0)
    return one, two


def shifted(stream_ext):
    ext = stream_ext.astype(f32)
    return (
        ext[HALO:],
        pltpu.roll(ext, 1, 0)[HALO:],
        pltpu.roll(ext, 2, 0)[HALO:],
    )


def mix_row(p_ref, which, stream):
    row = 6 + 3 * which + stream
    return p_ref[row : row + 1, :]


def short_conv(st_ref, p_ref, stream, masks):
    zero, one, two = shifted(st_ref[:, stream * D : (stream + 1) * D])
    return (
        mix_row(p_ref, 4, stream)
        + mix_row(p_ref, 1, stream) * zero
        + mix_row(p_ref, 2, stream) * (one * masks[0])
        + mix_row(p_ref, 3, stream) * (two * masks[1])
    )


def fetch(own_first, own, rcv, dst, sem):
    @pl.when(own_first)
    def _():
        pltpu.make_async_copy(own, dst, sem).start()

    @pl.when(jnp.logical_not(own_first))
    def _():
        pltpu.make_async_copy(rcv, dst, sem).start()


def rows_at(start, size):
    return pl.ds(pl.multiple_of(start, 16), size)


def fetch_in(own_first, own, rcv, weight, sems):
    def part(ref, stream):
        return ref.at[0, :, pl.ds(stream * D, D)]

    def dest(stream):
        return weight.at[:, pl.ds(stream * D, D)]

    for stream in range(3):
        fetch(own_first, part(own, stream), part(rcv, stream), dest(stream), sems.at[stream])

    def wait(stream):
        pltpu.make_async_copy(part(own, stream), dest(stream), sems.at[stream]).wait()

    return wait


SMEM = pl.BlockSpec(memory_space=pltpu.SMEM)
VMEM = pl.BlockSpec(memory_space=pltpu.VMEM)
ANY = pl.BlockSpec(memory_space=pl.ANY)


def run(body, outs, ins, specs, scratch, name, flops=0, bytes_accessed=0, deps=(), through=()):
    taken, skipped, results = len(ins), len(deps) + len(through), len(outs)

    def wrapped(*refs):
        last = taken + skipped + results
        body(*refs[:taken], *refs[taken + skipped : last], *refs[last + len(through) :])

    return pl.pallas_call(
        wrapped,
        out_shape=[jax.ShapeDtypeStruct(shape, dtype) for shape, dtype in outs]
        + [jax.ShapeDtypeStruct(value.shape, value.dtype) for value in through],
        in_specs=specs + [ANY] * skipped,
        out_specs=[SMEM if out == TICK else VMEM for out in outs] + [ANY] * len(through),
        input_output_aliases={
            taken + len(deps) + index: results + index for index in range(len(through))
        },
        scratch_shapes=scratch,
        compiler_params=pltpu.CompilerParams(vmem_limit_bytes=VMEM_LIMIT),
        cost_estimate=pl.CostEstimate(
            flops=1, bytes_accessed=1, transcendentals=0
        ),
        name=name,
    )(*ins, *deps, *through)


def in_part(block, shard_len, count):
    chan = D // count

    def body(sc, x_ref, halo_ref, p_ref, own, rcv, normed_ref, st_ref, tick_ref, *rest):
        outs = rest[:count]
        tick_ref[0, 0] = 0.0
        weight, sig_t, sems = rest[count:]
        wait = fetch_in(sc[0] == block, own, rcv, weight, sems)
        ext = jnp.concatenate([halo_ref[...].astype(f32), x_ref[...].astype(f32)], axis=0)
        unit, _ = norm_stats(ext)
        normed = (unit * p_ref[0:1, :] + p_ref[2:3, :]).astype(bf16)
        normed_ref[...] = normed[HALO:]
        for stream in range(3):
            wait(stream)
            cols = slice(stream * D, (stream + 1) * D)
            st_ref[:, cols] = (dot(normed, weight[:, cols]) + mix_row(p_ref, 0, stream)).astype(bf16)
        masks = place_masks(sc, shard_len, shard_len)
        signal = short_conv(st_ref, p_ref, 2, masks) * short_conv(st_ref, p_ref, 1, masks)
        sig_t[...] = signal.T.astype(bf16)
        for step in range(count):
            outs[step][...] = sig_t[rows_at((sc[1] ^ step) * chan, chan), :]

    def call(sc, x, halo, params, own, rcv):
        return run(
            body,
            [((shard_len, D), bf16), ((shard_len + HALO, 3 * D), bf16), TICK]
            + [((chan, shard_len), bf16)] * count,
            (sc, x, halo, params, own, rcv),
            [SMEM, VMEM, VMEM, VMEM, ANY, ANY],
            [
                pltpu.VMEM((D, 3 * D), bf16),
                pltpu.VMEM((D, shard_len), bf16),
                pltpu.SemaphoreType.DMA((3,)),
            ],
            f"in_part_{block}",
            2 * shard_len * D * 3 * D,
            D * 3 * D * 2,
        )

    return call


def piece_scalars(sc):
    starts = [sc[2 + doc] for doc in range(NDOCS)] + [SEQ]
    lows, offsets = [], [0]
    for doc in range(NDOCS):
        low, high = starts[doc] // BLK, (starts[doc + 1] - 1) // BLK
        lows.append(low)
        offsets.append(offsets[-1] + high - low + 1)
    pieces = []
    for piece in range(PIECES):
        begin, stop, low, first, last = starts[0], starts[1], lows[0], offsets[0], offsets[1]
        for doc in range(1, NDOCS):
            here = piece >= offsets[doc]
            begin = jnp.where(here, starts[doc], begin)
            stop = jnp.where(here, starts[doc + 1], stop)
            low = jnp.where(here, lows[doc], low)
            first = jnp.where(here, offsets[doc], first)
            last = jnp.where(here, offsets[doc + 1], last)
        live = piece < offsets[NDOCS]
        blk = jnp.minimum(low + piece - first, NB - 1)
        begin = jnp.where(live, begin, 0)
        stop = jnp.where(live, stop, 0)
        first = jnp.where(live, first, piece + 1)
        last = jnp.where(live, last, piece)
        pieces.append((blk, begin, stop, first, last))
    return pieces


def piece_mask(piece):
    pos = piece[0] * BLK + lax.broadcasted_iota(jnp.int32, (1, BLK), 1)
    return (pos >= piece[1]) & (pos < piece[2])


def gather_blocks(sc, ins, blocks, per_shard):
    if isinstance(ins, (list, tuple)):
        for step, ref in enumerate(ins):
            source = sc[1] ^ step
            for part in range(per_shard):
                blocks[source * per_shard + part] = ref[:, part * BLK : (part + 1) * BLK]
        return
    for source in range(NB // per_shard):
        for part in range(per_shard):
            blocks[source * per_shard + part] = ins[source, :, part * BLK : (part + 1) * BLK]


def to_freq(pieces, blocks, masked, freq, tables, chan):
    for index, piece in enumerate(pieces):
        keep = jnp.where(piece_mask(piece), 1.0, 0.0)
        masked[index * chan : (index + 1) * chan, :] = (
            blocks[piece[0]].astype(f32) * keep
        ).astype(bf16)
    values = masked[...]
    freq[...] = dot(values, tables[0][...]) + dot(values, tables[1][...])


def from_freq(pieces, freq, out_blocks, tables, chan):
    values = freq[...]
    high = values.astype(bf16)
    low = (values - high.astype(f32)).astype(bf16)
    back = dot(high, tables[2][...]) + dot(low, tables[2][...]) + dot(high, tables[3][...])
    for index, piece in enumerate(pieces):
        mine = back[index * chan : (index + 1) * chan, :]
        before = out_blocks[piece[0]]
        out_blocks[piece[0]] = jnp.where(piece_mask(piece), mine, before)


def scatter_blocks(sc, outs, out_blocks, per_shard):
    if isinstance(outs, (list, tuple)):
        for step, ref in enumerate(outs):
            target = sc[1] ^ step
            for part in range(per_shard):
                ref[:, part * BLK : (part + 1) * BLK] = out_blocks[
                    target * per_shard + part
                ].astype(bf16)
        return
    for target in range(NB // per_shard):
        for part in range(per_shard):
            outs[target, :, part * BLK : (part + 1) * BLK] = out_blocks[
                target * per_shard + part
            ].astype(bf16)


def conv_part(block, shard_len, count):
    chan = D // count
    per_shard = shard_len // BLK
    tiles = chan // TILE

    def body(sc, filt, *rest):
        ins, tables, rest = rest[:count], rest[count : count + 4], rest[count + 4 :]
        outs, blocks, tick_ref = rest[:count], rest[count], rest[count + 1]
        masked, freq, total, out_blocks = rest[count + 2 :]
        tick_ref[0, 0] = 0.0
        gather_blocks(sc, ins, blocks, per_shard)
        pieces = piece_scalars(sc)
        to_freq(pieces, blocks, masked, freq, tables, chan)
        for index, piece in enumerate(pieces):
            for tile in range(tiles):

                def step(other, carry, index=index, piece=piece, tile=tile):
                    sum_re, sum_im = carry
                    rows = rows_at(other * chan + tile * TILE, TILE)
                    sig_re, sig_im = freq[rows, :BLK], freq[rows, BLK:]
                    lag = index - other
                    here = slice(tile * TILE, (tile + 1) * TILE)
                    fil_re, fil_im = filt[lag, here, :BLK], filt[lag, here, BLK:]
                    return (
                        sum_re + fil_re * sig_re - fil_im * sig_im,
                        sum_im + fil_re * sig_im + fil_im * sig_re,
                    )

                zero = jnp.zeros((TILE, BLK), f32)
                sum_re, sum_im = lax.fori_loop(piece[3], index + 1, step, (zero, zero))
                here = slice(index * chan + tile * TILE, index * chan + (tile + 1) * TILE)
                total[here, :BLK] = sum_re
                total[here, BLK:] = sum_im
        out_blocks[...] = jnp.zeros_like(out_blocks)
        from_freq(pieces, total, out_blocks, tables, chan)
        scatter_blocks(sc, outs, out_blocks, per_shard)

    def call(sc, filt, ins, tables, deps):
        return run(
            body,
            [((chan, shard_len), bf16)] * count + [((NB, chan, BLK), bf16), TICK],
            (sc, filt, *ins, *tables),
            [SMEM] + [VMEM] * (count + 5),
            [
                pltpu.VMEM((PIECES * chan, BLK), bf16),
                pltpu.VMEM((PIECES * chan, FREQ), f32),
                pltpu.VMEM((PIECES * chan, FREQ), f32),
                pltpu.VMEM((NB, chan, BLK), f32),
            ],
            f"conv_part_{block}",
            10 * PIECES * chan * BLK * FREQ,
            NB * chan * FREQ * 4,
            deps,
        )

    return call


def conv_back(block, shard_len, count):
    chan = D // count
    per_shard = shard_len // BLK
    tiles = chan // TILE

    def body(sc, filt, blocks, *rest):
        ins, tables, rest = rest[0], rest[1:5], rest[5:]
        outs, d_filt, tick_ref = rest[:3]
        d_blocks, masked, freq, d_freq, total, out_blocks = rest[3:]
        tick_ref[0, 0] = 0.0
        gather_blocks(sc, ins, d_blocks, per_shard)
        pieces = piece_scalars(sc)
        to_freq(pieces, blocks, masked, freq, tables, chan)
        to_freq(pieces, d_blocks, masked, d_freq, tables, chan)
        d_filt[...] = jnp.zeros_like(d_filt)
        for index, piece in enumerate(pieces):
            for tile in range(tiles):
                rows = slice(index * chan + tile * TILE, index * chan + (tile + 1) * TILE)
                here = slice(tile * TILE, (tile + 1) * TILE)

                def step(other, carry, index=index, here=here, rows=rows, tile=tile):
                    sum_re, sum_im = carry
                    sig_re, sig_im = freq[rows, :BLK], freq[rows, BLK:]
                    there = rows_at(other * chan + tile * TILE, TILE)
                    der_re, der_im = d_freq[there, :BLK], d_freq[there, BLK:]
                    lag = other - index
                    fil_re, fil_im = filt[lag, here, :BLK], filt[lag, here, BLK:]
                    d_filt[lag, here, :BLK] += sig_re * der_re + sig_im * der_im
                    d_filt[lag, here, BLK:] += sig_re * der_im - sig_im * der_re
                    return (
                        sum_re + fil_re * der_re + fil_im * der_im,
                        sum_im + fil_re * der_im - fil_im * der_re,
                    )

                zero = jnp.zeros((TILE, BLK), f32)
                sum_re, sum_im = lax.fori_loop(index, piece[4], step, (zero, zero))
                total[rows, :BLK] = sum_re
                total[rows, BLK:] = sum_im
        out_blocks[...] = jnp.zeros_like(out_blocks)
        from_freq(pieces, total, out_blocks, tables, chan)
        scatter_blocks(sc, outs, out_blocks, per_shard)

    def call(sc, filt, blocks, ins, tables, deps):
        return run(
            body,
            [((count, chan, shard_len), bf16), ((NB, chan, FREQ), f32), TICK],
            (sc, filt, blocks, ins, *tables),
            [SMEM] + [VMEM] * 7,
            [
                pltpu.VMEM((NB, chan, BLK), bf16),
                pltpu.VMEM((PIECES * chan, BLK), bf16),
                pltpu.VMEM((PIECES * chan, FREQ), f32),
                pltpu.VMEM((PIECES * chan, FREQ), f32),
                pltpu.VMEM((PIECES * chan, FREQ), f32),
                pltpu.VMEM((NB, chan, BLK), f32),
            ],
            f"conv_back_{block}",
            14 * PIECES * chan * BLK * FREQ,
            NB * chan * FREQ * 8,
            deps,
        )

    return call


def token_major(ins):
    return ins[...].reshape(D, ins.shape[2]).astype(f32).T


def weight_scratch():
    return [
        pltpu.VMEM((D, D), bf16),
        pltpu.VMEM((D, FF), bf16),
        pltpu.VMEM((FF, D), bf16),
        pltpu.SemaphoreType.DMA((1 + 2 * (FF // FF_TILE),)),
    ]


def fetch_mlp(own_first, pairs, dsts, sems, out_first):
    tiles = FF // FF_TILE
    (out_own, out_rcv), (up_own, up_rcv), (down_own, down_rcv) = pairs
    w_out, w_up, w_down = dsts

    def start_out():
        fetch(own_first, out_own.at[0], out_rcv.at[0], w_out, sems.at[0])

    def start_up(tile):
        cols = pl.ds(tile * FF_TILE, FF_TILE)
        fetch(
            own_first,
            up_own.at[0, :, cols],
            up_rcv.at[0, :, cols],
            w_up.at[:, cols],
            sems.at[1 + tile],
        )

    def start_down(tile):
        rows = pl.ds(tile * FF_TILE, FF_TILE)
        fetch(
            own_first,
            down_own.at[0, rows],
            down_rcv.at[0, rows],
            w_down.at[rows],
            sems.at[1 + tiles + tile],
        )

    if out_first:
        start_out()
    for tile in range(tiles):
        if out_first:
            start_up(tile)
            start_down(tile)
        else:
            start_down(tile)
            start_up(tile)
    if not out_first:
        start_out()

    def wait_out():
        pltpu.make_async_copy(out_own.at[0], w_out, sems.at[0]).wait()

    def wait_up(tile):
        cols = pl.ds(pl.multiple_of(tile * FF_TILE, FF_TILE), FF_TILE)
        pltpu.make_async_copy(up_own.at[0, :, cols], w_up.at[:, cols], sems.at[1 + tile]).wait()
        return cols

    def wait_down(tile):
        rows = pl.ds(pl.multiple_of(tile * FF_TILE, FF_TILE), FF_TILE)
        pltpu.make_async_copy(
            down_own.at[0, rows], w_down.at[rows], sems.at[1 + tiles + tile]
        ).wait()
        return rows

    return wait_out, wait_up, wait_down


GELU_SCALE = 0.7978845608028654
GELU_CUBE = 0.044715


def out_part(block, shard_len, count):
    chan = D // count

    def body(sc, x_ref, st_ref, normed_one, p_ref, bias_ref, *rest):
        ins, rest = rest[:count], rest[count:]
        pairs = (rest[0:2], rest[2:4], rest[4:6])
        result_ref, residual_ref, mine_ref, other_ref, slope_ref, cmix_ref = rest[6:12]
        turned, w_out, w_up, w_down, sems, normed_ref, gated_ref, hidden_ref = rest[12:]

        def keep_halves(ref, start, half):
            for side, target in ((sc[0], mine_ref), (1 - sc[0], other_ref)):
                cols = pl.ds(pl.multiple_of(side * half, half), half)
                target[:, start : start + half] = ref[:, cols]

        wait_out, wait_up, wait_down = fetch_mlp(
            sc[0] == block, pairs, (w_out, w_up, w_down), sems, True
        )
        masks = place_masks(sc, shard_len, shard_len)
        for step, ref in enumerate(ins):
            turned[rows_at((sc[1] ^ step) * chan, chan), :] = ref[...]
        conv = turned[...].astype(f32).T
        signal = short_conv(st_ref, p_ref, 2, masks) * short_conv(st_ref, p_ref, 1, masks)
        cmix = conv + p_ref[21:22, :] * signal
        cmix_ref[...] = cmix
        gated = (cmix * short_conv(st_ref, p_ref, 0, masks)).astype(bf16)
        gated_ref[...] = gated
        wait_out()
        residual = x_ref[...].astype(f32) + dot(gated, w_out[...]) + p_ref[3:4, :]
        residual_ref[...] = residual
        unit, _ = norm_stats(residual)
        normed_ref[...] = (unit * p_ref[1:2, :] + p_ref[4:5, :]).astype(bf16)
        result_ref[...] = residual + p_ref[5:6, :]

        @pl.loop(0, FF // FF_TILE)
        def _(tile):
            cols = wait_up(tile)
            pre = dot(normed_ref[...], w_up[:, cols]) + bias_ref[:, cols]
            square = pre * pre
            bent = jnp.tanh(GELU_SCALE * pre * (1.0 + GELU_CUBE * square))
            half = 0.5 * (1.0 + bent)
            slope = half + (0.5 * GELU_SCALE) * pre * (1.0 - bent * bent) * (
                1.0 + 3.0 * GELU_CUBE * square
            )
            hidden = (pre * half).astype(bf16)
            hidden_ref[:, cols] = hidden
            slope_ref[:, cols] = slope.astype(bf16)
            rows = wait_down(tile)
            result_ref[...] += dot(hidden, w_down[rows, :])

        keep_halves(hidden_ref, ACT_HIDDEN, FF // 2)
        keep_halves(normed_ref, ACT_TWO, HALF)
        keep_halves(gated_ref, ACT_GATED, HALF)
        keep_halves(normed_one, ACT_NORMED, HALF)

    def call(sc, x, st, normed, params, up_bias, ins, weights):
        return run(
            body,
            [
                ((shard_len, D), f32),
                ((shard_len, D), f32),
                ((shard_len, ACT_COLS), bf16),
                ((shard_len, ACT_COLS), bf16),
                ((shard_len, FF), bf16),
                ((shard_len, D), f32),
            ],
            (sc, x, st, normed, params, up_bias, *ins, *weights),
            [SMEM] + [VMEM] * (5 + count) + [ANY] * 6,
            [pltpu.VMEM((D, shard_len), bf16)]
            + weight_scratch()
            + [
                pltpu.VMEM((shard_len, D), bf16),
                pltpu.VMEM((shard_len, D), bf16),
                pltpu.VMEM((shard_len, FF), bf16),
            ],
            f"out_part_{block}",
            2 * shard_len * D * (D + 2 * FF),
            D * (D + 2 * FF) * 2,
        )

    return call


def out_back(block, shard_len, count):
    chan = D // count

    def body(sc, grad_ref, residual_ref, slope_ref, st_ref, p_ref, *rest):
        pairs = (rest[0:2], rest[2:4], rest[4:6])
        grads_ref, dres_ref, dg_ref, vec_ref, dub_ref, tick_ref = rest[6:12]
        outs, rest = rest[12], rest[13:]
        tick_ref[0, 0] = 0.0
        turned, w_out, w_up, w_down, sems, total = rest
        wait_out, wait_up, wait_down = fetch_mlp(
            sc[0] == block, pairs, (w_out, w_up, w_down), sems, False
        )
        grad = grad_ref[...].astype(f32)
        gm = grad.astype(bf16)
        grads_ref[:, GRAD_MLP : GRAD_MLP + D] = gm
        total[...] = jnp.zeros_like(total)

        @pl.loop(0, FF // FF_TILE)
        def _(tile):
            rows = wait_down(tile)
            d_hidden = dot(grads_ref[:, GRAD_MLP : GRAD_MLP + D], w_down[rows, :], NT)
            d_pre = (d_hidden * slope_ref[:, rows].astype(f32)).astype(bf16)
            grads_ref[:, rows] = d_pre
            dub_ref[:, rows] = jnp.broadcast_to(col_sum(d_pre.astype(f32)), (8, FF_TILE))
            cols = wait_up(tile)
            total[...] += dot(d_pre, w_up[:, cols], NT)

        d_normed = total[...]
        unit, scale = norm_stats(residual_ref[...])
        d_res = grad + norm_back(d_normed, p_ref[1:2, :], unit, scale)
        dres_ref[...] = d_res
        gb = d_res.astype(bf16)
        grads_ref[:, GRAD_BRANCH : GRAD_BRANCH + D] = gb
        wait_out()
        dg = dot(gb, w_out[...], NT).astype(bf16)
        dg_ref[...] = dg
        masks = place_masks(sc, shard_len, shard_len)
        d_conv = dg.astype(f32) * short_conv(st_ref, p_ref, 0, masks)
        turned[...] = d_conv.T.astype(bf16)
        for step in range(count):
            outs[step] = turned[step * chan : (step + 1) * chan, :]
        vec_ref[...] = jnp.concatenate(
            [
                col_sum(d_normed * unit),
                col_sum(d_normed),
                col_sum(gb.astype(f32)),
                col_sum(gm.astype(f32)),
                jnp.zeros((4, D), f32),
            ],
            axis=0,
        )

    def call(sc, grad, residual, slope, st, params, weights, deps):
        return run(
            body,
            [
                ((shard_len, GRAD_COLS), bf16),
                ((shard_len, D), f32),
                ((shard_len, D), bf16),
                ((8, D), f32),
                ((8, FF), f32),
                TICK,
            ]
            + [((count, chan, shard_len), bf16)],
            (sc, grad, residual, slope, st, params, *weights),
            [SMEM] + [VMEM] * 5 + [ANY] * 6,
            [pltpu.VMEM((D, shard_len), bf16)]
            + weight_scratch()
            + [pltpu.VMEM((shard_len, D), f32)],
            f"out_back_{block}",
            2 * shard_len * D * (D + 2 * FF),
            D * (D + 2 * FF) * 2,
            deps,
        )

    return call


def short_back(block, shard_len, count):
    chan = D // count

    def body(sc, st_ref, dg_ref, cmix_ref, p_ref, *rest):
        ins, ds_ref, head_ref, vec_ref, tick_ref = rest
        tick_ref[0, 0] = 0.0
        masks = place_masks(sc, shard_len, shard_len)
        d_signal = token_major(ins)
        dg = dg_ref[...].astype(f32)
        d_conv = dg * short_conv(st_ref, p_ref, 0, masks)
        inner = short_conv(st_ref, p_ref, 1, masks)
        value = short_conv(st_ref, p_ref, 2, masks)
        d_signal = d_signal + p_ref[21:22, :] * d_conv
        rows = [None] * 16
        rows[12] = col_sum(d_conv * value * inner)
        for stream, d_short in enumerate((dg * cmix_ref[...], d_signal * value, d_signal * inner)):
            cols = slice(stream * D, (stream + 1) * D)
            ds_ref[:, cols] = d_short
            head_ref[:, cols] = d_short[:HALO]
            zero, one, two = shifted(st_ref[:, cols])
            rows[stream] = col_sum(d_short * zero)
            rows[3 + stream] = col_sum(d_short * (one * masks[0]))
            rows[6 + stream] = col_sum(d_short * (two * masks[1]))
            rows[9 + stream] = col_sum(d_short)
        for index in range(13, 16):
            rows[index] = jnp.zeros((1, D), f32)
        vec_ref[...] = jnp.concatenate(rows, axis=0)

    def call(sc, st, dg, cmix, params, ins, deps, through):
        return run(
            body,
            [((shard_len, 3 * D), f32), ((HALO, 3 * D), f32), ((16, D), f32), TICK],
            (sc, st, dg, cmix, params, ins),
            [SMEM] + [VMEM] * 5,
            [],
            f"short_back_{block}",
            40 * shard_len * D,
            shard_len * D * 20,
            deps,
            through,
        )

    return call


def in_back(block, shard_len):
    def body(sc, ds_ref, halo_ref, x_ref, dres_ref, p_ref, own, rcv, dst_ref, dx_ref, vec_ref, weight, sems):
        wait = fetch_in(sc[0] == block, own, rcv, weight, sems)
        long = shard_len + HALO
        one, two = place_masks(sc, long, shard_len)
        d_normed = jnp.zeros((shard_len, D), f32)
        rows = []
        for stream in range(3):
            cols = slice(stream * D, (stream + 1) * D)
            ext = jnp.concatenate([ds_ref[:, cols], halo_ref[:, cols]], axis=0)
            d_stream = (
                mix_row(p_ref, 1, stream) * ext[:shard_len]
                + mix_row(p_ref, 2, stream) * pltpu.roll(ext * one, long - 1, 0)[:shard_len]
                + mix_row(p_ref, 3, stream) * pltpu.roll(ext * two, long - 2, 0)[:shard_len]
            ).astype(bf16)
            dst_ref[:, cols] = d_stream
            rows.append(col_sum(d_stream.astype(f32)))
            wait(stream)
            d_normed = d_normed + dot(d_stream, weight[:, cols], NT)
        unit, scale = norm_stats(x_ref[...].astype(f32))
        dx_ref[...] = dres_ref[...] + norm_back(d_normed, p_ref[0:1, :], unit, scale)
        vec_ref[...] = jnp.concatenate(
            [col_sum(d_normed * unit), col_sum(d_normed)] + rows + [jnp.zeros((3, D), f32)], axis=0
        )

    def call(sc, d_short, halo, x, d_res, params, own, rcv, deps):
        return run(
            body,
            [((shard_len, 3 * D), bf16), ((shard_len, D), f32), ((8, D), f32)],
            (sc, d_short, halo, x, d_res, params, own, rcv),
            [SMEM] + [VMEM] * 5 + [ANY] * 2,
            [pltpu.VMEM((D, 3 * D), bf16), pltpu.SemaphoreType.DMA((3,))],
            f"in_back_{block}",
            2 * shard_len * D * 3 * D,
            D * 3 * D * 2,
            deps,
        )

    return call


def weight_grad(name, parts, first_bits, shard_len, shards, count):
    groups = len(first_bits)
    sizes = [0] * groups
    for _, rows, _, cols, splits in parts:
        for group, _, size in splits:
            sizes[group] += size * (cols // HALF)
    shapes, firsts = [], []
    for size, bit in zip(sizes, first_bits):
        firsts.append(len(shapes))
        shapes += [(shards, size, HALF)] if bit is None else [(shards // 2, size, HALF)] * 2

    def body(sc, g_own, g_rcv, a_own, a_rcv, *outs):
        outs[-1][0, 0] = 0.0
        me = sc[2 + NDOCS] * count
        bases = [0] * groups
        for g_start, rows, a_start, cols, splits in parts:
            block = rows // shards
            chunk = 8 * block if block % 32 else 4 * block
            acts = slice(a_start, a_start + cols)
            starts = list(bases)

            @pl.loop(0, rows // chunk)
            def _(step, starts=starts, g_start=g_start, chunk=chunk, block=block, acts=acts, cols=cols, splits=splits):
                here = pl.ds(pl.multiple_of(g_start + step * chunk, 128), chunk)
                full = dot(g_own[:, here], a_own[:, acts], TN) + dot(g_rcv[:, here], a_rcv[:, acts], TN)
                for index in range(chunk // block):
                    device = step * (chunk // block) + index
                    for group, begin, size in splits:
                        bit = first_bits[group]
                        if bit is None:
                            slot = device
                        else:
                            away = device ^ me
                            low = away & ((1 << bit) - 1)
                            slot = ((away >> (bit + 1)) << bit) | low
                            sent = (away >> bit) & 1

                        def store(ref, group=group, begin=begin, size=size, slot=slot, index=index):
                            for part in range(cols // HALF):
                                top = starts[group] + part * size
                                ref[slot, top : top + size, :] = full[
                                    index * block + begin : index * block + begin + size,
                                    part * HALF : (part + 1) * HALF,
                                ].astype(bf16)

                        first = firsts[group]
                        if bit is None:
                            store(outs[first])
                        else:
                            pl.when(sent == 1)(functools.partial(store, outs[first]))
                            pl.when(sent == 0)(functools.partial(store, outs[first + 1]))

            for group, _, size in splits:
                bases[group] += size * (cols // HALF)

    def call(sc, *ins, deps=()):
        flops = sum(4 * shard_len * rows * cols for _, rows, _, cols, _ in parts)
        outs = run(
            body,
            [(shape, bf16) for shape in shapes] + [TICK],
            (sc, *ins),
            [SMEM] + [VMEM] * 4,
            [],
            name,
            flops,
            flops // 256,
            deps,
        )
        return [
            outs[first] if bit is None else outs[first : first + 2]
            for first, bit in zip(firsts, first_bits)
        ], outs[-1]

    return call


def weight_grad_plain(parts, first_bits, shards, me):
    groups = len(first_bits)

    def call(_, g_own, g_rcv, a_own, a_rcv, deps=()):
        gathered = [[] for _ in range(groups)]
        for g_start, rows, a_start, cols, splits in parts:
            block = rows // shards
            full = sum(
                jnp.einsum(
                    "tn,tk->nk",
                    g[:, g_start : g_start + rows],
                    a[:, a_start : a_start + cols],
                    preferred_element_type=f32,
                )
                for g, a in ((g_own, a_own), (g_rcv, a_rcv))
            ).astype(bf16)
            full = full.reshape(shards, block, cols // HALF, HALF).transpose(0, 2, 1, 3)
            for group, begin, size in splits:
                piece = full[:, :, begin : begin + size]
                gathered[group].append(piece.reshape(shards, -1, HALF))
        outs = []
        for group in range(groups):
            whole = jnp.concatenate(gathered[group], axis=1)
            bit = first_bits[group]
            if bit is None:
                outs.append(whole)
                continue
            whole = whole[jnp.arange(shards, dtype=jnp.int32) ^ me]
            whole = whole.reshape((shards >> (bit + 1), 2, 1 << bit) + whole.shape[1:])
            outs.append(
                [whole[:, side].reshape((shards // 2,) + whole.shape[3:]) for side in (1, 0)]
            )
        return outs, jnp.zeros((1, 1), f32)

    return call


def halving(name, groups, count):
    def call(deps, through=None):
        ins, outs, in_specs, out_specs, lists = [], [], [], [], []
        alias = {}
        steps = None
        for group in groups:
            height, sizes = sum(kept.shape[1] for kept, _, _ in group), []
            for kept, got, spot in group:
                blocks, rows, cols = kept.shape
                inner = count << spot
                outer = blocks // (2 * inner)
                steps = outer * inner
                ins += [v.reshape(outer, 2, inner, rows, cols) for v in (kept, got)]
                in_specs += [
                    pl.BlockSpec(
                        (1, 2, 1, rows, cols), lambda i, inner=inner: (i // inner, 0, i % inner, 0, 0)
                    )
                ] * 2
                sizes.append(rows)
            outs += [jax.ShapeDtypeStruct((outer, inner, height, cols), bf16)] * 2
            out_specs += [
                pl.BlockSpec(
                    (1, 1, height, cols), lambda i, inner=inner: (i // inner, i % inner, 0, 0)
                )
            ] * 2
            lists.append(sizes)
        taken = len(ins)
        if through is not None:
            alias = {taken + len(deps): len(outs) + 1}
            deps = [*deps, through]

        def body(*refs):
            out_refs = refs[taken + len(deps) :]
            out_refs[2 * len(groups)][0, 0] = 0.0
            index = 0
            for group, sizes in enumerate(lists):
                begin = 0
                for size in sizes:
                    kept, got = refs[index : index + 2]
                    index += 2
                    for side, ref in ((1, out_refs[2 * group]), (0, out_refs[2 * group + 1])):
                        ref[0, 0, begin : begin + size, :] = (
                            kept[0, side, 0].astype(f32) + got[0, side, 0].astype(f32)
                        ).astype(bf16)
                    begin += size

        values = pl.pallas_call(
            body,
            grid=(steps,),
            out_shape=outs
            + [jax.ShapeDtypeStruct(*TICK)]
            + [jax.ShapeDtypeStruct(through.shape, through.dtype) for _ in alias],
            in_specs=in_specs + [ANY] * len(deps),
            out_specs=out_specs + [SMEM] + [ANY] * len(alias),
            input_output_aliases=alias,
            compiler_params=pltpu.CompilerParams(vmem_limit_bytes=VMEM_LIMIT),
            cost_estimate=pl.CostEstimate(flops=1, bytes_accessed=1, transcendentals=0),
            name=name,
        )(*ins, *deps)
        flat = [v.reshape((-1,) + v.shape[2:]) for v in values[: 2 * len(groups)]]
        pairs_out = [flat[2 * group : 2 * group + 2] for group in range(len(groups))]
        return pairs_out, values[2 * len(groups)], values[-1] if alias else None

    return call


def relay(name, deps):
    def body(tick_ref):
        tick_ref[0, 0] = 0.0

    return run(body, [TICK], [], [], [], name, deps=deps)[0]


def merging(name, sizes, count):
    def call(terms, deps):
        taken, rows = 2 * len(terms), sum(sizes)

        def body(*refs):
            out_ref, tick_ref = refs[taken + len(deps) :]
            tick_ref[0, 0] = 0.0
            begin = 0
            for group, size in enumerate(sizes):
                kept, got = refs[2 * group : 2 * group + 2]
                out_ref[0, begin : begin + size, :] = (
                    kept[0].astype(f32) + got[0].astype(f32)
                ).astype(bf16)
                begin += size

        def block(size):
            return pl.BlockSpec((1, size, HALF), lambda i: (i, 0, 0))

        return pl.pallas_call(
            body,
            grid=(count,),
            out_shape=[
                jax.ShapeDtypeStruct((count, rows, HALF), bf16),
                jax.ShapeDtypeStruct(*TICK),
            ],
            in_specs=[block(size) for size in sizes for _ in range(2)] + [ANY] * len(deps),
            out_specs=[block(rows), SMEM],
            compiler_params=pltpu.CompilerParams(vmem_limit_bytes=VMEM_LIMIT),
            cost_estimate=pl.CostEstimate(flops=1, bytes_accessed=1, transcendentals=0),
            name=name,
        )(*[value for kept, got, _ in terms for value in (kept, got)], *deps)

    return call


def pairs(count, step):
    return [(index, index ^ step) for index in range(count)]


def swap(value):
    return lax.ppermute(value, "section", pairs(2, 1))


def exchange_apart(chunks):
    count = len(chunks)
    return [chunks[0]] + [
        lax.ppermute(chunks[step], "seq", pairs(count, step)) for step in range(1, count)
    ]


def exchange(chunks):
    return lax.all_to_all(chunks, "seq", split_axis=0, concat_axis=0, tiled=True)


class Reduction:
    def __init__(self, groups, dp_count, count):
        self.sizes = (dp_count, count)
        self.terms = []
        for (sent, kept), bits in groups:
            self.terms.append((kept, self.over_dp(sent, bits[0]), list(bits[1:])))

    def arrived(self):
        return [got for _, got, _ in self.terms]

    def over_dp(self, value, bit):
        return lax.ppermute(value, "dp", pairs(self.sizes[0], (1 << bit) // self.sizes[1]))

    def plane(self, name, tick, deps=(), through=None):
        handed = through
        for turn in range(len(self.terms[0][2])):
            orders, groups = [], []
            for kept, got, left in self.terms:
                if left not in orders:
                    orders.append(left)
                    groups.append([])
                spot = sum(1 for other in left[1:] if other < left[0])
                groups[orders.index(left)].append((kept, got, spot))
            values, tick, passed = halving(f"{name}_{turn}", groups, self.sizes[1])(
                [tick, *deps], None if turn else through
            )
            handed = handed if passed is None else passed
            self.terms = [
                (keep, self.over_dp(send, left[0]), left[1:])
                for (send, keep), left in zip(values, orders)
            ]
        return tick, handed

    def rest(self, name, deps):
        sizes = [kept.shape[1] for kept, _, _ in self.terms]
        if any(size % 16 for size in sizes):
            parts = [
                (kept.astype(f32) + got.astype(f32)).astype(bf16) for kept, got, _ in self.terms
            ]
            return jnp.concatenate(parts, axis=1), jnp.zeros((1, 1), f32)
        return merging(name, sizes, self.sizes[1])(self.terms, deps)


def joined(parts):
    whole = Reduction([], *parts[0].sizes)
    for part in parts:
        whole.terms += part.terms
    return whole


def line_sum(values):
    return jnp.sum(exchange(values).astype(f32), axis=0)


def scatter(value, axis):
    blocks, rows, cols = value.shape
    value = value.reshape(blocks * rows, cols)
    return lax.psum_scatter(value, axis, scatter_dimension=0, tiled=True).reshape(-1, rows, cols)


def mat(spec, left, right):
    return jnp.einsum(spec, left, right, precision=highest, preferred_element_type=f32)


def filter_state(net, last, decay, pos, window):
    first_w, inner_b, second_w = net[:EMB], net[EMB : EMB + 2], net[EMB + 2 :]
    pre_a = mat("ef,en->fn", first_w, pos) + inner_b[0][:, None]
    hid_a = jnp.sin(pre_a)
    pre_b = mat("gf,gn->fn", second_w, hid_a) + inner_b[1][:, None]
    hid_b = jnp.sin(pre_b)
    taps = mat("fc,fn->cn", last, hid_b) * decay
    blocks = taps.reshape(taps.shape[0], NB, BLK)
    filt = mat("cmn,nk->mck", blocks, window[BLK:])
    behind = mat("cmn,nk->mck", blocks[:, :-1], window[:BLK])
    filt = filt + jnp.pad(behind, ((1, 0), (0, 0), (0, 0)))
    energy = taps * taps
    share = jnp.sum(jnp.sum(energy[:, LONG_LAG:], axis=1) / (jnp.sum(energy, axis=1) + 1e-06))
    return filt, share, (pre_a, hid_a, pre_b, hid_b, second_w)


def split(value):
    high = value.astype(bf16)
    return high, (value - high.astype(f32)).astype(bf16)


def dot_split(left, right, dims):
    total = dot(left[0], right[0], dims)
    if left[1] is not None:
        total = total + dot(left[1], right[0], dims)
    if right[1] is not None:
        total = total + dot(left[0], right[1], dims)
    return total


NN = ((1,), (0,))
POS_ROWS = 40


def net_back(block, chan):
    def body(d_filt, pre_a, hid_a, pre_b, hid_b, second, last, decay, pos, win_hi, win_lo, first_ref, second_ref, last_ref, tick_ref, taps):
        tick_ref[0, 0] = 0.0
        behind = (win_hi[:BLK, :], win_lo[:BLK, :])
        ahead = (win_hi[BLK:, :], win_lo[BLK:, :])
        for m in range(NB):
            d_block = dot_split(split(d_filt[m]), ahead, NT)
            if m + 1 < NB:
                d_block = d_block + dot_split(split(d_filt[m + 1]), behind, NT)
            cols = slice(m * BLK, (m + 1) * BLK)
            taps[:, cols] = d_block * (decay[:, cols] * (1.0 / BLK))
        d_out = split(taps[...])
        ones = jnp.ones((8, SEQ), f32)
        last_ref[...] = dot_split(split(hid_b[...]), d_out, NT)
        d_b = split(dot_split((last[...].astype(bf16), None), d_out, NN) * jnp.cos(pre_b[...]))
        second_ref[...] = dot_split(
            split(jnp.concatenate([hid_a[...], ones], axis=0)), d_b, NT
        )
        d_a = split(dot_split((second[...].astype(bf16), None), d_b, NN) * jnp.cos(pre_a[...]))
        first_ref[...] = dot_split(split(pos[...]), d_a, NT)

    def call(d_filt, state, last, decay, pos, window, deps):
        return run(
            body,
            [((POS_ROWS, FILT), f32), ((FILT + 8, FILT), f32), ((FILT, chan), f32), TICK],
            (d_filt, *state, last, decay, pos, *window),
            [VMEM] * 11,
            [pltpu.VMEM((chan, SEQ), f32)],
            f"net_back_{block}",
            0,
            0,
            deps,
        )

    return call


def local(
    layer_input,
    out_cot,
    doc_lengths,
    norm_gains,
    biases,
    in_weight,
    mix_vecs,
    filt_first,
    filt_inner_bias,
    filt_second,
    filt_last,
    filt_skip,
    out_weight,
    up_weight,
    up_bias,
    down_weight,
):
    count = lax.axis_size("seq")
    dp_count = lax.axis_size("dp")
    section = lax.axis_index("section")
    place = lax.axis_index("seq")
    first = section == 0
    shard_len = layer_input.shape[2]
    chan = D // count
    fwd_hi, fwd_lo, inv_hi, inv_lo, window = block_tables()
    tables = tuple(jnp.asarray(t) for t in (fwd_hi, fwd_lo, inv_hi, inv_lo))
    window = jnp.asarray(window)
    pos = jnp.asarray(position_table())
    pos_ext = jnp.asarray(
        np.concatenate(
            [position_table(), np.ones((1, SEQ)), np.zeros((POS_ROWS - EMB - 1, SEQ))]
        ).astype(np.float32)
    )
    window_split = tuple(jnp.asarray(part) for part in split_table(block_tables()[4].astype(np.float64)))

    def own_micro(value):
        return lax.dynamic_index_in_dim(value, section, 0, keepdims=False)[0]

    x_zero = own_micro(layer_input)
    cot = own_micro(out_cot)
    lengths = own_micro(doc_lengths)
    starts = jnp.cumsum(lengths) - lengths
    sc = jnp.concatenate(
        [jnp.stack([section, place]), starts, lax.axis_index("dp")[None]]
    ).astype(jnp.int32)

    def behind(rows):
        return lax.ppermute(rows, "seq", [(index, index + 1) for index in range(count - 1)])

    def ahead(rows):
        return lax.ppermute(rows, "seq", [(index + 1, index) for index in range(count - 1)])

    halo = behind(x_zero[-HALO:])
    small = jnp.concatenate(
        [
            norm_gains[0],
            biases[0],
            mix_vecs[0].reshape(15, D),
            filt_skip[0],
            up_bias[0].reshape(4, D),
            filt_last[0],
        ],
        axis=0,
    )
    net = jnp.concatenate([filt_first[0], filt_inner_bias[0], filt_second[0]], axis=0)
    small_rcv, net_rcv = swap(small), swap(net)
    rcv_in, rcv_out, rcv_up, rcv_down = (
        swap(in_weight),
        swap(out_weight),
        swap(up_weight),
        swap(down_weight),
    )
    mlp_pairs = (out_weight, rcv_out, up_weight, rcv_up, down_weight, rcv_down)
    params, nets = [], []
    for block in range(2):
        mine = section == block
        params.append(jnp.where(mine, small, small_rcv).astype(f32))
        nets.append(jnp.where(mine, net, net_rcv).astype(f32))
    tokens = [p[:24] for p in params]
    up_biases = [p[22:26].reshape(1, FF) for p in params]
    lasts = [lax.dynamic_slice_in_dim(p[26:90], place * chan, chan, 1) for p in params]
    chan_ids = (jnp.arange(chan, dtype=jnp.int32) + place * chan).astype(f32)
    times = jnp.arange(SEQ, dtype=f32) / SEQ
    decay = jnp.exp(-(3.0 + 12.0 * chan_ids / (D - 1))[:, None] * times[None, :])

    x = x_zero
    kept = []
    results = []
    filters = []
    for block in range(2):
        normed, st, tick, *chunks = in_part(block, shard_len, count)(
            sc, x, halo, tokens[block], in_weight, rcv_in
        )
        if block == 0:
            filters.append(filter_state(nets[0] + tick[0, 0], lasts[0], decay, pos, window))
        *chunks, blocks, tick = conv_part(block, shard_len, count)(
            sc, filters[block][0], exchange_apart(chunks), tables, [k[5] for k in kept]
        )
        if block == 0:
            filters.append(filter_state(nets[1] + tick[0, 0], lasts[1], decay, pos, window))
        result, residual, acts, acts_other, slope, cmix = out_part(block, shard_len, count)(
            sc, x, st, normed, tokens[block], up_biases[block], exchange_apart(chunks), mlp_pairs
        )
        kept.append((x, st, blocks, residual, acts, swap(acts_other), slope, cmix))
        results.append(result)
        x = result
        if block == 0:
            halo = behind(result[-HALO:])

    def choose(values):
        return jnp.where(first, values[0], values[1]), jnp.where(first, values[1], values[0])

    def swapped(values):
        mine, other = choose(values)
        got = swap(other)

        def stacked(tick=None):
            pair = jnp.stack([jnp.where(first, mine, got), jnp.where(first, got, mine)])
            return pair if tick is None else pair + tick[0, 0]

        return stacked, [got]

    outputs, got_results = swapped(results)
    shards = dp_count * count
    shard = lax.axis_index("dp") * count + place
    low_bit = count.bit_length() - 1
    up_bits = list(range(low_bit, low_bit + dp_count.bit_length() - 1))
    down_bits = up_bits[::-1]
    rows, wide_rows, ff_rows = D // shards, 3 * D // shards, FF // shards
    split = SPLIT if wide_rows > SPLIT else wide_rows // 2
    top, ff_top = rows - rows // 3, ff_rows - ff_rows // 3
    parts_zero = [
        (GRAD_MLP, D, ACT_HIDDEN, FF // 2, [(0, 0, top), (1, top, rows - top)]),
        (GRAD_BRANCH, D, ACT_GATED, HALF, [(0, 0, top), (1, top, rows - top)]),
        (GRAD_PRE, FF, ACT_TWO, HALF, [(2, 0, ff_top), (3, ff_top, ff_rows - ff_top)]),
    ]
    parts_in = [(0, 3 * D, ACT_NORMED, HALF, [(0, 0, split), (1, split, wide_rows - split)])]
    parts_early = [
        (GRAD_MLP, D, ACT_HIDDEN, FF // 2, [(0, 0, rows)]),
        (GRAD_BRANCH, D, ACT_GATED, HALF, [(0, 0, rows)]),
        (GRAD_PRE, FF, ACT_TWO, HALF, [(0, 0, ff_rows)]),
    ]
    whole_tiles = rows % 16 == 0

    def grads_of(name, parts, first_bits):
        if whole_tiles:
            return weight_grad(name, parts, first_bits, shard_len, shards, count)
        return weight_grad_plain(parts, first_bits, shards, shard - place)

    def back(block, grad, wait_out, wait_conv, wait_short, wait_in, through=()):
        x, st, blocks, residual, acts, acts_got, slope, cmix = kept[block]
        grads, d_res, dg, vec_out, d_up_bias, tick, chunks = out_back(block, shard_len, count)(
            sc, grad, residual, slope, st, tokens[block], mlp_pairs, wait_out
        )
        state = dict(grads=(grads, swap(grads), acts, acts_got), acts=(acts, acts_got))
        chunks, d_filt, tick = conv_back(block, shard_len, count)(
            sc, filters[block][0], blocks, exchange(chunks), tables, wait_conv(state, tick)
        )
        state["d_filt"] = d_filt
        d_short, head, vec_short, tick, *state["handed"] = short_back(block, shard_len, count)(
            sc, st, dg, cmix, tokens[block], exchange(chunks), wait_short(state, tick), through
        )
        d_st, d_x, vec_in = in_back(block, shard_len)(
            sc, d_short, ahead(head), x, d_res, tokens[block], in_weight, rcv_in, wait_in(state, tick)
        )
        state["grads_in"] = (d_st, swap(d_st), acts, acts_got)
        state["vecs"] = (vec_in, vec_out, vec_short, d_up_bias)
        return d_x, state

    def grads_split(name, state, key, parts, bits, deps):
        values, end = grads_of(name, parts, [group[0] for group in bits])(
            sc, *state[key], deps=deps
        )
        moving = [Reduction([pair], dp_count, count) for pair in zip(values, bits)]
        return moving, [value[0] for value in values], end

    def early_one(state, tick):
        (value,), _ = grads_of("grad_early_1", parts_early, [None])(
            sc, *state["grads"], deps=[tick]
        )
        state["early"] = value
        return [value]

    def net_grads(block, state, tick):
        first_ext, second_ext, d_last, end = net_back(block, chan)(
            state["d_filt"], filters[block][2], lasts[block], decay, pos_ext, window_split, [tick]
        )
        d_net = jnp.concatenate(
            [first_ext[: EMB + 1], second_ext[FILT : FILT + 1], second_ext[:FILT]], axis=0
        )
        state["net"] = (d_last, d_net)
        return [end]

    d_mid, one = back(
        1,
        cot,
        [],
        lambda state, tick: list(got_results),
        lambda state, tick: early_one(state, tick) + net_grads(1, state, tick),
        lambda state, tick: [],
    )

    def cut(value):
        height, width = value.shape
        return value.reshape(height, shards, width // shards).swapaxes(0, 1).reshape(shards, -1)

    def small_grads(block, state, tick):
        vec_in, vec_out, vec_short, d_up_bias = state["vecs"]
        d_last, d_net = state["net"]
        vec_in, vec_out, vec_short, d_up_bias, d_last, d_net = (
            value + tick[0, 0]
            for value in (vec_in, vec_out, vec_short, d_up_bias, d_last, d_net)
        )
        vecs = jnp.concatenate(
            [
                vec_in[0:1],
                vec_out[0:1],
                vec_in[1:2],
                vec_out[2:3],
                vec_out[1:2],
                vec_out[3:4],
                vec_short[12:13],
            ],
            axis=0,
        )
        mixes = jnp.concatenate([vec_in[2:5], vec_short[0:12]], axis=0).reshape(5, 3 * D)
        last_full = lax.dynamic_update_slice_in_dim(
            jnp.zeros((FILT, D), f32), d_last, place * chan, 1
        )
        return (
            jnp.concatenate(
                [
                    cut(vecs),
                    cut(mixes),
                    cut(d_up_bias[0:1]),
                    cut(last_full),
                    jnp.broadcast_to(d_net.reshape(1, -1), (shards, d_net.size)),
                ],
                axis=1,
            )
        )

    moving, moving_in = [], []

    def wait_conv_zero(state, tick):
        got, sent, _ = grads_split(
            "grad_early_0",
            state,
            "grads",
            parts_zero,
            [up_bits, up_bits, down_bits, down_bits],
            [tick],
        )
        moving.extend(got)
        return sent

    def wait_short_zero(state, tick):
        ends = net_grads(0, state, tick)
        got, sent, _ = grads_split(
            "grad_in_1", one, "grads_in", parts_in, [up_bits, down_bits], ends
        )
        moving_in.extend(got)
        return sent + ends + moving[0].arrived() + moving[2].arrived()

    def wait_in_zero(state, tick):
        one["pack"] = small_grads(1, one, tick)
        arrived = moving[1].arrived() + moving[3].arrived() + joined(moving_in).arrived()
        return arrived + [one["pack"]]

    d_start, zero = back(
        0,
        d_mid,
        [],
        wait_conv_zero,
        wait_short_zero,
        wait_in_zero,
        [scatter(one["early"], "dp")],
    )
    in_grads, got_grads = swapped([d_start, d_mid])
    early = joined(moving)
    tick, _ = early.plane(
        "halve_early",
        zero["vecs"][0],
        got_grads + [zero["grads_in"][1]],
    )
    one["seq"] = scatter(zero["handed"][0], "seq")
    one["all"] = one["seq"][0].astype(f32)
    got, _, tick = grads_split(
        "grad_in_0", zero, "grads_in", parts_in, [up_bits, down_bits], [tick]
    )
    late = joined(moving_in + got)
    late_cuts = [0, split, 2 * split, wide_rows + split, 2 * wide_rows]
    pack_tick = relay("after_in", [tick] + joined(got).arrived())

    packs = [small_grads(0, zero, pack_tick), one["pack"]]
    penalty = (filters[0][1] + 4.0 * filters[1][1]) / (chan * dp_count)
    penalty_high = penalty.astype(bf16)
    penalty_low = (penalty - penalty_high.astype(f32)).astype(bf16)
    mine, other = choose(packs)
    got = swap(other.astype(bf16))
    early_rest, tick = early.rest("merge_early", [tick, mine, got, one["seq"]])
    late.plane("halve_late", tick)
    early_zero = scatter(early_rest, "seq")[0].astype(f32)
    pack = (mine + got.astype(f32) + tick[0, 0]).astype(bf16)
    ends = jnp.broadcast_to(jnp.stack([penalty_high, penalty_low])[None], (shards, 2))
    pack = jnp.concatenate([pack, ends], axis=1)
    width = pack.shape[1]
    pack = jnp.pad(pack, ((0, 0), (0, 1024 - width % 1024))).reshape(shards, -1, 128)
    pack = lax.all_to_all(pack, ("dp", "seq"), split_axis=0, concat_axis=0, tiled=True)
    pack = jnp.sum(pack.astype(f32), axis=0).reshape(-1)

    late_rest, last_tick = late.rest("merge_late", [pack])
    late = line_sum(late_rest)
    late = [
        jnp.concatenate([late[late_cuts[k] : late_cuts[k + 1]] for k in (side, side + 2)], axis=0)
        for side in (1, 0)
    ]
    first_a, second_a = FF // D * top + top, (FF // D + 1) * rows
    cuts = [FF // D * top, first_a, first_a + FF // D * (rows - top), second_a]

    def spread_out(value):
        low = value[: cuts[0]].reshape(-1, top, HALF)
        high = value[cuts[1] : cuts[2]].reshape(-1, rows - top, HALF)
        return jnp.concatenate(
            [
                jnp.concatenate([low, high], axis=1).reshape(-1, HALF),
                value[cuts[0] : cuts[1]],
                value[cuts[2] :],
            ],
            axis=0,
        )

    early_zero = spread_out(early_zero)

    def turned(value):
        return value.swapaxes(-1, -2).reshape(1, -1, value.shape[-2])

    full = swapped([early_zero, one["all"]])[0]()
    full_in = swapped(late)[0]()
    down_rows = rows * (FF // D)
    edges = [down_rows, down_rows + rows]
    down = full[:, : edges[0]].reshape(2, FF // D, rows, HALF)
    taken = [0]

    def part(height, cols):
        begin = taken[0]
        taken[0] += height * cols
        return pack[begin : begin + height * cols].reshape(1, height, cols)

    vecs = part(7, rows)
    mixes = part(5, wide_rows)
    d_up_bias = part(1, ff_rows)
    d_last = part(FILT, rows)
    d_net = part(EMB + 2 + FILT, FILT)
    penalty = jnp.sum(part(1, 2))
    return (
        outputs(last_tick)[None, :, None],
        in_grads(last_tick)[None, :, None],
        vecs[:, 0:2],
        vecs[:, 2:6],
        turned(full_in),
        mixes,
        d_net[:, :EMB],
        d_net[:, EMB : EMB + 2],
        d_net[:, EMB + 2 :],
        d_last,
        vecs[:, 6:7],
        turned(full[:, edges[0] : edges[1]]),
        turned(full[:, edges[1] :]),
        d_up_bias,
        turned(down),
        penalty,
    )


def solution(mesh):
    by_section = P("section")
    shard = P("section", None, ("dp", "seq"))
    tokens = P("section", None, "dp", "seq", None)
    return jax.shard_map(
        local,
        mesh=mesh,
        in_specs=(P(None, "dp", "seq", None), P(None, "dp", "seq", None), P(None, "dp", None))
        + (by_section,) * 13,
        out_specs=(tokens, tokens, shard, shard, shard, shard)
        + (by_section,) * 3
        + (shard,) * 6
        + (P(),),
        check_vma=False,
    )
```

```python
import functools

import jax
import jax.numpy as jnp
import ml_dtypes
import numpy as np
from jax import lax
from jax.experimental import pallas as pl
from jax.experimental.pallas import tpu as pltpu
from jax.sharding import PartitionSpec as P

D = 768
FF = 3072
EMB = 33
FILT = 64
SEQ = 1024
NDOCS = 3
LONG_LAG = 32
BLK = 128
NB = SEQ // BLK
FREQ = 2 * BLK
PIECES = NB + NDOCS - 1
HALO = 16
TILE = 48
FF_TILE = 512

eps = 1e-05
highest = lax.Precision.HIGHEST
f32 = jnp.float32
bf16 = jnp.bfloat16
TICK = ((1, 1), f32)
HALF = D // 2
ACT_HIDDEN = 0
ACT_TWO = FF // 2
ACT_GATED = ACT_TWO + HALF
ACT_NORMED = ACT_GATED + HALF
ACT_COLS = ACT_NORMED + HALF
GRAD_PRE = 0
GRAD_MLP = FF
GRAD_BRANCH = FF + D
GRAD_COLS = FF + 2 * D
SPLIT = 80
VMEM_LIMIT = 56 * 1024 * 1024


def split_table(table):
    high = table.astype(ml_dtypes.bfloat16)
    low = (table - high.astype(np.float64)).astype(ml_dtypes.bfloat16)
    return high, low


def ring_table(offsets):
    theta = 2.0 * np.pi * (np.arange(BLK) + 0.5) / FREQ
    angles = offsets[:, None] * theta[None, :]
    return np.concatenate([np.cos(angles), -np.sin(angles)], axis=1)


def block_tables():
    fwd = ring_table(np.arange(BLK, dtype=np.float64))
    fwd_hi, fwd_lo = split_table(fwd)
    inv_hi, inv_lo = split_table(fwd.T / BLK)
    window = ring_table(np.arange(FREQ, dtype=np.float64) - BLK)
    window[0] = 0.0
    return fwd_hi, fwd_lo, inv_hi, inv_lo, window.astype(np.float32)


def position_table():
    positions = np.arange(SEQ, dtype=np.float32)
    band_count = (EMB - 1) // 2
    band_freq = np.float32(0.0001) + np.arange(band_count, dtype=np.float32) * np.float32(
        (band_count - 1 - 0.0001) / (band_count - 1)
    )
    angles = np.float32(2.0 * np.pi / SEQ) * positions[:, None] * band_freq[None, :]
    return np.concatenate(
        [(positions / SEQ)[:, None], np.cos(angles), np.sin(angles)], axis=1
    ).T.astype(np.float32)


def dot(left, right, dims=((1,), (0,))):
    return lax.dot_general(left, right, (dims, ((), ())), preferred_element_type=f32)


NT = ((1,), (1,))
TN = ((0,), (0,))


def norm_stats(values):
    centre = jnp.mean(values, axis=-1, keepdims=True)
    centred = values - centre
    variance = jnp.mean(centred * centred, axis=-1, keepdims=True)
    scale = lax.rsqrt(variance + eps)
    return centred * scale, scale


def norm_back(grad, gain, unit, scale):
    scaled = grad * gain
    return scale * (
        scaled
        - jnp.mean(scaled, axis=-1, keepdims=True)
        - unit * jnp.mean(scaled * unit, axis=-1, keepdims=True)
    )


def col_sum(values):
    return jnp.sum(values, axis=0, keepdims=True)


def place_masks(sc, rows, shard_len):
    pos = sc[1] * shard_len + lax.broadcasted_iota(jnp.int32, (rows, 1), 0)
    starts = pos == sc[2]
    after = pos == sc[2] + 1
    for doc in range(1, NDOCS):
        starts = starts | (pos == sc[2 + doc])
        after = after | (pos == sc[2 + doc] + 1)
    one = jnp.where(starts, 0.0, 1.0)
    two = jnp.where(starts | after, 0.0, 1.0)
    return one, two


def shifted(stream_ext):
    ext = stream_ext.astype(f32)
    return (
        ext[HALO:],
        pltpu.roll(ext, 1, 0)[HALO:],
        pltpu.roll(ext, 2, 0)[HALO:],
    )


def mix_row(p_ref, which, stream):
    row = 6 + 3 * which + stream
    return p_ref[row : row + 1, :]


def short_conv(st_ref, p_ref, stream, masks):
    zero, one, two = shifted(st_ref[:, stream * D : (stream + 1) * D])
    return (
        mix_row(p_ref, 4, stream)
        + mix_row(p_ref, 1, stream) * zero
        + mix_row(p_ref, 2, stream) * (one * masks[0])
        + mix_row(p_ref, 3, stream) * (two * masks[1])
    )


def fetch(own_first, own, rcv, dst, sem):
    @pl.when(own_first)
    def _():
        pltpu.make_async_copy(own, dst, sem).start()

    @pl.when(jnp.logical_not(own_first))
    def _():
        pltpu.make_async_copy(rcv, dst, sem).start()


def rows_at(start, size):
    return pl.ds(pl.multiple_of(start, 16), size)


def fetch_in(own_first, own, rcv, weight, sems):
    def part(ref, stream):
        return ref.at[0, :, pl.ds(stream * D, D)]

    def dest(stream):
        return weight.at[:, pl.ds(stream * D, D)]

    for stream in range(3):
        fetch(own_first, part(own, stream), part(rcv, stream), dest(stream), sems.at[stream])

    def wait(stream):
        pltpu.make_async_copy(part(own, stream), dest(stream), sems.at[stream]).wait()

    return wait


SMEM = pl.BlockSpec(memory_space=pltpu.SMEM)
VMEM = pl.BlockSpec(memory_space=pltpu.VMEM)
ANY = pl.BlockSpec(memory_space=pl.ANY)


def run(body, outs, ins, specs, scratch, name, flops=0, bytes_accessed=0, deps=(), through=()):
    taken, skipped, results = len(ins), len(deps) + len(through), len(outs)

    def wrapped(*refs):
        last = taken + skipped + results
        body(*refs[:taken], *refs[taken + skipped : last], *refs[last + len(through) :])

    return pl.pallas_call(
        wrapped,
        out_shape=[jax.ShapeDtypeStruct(shape, dtype) for shape, dtype in outs]
        + [jax.ShapeDtypeStruct(value.shape, value.dtype) for value in through],
        in_specs=specs + [ANY] * skipped,
        out_specs=[SMEM if out == TICK else VMEM for out in outs] + [ANY] * len(through),
        input_output_aliases={
            taken + len(deps) + index: results + index for index in range(len(through))
        },
        scratch_shapes=scratch,
        compiler_params=pltpu.CompilerParams(vmem_limit_bytes=VMEM_LIMIT),
        cost_estimate=pl.CostEstimate(
            flops=1, bytes_accessed=1, transcendentals=0
        ),
        name=name,
    )(*ins, *deps, *through)


def in_part(block, shard_len, count):
    chan = D // count

    def body(sc, x_ref, halo_ref, p_ref, own, rcv, normed_ref, st_ref, tick_ref, *rest):
        outs = rest[:count]
        tick_ref[0, 0] = 0.0
        weight, sig_t, sems = rest[count:]
        wait = fetch_in(sc[0] == block, own, rcv, weight, sems)
        ext = jnp.concatenate([halo_ref[...].astype(f32), x_ref[...].astype(f32)], axis=0)
        unit, _ = norm_stats(ext)
        normed = (unit * p_ref[0:1, :] + p_ref[2:3, :]).astype(bf16)
        normed_ref[...] = normed[HALO:]
        for stream in range(3):
            wait(stream)
            cols = slice(stream * D, (stream + 1) * D)
            st_ref[:, cols] = (dot(normed, weight[:, cols]) + mix_row(p_ref, 0, stream)).astype(bf16)
        masks = place_masks(sc, shard_len, shard_len)
        signal = short_conv(st_ref, p_ref, 2, masks) * short_conv(st_ref, p_ref, 1, masks)
        sig_t[...] = signal.T.astype(bf16)
        for step in range(count):
            outs[step][...] = sig_t[rows_at((sc[1] ^ step) * chan, chan), :]

    def call(sc, x, halo, params, own, rcv, deps):
        return run(
            body,
            [((shard_len, D), bf16), ((shard_len + HALO, 3 * D), bf16), TICK]
            + [((chan, shard_len), bf16)] * count,
            (sc, x, halo, params, own, rcv),
            [SMEM, VMEM, VMEM, VMEM, ANY, ANY],
            [
                pltpu.VMEM((D, 3 * D), bf16),
                pltpu.VMEM((D, shard_len), bf16),
                pltpu.SemaphoreType.DMA((3,)),
            ],
            f"in_part_{block}",
            2 * shard_len * D * 3 * D,
            D * 3 * D * 2,
            deps,
        )

    return call


def piece_scalars(sc):
    starts = [sc[2 + doc] for doc in range(NDOCS)] + [SEQ]
    lows, offsets = [], [0]
    for doc in range(NDOCS):
        low, high = starts[doc] // BLK, (starts[doc + 1] - 1) // BLK
        lows.append(low)
        offsets.append(offsets[-1] + high - low + 1)
    pieces = []
    for piece in range(PIECES):
        begin, stop, low, first, last = starts[0], starts[1], lows[0], offsets[0], offsets[1]
        for doc in range(1, NDOCS):
            here = piece >= offsets[doc]
            begin = jnp.where(here, starts[doc], begin)
            stop = jnp.where(here, starts[doc + 1], stop)
            low = jnp.where(here, lows[doc], low)
            first = jnp.where(here, offsets[doc], first)
            last = jnp.where(here, offsets[doc + 1], last)
        live = piece < offsets[NDOCS]
        blk = jnp.minimum(low + piece - first, NB - 1)
        begin = jnp.where(live, begin, 0)
        stop = jnp.where(live, stop, 0)
        first = jnp.where(live, first, piece + 1)
        last = jnp.where(live, last, piece)
        pieces.append((blk, begin, stop, first, last))
    return pieces


def piece_mask(piece):
    pos = piece[0] * BLK + lax.broadcasted_iota(jnp.int32, (1, BLK), 1)
    return (pos >= piece[1]) & (pos < piece[2])


def gather_blocks(sc, ins, blocks, per_shard):
    if isinstance(ins, (list, tuple)):
        for step, ref in enumerate(ins):
            source = sc[1] ^ step
            for part in range(per_shard):
                blocks[source * per_shard + part] = ref[:, part * BLK : (part + 1) * BLK]
        return
    for source in range(NB // per_shard):
        for part in range(per_shard):
            blocks[source * per_shard + part] = ins[source, :, part * BLK : (part + 1) * BLK]


def to_freq(pieces, blocks, masked, freq, tables, chan):
    for index, piece in enumerate(pieces):
        keep = jnp.where(piece_mask(piece), 1.0, 0.0)
        masked[index * chan : (index + 1) * chan, :] = (
            blocks[piece[0]].astype(f32) * keep
        ).astype(bf16)
    values = masked[...]
    freq[...] = dot(values, tables[0][...]) + dot(values, tables[1][...])


def from_freq(pieces, freq, out_blocks, tables, chan):
    values = freq[...]
    high = values.astype(bf16)
    low = (values - high.astype(f32)).astype(bf16)
    back = dot(high, tables[2][...]) + dot(low, tables[2][...]) + dot(high, tables[3][...])
    for index, piece in enumerate(pieces):
        mine = back[index * chan : (index + 1) * chan, :]
        before = out_blocks[piece[0]]
        out_blocks[piece[0]] = jnp.where(piece_mask(piece), mine, before)


def scatter_blocks(sc, outs, out_blocks, per_shard):
    if isinstance(outs, (list, tuple)):
        for step, ref in enumerate(outs):
            target = sc[1] ^ step
            for part in range(per_shard):
                ref[:, part * BLK : (part + 1) * BLK] = out_blocks[
                    target * per_shard + part
                ].astype(bf16)
        return
    for target in range(NB // per_shard):
        for part in range(per_shard):
            outs[target, :, part * BLK : (part + 1) * BLK] = out_blocks[
                target * per_shard + part
            ].astype(bf16)


def conv_part(block, shard_len, count):
    chan = D // count
    per_shard = shard_len // BLK
    tiles = chan // TILE

    def body(sc, filt, *rest):
        ins, tables, rest = rest[:count], rest[count : count + 4], rest[count + 4 :]
        outs, blocks, tick_ref = rest[:count], rest[count], rest[count + 1]
        masked, freq, total, out_blocks = rest[count + 2 :]
        tick_ref[0, 0] = 0.0
        gather_blocks(sc, ins, blocks, per_shard)
        pieces = piece_scalars(sc)
        to_freq(pieces, blocks, masked, freq, tables, chan)
        for index, piece in enumerate(pieces):
            for tile in range(tiles):

                def step(other, carry, index=index, piece=piece, tile=tile):
                    sum_re, sum_im = carry
                    rows = rows_at(other * chan + tile * TILE, TILE)
                    sig_re, sig_im = freq[rows, :BLK], freq[rows, BLK:]
                    lag = index - other
                    here = slice(tile * TILE, (tile + 1) * TILE)
                    fil_re, fil_im = filt[lag, here, :BLK], filt[lag, here, BLK:]
                    return (
                        sum_re + fil_re * sig_re - fil_im * sig_im,
                        sum_im + fil_re * sig_im + fil_im * sig_re,
                    )

                zero = jnp.zeros((TILE, BLK), f32)
                sum_re, sum_im = lax.fori_loop(piece[3], index + 1, step, (zero, zero))
                here = slice(index * chan + tile * TILE, index * chan + (tile + 1) * TILE)
                total[here, :BLK] = sum_re
                total[here, BLK:] = sum_im
        out_blocks[...] = jnp.zeros_like(out_blocks)
        from_freq(pieces, total, out_blocks, tables, chan)
        scatter_blocks(sc, outs, out_blocks, per_shard)

    def call(sc, filt, ins, tables, deps):
        return run(
            body,
            [((chan, shard_len), bf16)] * count + [((NB, chan, BLK), bf16), TICK],
            (sc, filt, *ins, *tables),
            [SMEM] + [VMEM] * (count + 5),
            [
                pltpu.VMEM((PIECES * chan, BLK), bf16),
                pltpu.VMEM((PIECES * chan, FREQ), f32),
                pltpu.VMEM((PIECES * chan, FREQ), f32),
                pltpu.VMEM((NB, chan, BLK), f32),
            ],
            f"conv_part_{block}",
            10 * PIECES * chan * BLK * FREQ,
            NB * chan * FREQ * 4,
            deps,
        )

    return call


def conv_back(block, shard_len, count):
    chan = D // count
    per_shard = shard_len // BLK
    tiles = chan // TILE

    def body(sc, filt, blocks, *rest):
        ins, rest = take(rest, block, count)
        tables, rest = rest[:4], rest[4:]
        outs, rest = take(rest, block, count)
        d_filt, tick_ref = rest[:2]
        d_blocks, masked, freq, d_freq, total, out_blocks = rest[2:]
        tick_ref[0, 0] = 0.0
        gather_blocks(sc, ins, d_blocks, per_shard)
        pieces = piece_scalars(sc)
        to_freq(pieces, blocks, masked, freq, tables, chan)
        to_freq(pieces, d_blocks, masked, d_freq, tables, chan)
        d_filt[...] = jnp.zeros_like(d_filt)
        for index, piece in enumerate(pieces):
            for tile in range(tiles):
                rows = slice(index * chan + tile * TILE, index * chan + (tile + 1) * TILE)
                here = slice(tile * TILE, (tile + 1) * TILE)

                def step(other, carry, index=index, here=here, rows=rows, tile=tile):
                    sum_re, sum_im = carry
                    sig_re, sig_im = freq[rows, :BLK], freq[rows, BLK:]
                    there = rows_at(other * chan + tile * TILE, TILE)
                    der_re, der_im = d_freq[there, :BLK], d_freq[there, BLK:]
                    lag = other - index
                    fil_re, fil_im = filt[lag, here, :BLK], filt[lag, here, BLK:]
                    d_filt[lag, here, :BLK] += sig_re * der_re + sig_im * der_im
                    d_filt[lag, here, BLK:] += sig_re * der_im - sig_im * der_re
                    return (
                        sum_re + fil_re * der_re + fil_im * der_im,
                        sum_im + fil_re * der_im - fil_im * der_re,
                    )

                zero = jnp.zeros((TILE, BLK), f32)
                sum_re, sum_im = lax.fori_loop(index, piece[4], step, (zero, zero))
                total[rows, :BLK] = sum_re
                total[rows, BLK:] = sum_im
        out_blocks[...] = jnp.zeros_like(out_blocks)
        from_freq(pieces, total, out_blocks, tables, chan)
        scatter_blocks(sc, outs, out_blocks, per_shard)

    def call(sc, filt, blocks, ins, tables, deps):
        return run(
            body,
            chunk_shapes(block, count, chan, shard_len) + [((NB, chan, FREQ), f32), TICK],
            (sc, filt, blocks, *ins, *tables),
            [SMEM] + [VMEM] * (6 + len(ins)),
            [
                pltpu.VMEM((NB, chan, BLK), bf16),
                pltpu.VMEM((PIECES * chan, BLK), bf16),
                pltpu.VMEM((PIECES * chan, FREQ), f32),
                pltpu.VMEM((PIECES * chan, FREQ), f32),
                pltpu.VMEM((PIECES * chan, FREQ), f32),
                pltpu.VMEM((NB, chan, BLK), f32),
            ],
            f"conv_back_{block}",
            14 * PIECES * chan * BLK * FREQ,
            NB * chan * FREQ * 8,
            deps,
        )

    return call


def chunk_shapes(block, count, chan, shard_len):
    if block == 1:
        return [((chan, shard_len), bf16)] * count
    return [((count, chan, shard_len), bf16)]


def take(refs, block, count):
    if block == 1:
        return list(refs[:count]), refs[count:]
    return refs[0], refs[1:]


def token_major(ins):
    return ins[...].reshape(D, ins.shape[2]).astype(f32).T


def weight_scratch():
    return [
        pltpu.VMEM((D, D), bf16),
        pltpu.VMEM((D, FF), bf16),
        pltpu.VMEM((FF, D), bf16),
        pltpu.SemaphoreType.DMA((1 + 2 * (FF // FF_TILE),)),
    ]


def fetch_mlp(own_first, pairs, dsts, sems, out_first):
    tiles = FF // FF_TILE
    (out_own, out_rcv), (up_own, up_rcv), (down_own, down_rcv) = pairs
    w_out, w_up, w_down = dsts

    def start_out():
        fetch(own_first, out_own.at[0], out_rcv.at[0], w_out, sems.at[0])

    def start_up(tile):
        cols = pl.ds(tile * FF_TILE, FF_TILE)
        fetch(
            own_first,
            up_own.at[0, :, cols],
            up_rcv.at[0, :, cols],
            w_up.at[:, cols],
            sems.at[1 + tile],
        )

    def start_down(tile):
        rows = pl.ds(tile * FF_TILE, FF_TILE)
        fetch(
            own_first,
            down_own.at[0, rows],
            down_rcv.at[0, rows],
            w_down.at[rows],
            sems.at[1 + tiles + tile],
        )

    if out_first:
        start_out()
    for tile in range(tiles):
        if out_first:
            start_up(tile)
            start_down(tile)
        else:
            start_down(tile)
            start_up(tile)
    if not out_first:
        start_out()

    def wait_out():
        pltpu.make_async_copy(out_own.at[0], w_out, sems.at[0]).wait()

    def wait_up(tile):
        cols = pl.ds(pl.multiple_of(tile * FF_TILE, FF_TILE), FF_TILE)
        pltpu.make_async_copy(up_own.at[0, :, cols], w_up.at[:, cols], sems.at[1 + tile]).wait()
        return cols

    def wait_down(tile):
        rows = pl.ds(pl.multiple_of(tile * FF_TILE, FF_TILE), FF_TILE)
        pltpu.make_async_copy(
            down_own.at[0, rows], w_down.at[rows], sems.at[1 + tiles + tile]
        ).wait()
        return rows

    return wait_out, wait_up, wait_down


GELU_SCALE = 0.7978845608028654
GELU_CUBE = 0.044715


def out_part(block, shard_len, count):
    chan = D // count

    def body(sc, x_ref, st_ref, normed_one, p_ref, bias_ref, *rest):
        ins, rest = rest[:count], rest[count:]
        pairs = (rest[0:2], rest[2:4], rest[4:6])
        result_ref, residual_ref, mine_ref, other_ref, slope_ref, cmix_ref = rest[6:12]
        turned, w_out, w_up, w_down, sems, normed_ref, gated_ref, hidden_ref = rest[12:]

        def keep_halves(ref, start, half):
            for side, target in ((sc[0], mine_ref), (1 - sc[0], other_ref)):
                cols = pl.ds(pl.multiple_of(side * half, half), half)
                target[:, start : start + half] = ref[:, cols]

        wait_out, wait_up, wait_down = fetch_mlp(
            sc[0] == block, pairs, (w_out, w_up, w_down), sems, True
        )
        masks = place_masks(sc, shard_len, shard_len)
        for step, ref in enumerate(ins):
            turned[rows_at((sc[1] ^ step) * chan, chan), :] = ref[...]
        conv = turned[...].astype(f32).T
        signal = short_conv(st_ref, p_ref, 2, masks) * short_conv(st_ref, p_ref, 1, masks)
        cmix = conv + p_ref[21:22, :] * signal
        cmix_ref[...] = cmix
        gated = (cmix * short_conv(st_ref, p_ref, 0, masks)).astype(bf16)
        gated_ref[...] = gated
        wait_out()
        residual = x_ref[...].astype(f32) + dot(gated, w_out[...]) + p_ref[3:4, :]
        residual_ref[...] = residual
        unit, _ = norm_stats(residual)
        normed_ref[...] = (unit * p_ref[1:2, :] + p_ref[4:5, :]).astype(bf16)
        result_ref[...] = residual + p_ref[5:6, :]

        @pl.loop(0, FF // FF_TILE)
        def _(tile):
            cols = wait_up(tile)
            pre = dot(normed_ref[...], w_up[:, cols]) + bias_ref[:, cols]
            square = pre * pre
            bent = jnp.tanh(GELU_SCALE * pre * (1.0 + GELU_CUBE * square))
            half = 0.5 * (1.0 + bent)
            slope = half + (0.5 * GELU_SCALE) * pre * (1.0 - bent * bent) * (
                1.0 + 3.0 * GELU_CUBE * square
            )
            hidden = (pre * half).astype(bf16)
            hidden_ref[:, cols] = hidden
            slope_ref[:, cols] = slope.astype(bf16)
            rows = wait_down(tile)
            result_ref[...] += dot(hidden, w_down[rows, :])

        keep_halves(hidden_ref, ACT_HIDDEN, FF // 2)
        keep_halves(normed_ref, ACT_TWO, HALF)
        keep_halves(gated_ref, ACT_GATED, HALF)
        keep_halves(normed_one, ACT_NORMED, HALF)

    def call(sc, x, st, normed, params, up_bias, ins, weights):
        return run(
            body,
            [
                ((shard_len, D), f32),
                ((shard_len, D), f32),
                ((shard_len, ACT_COLS), bf16),
                ((shard_len, ACT_COLS), bf16),
                ((shard_len, FF), bf16),
                ((shard_len, D), f32),
            ],
            (sc, x, st, normed, params, up_bias, *ins, *weights),
            [SMEM] + [VMEM] * (5 + count) + [ANY] * 6,
            [pltpu.VMEM((D, shard_len), bf16)]
            + weight_scratch()
            + [
                pltpu.VMEM((shard_len, D), bf16),
                pltpu.VMEM((shard_len, D), bf16),
                pltpu.VMEM((shard_len, FF), bf16),
            ],
            f"out_part_{block}",
            2 * shard_len * D * (D + 2 * FF),
            D * (D + 2 * FF) * 2,
        )

    return call


def out_back(block, shard_len, count):
    chan = D // count

    def body(sc, grad_ref, residual_ref, slope_ref, st_ref, p_ref, *rest):
        pairs = (rest[0:2], rest[2:4], rest[4:6])
        grads_ref, dres_ref, dg_ref, vec_ref, dub_ref, tick_ref = rest[6:12]
        outs, rest = take(rest[12:], block, count)
        tick_ref[0, 0] = 0.0
        turned, w_out, w_up, w_down, sems, total = rest
        wait_out, wait_up, wait_down = fetch_mlp(
            sc[0] == block, pairs, (w_out, w_up, w_down), sems, False
        )
        grad = grad_ref[...].astype(f32)
        gm = grad.astype(bf16)
        grads_ref[:, GRAD_MLP : GRAD_MLP + D] = gm
        total[...] = jnp.zeros_like(total)

        @pl.loop(0, FF // FF_TILE)
        def _(tile):
            rows = wait_down(tile)
            d_hidden = dot(grads_ref[:, GRAD_MLP : GRAD_MLP + D], w_down[rows, :], NT)
            d_pre = (d_hidden * slope_ref[:, rows].astype(f32)).astype(bf16)
            grads_ref[:, rows] = d_pre
            dub_ref[:, rows] = jnp.broadcast_to(col_sum(d_pre.astype(f32)), (8, FF_TILE))
            cols = wait_up(tile)
            total[...] += dot(d_pre, w_up[:, cols], NT)

        d_normed = total[...]
        unit, scale = norm_stats(residual_ref[...])
        d_res = grad + norm_back(d_normed, p_ref[1:2, :], unit, scale)
        dres_ref[...] = d_res
        gb = d_res.astype(bf16)
        grads_ref[:, GRAD_BRANCH : GRAD_BRANCH + D] = gb
        wait_out()
        dg = dot(gb, w_out[...], NT).astype(bf16)
        dg_ref[...] = dg
        masks = place_masks(sc, shard_len, shard_len)
        d_conv = dg.astype(f32) * short_conv(st_ref, p_ref, 0, masks)
        turned[...] = d_conv.T.astype(bf16)
        for step in range(count):
            if isinstance(outs, list):
                outs[step][...] = turned[rows_at((sc[1] ^ step) * chan, chan), :]
            else:
                outs[step] = turned[step * chan : (step + 1) * chan, :]
        vec_ref[...] = jnp.concatenate(
            [
                col_sum(d_normed * unit),
                col_sum(d_normed),
                col_sum(gb.astype(f32)),
                col_sum(gm.astype(f32)),
                jnp.zeros((4, D), f32),
            ],
            axis=0,
        )

    def call(sc, grad, residual, slope, st, params, weights, deps):
        return run(
            body,
            [
                ((shard_len, GRAD_COLS), bf16),
                ((shard_len, D), f32),
                ((shard_len, D), bf16),
                ((8, D), f32),
                ((8, FF), f32),
                TICK,
            ]
            + chunk_shapes(block, count, chan, shard_len),
            (sc, grad, residual, slope, st, params, *weights),
            [SMEM] + [VMEM] * 5 + [ANY] * 6,
            [pltpu.VMEM((D, shard_len), bf16)]
            + weight_scratch()
            + [pltpu.VMEM((shard_len, D), f32)],
            f"out_back_{block}",
            2 * shard_len * D * (D + 2 * FF),
            D * (D + 2 * FF) * 2,
            deps,
        )

    return call


def short_back(block, shard_len, count):
    chan = D // count

    def body(sc, st_ref, dg_ref, cmix_ref, p_ref, *rest):
        ins, rest = take(rest, block, count)
        ds_ref, head_ref, vec_ref, tick_ref, turned = rest
        tick_ref[0, 0] = 0.0
        masks = place_masks(sc, shard_len, shard_len)
        if isinstance(ins, list):
            for step, ref in enumerate(ins):
                turned[rows_at((sc[1] ^ step) * chan, chan), :] = ref[...]
            d_signal = turned[...].astype(f32).T
        else:
            d_signal = token_major(ins)
        dg = dg_ref[...].astype(f32)
        d_conv = dg * short_conv(st_ref, p_ref, 0, masks)
        inner = short_conv(st_ref, p_ref, 1, masks)
        value = short_conv(st_ref, p_ref, 2, masks)
        d_signal = d_signal + p_ref[21:22, :] * d_conv
        rows = [None] * 16
        rows[12] = col_sum(d_conv * value * inner)
        for stream, d_short in enumerate((dg * cmix_ref[...], d_signal * value, d_signal * inner)):
            cols = slice(stream * D, (stream + 1) * D)
            ds_ref[:, cols] = d_short
            head_ref[:, cols] = d_short[:HALO]
            zero, one, two = shifted(st_ref[:, cols])
            rows[stream] = col_sum(d_short * zero)
            rows[3 + stream] = col_sum(d_short * (one * masks[0]))
            rows[6 + stream] = col_sum(d_short * (two * masks[1]))
            rows[9 + stream] = col_sum(d_short)
        for index in range(13, 16):
            rows[index] = jnp.zeros((1, D), f32)
        vec_ref[...] = jnp.concatenate(rows, axis=0)

    def call(sc, st, dg, cmix, params, ins, deps):
        return run(
            body,
            [((shard_len, 3 * D), f32), ((HALO, 3 * D), f32), ((16, D), f32), TICK],
            (sc, st, dg, cmix, params, *ins),
            [SMEM] + [VMEM] * (4 + len(ins)),
            [pltpu.VMEM((D, shard_len), bf16)],
            f"short_back_{block}",
            40 * shard_len * D,
            shard_len * D * 20,
            deps,
        )

    return call


def in_back(block, shard_len):
    def body(sc, ds_ref, halo_ref, x_ref, dres_ref, p_ref, own, rcv, dst_ref, dx_ref, vec_ref, weight, sems):
        wait = fetch_in(sc[0] == block, own, rcv, weight, sems)
        long = shard_len + HALO
        one, two = place_masks(sc, long, shard_len)
        d_normed = jnp.zeros((shard_len, D), f32)
        rows = []
        for stream in range(3):
            cols = slice(stream * D, (stream + 1) * D)
            ext = jnp.concatenate([ds_ref[:, cols], halo_ref[:, cols]], axis=0)
            d_stream = (
                mix_row(p_ref, 1, stream) * ext[:shard_len]
                + mix_row(p_ref, 2, stream) * pltpu.roll(ext * one, long - 1, 0)[:shard_len]
                + mix_row(p_ref, 3, stream) * pltpu.roll(ext * two, long - 2, 0)[:shard_len]
            ).astype(bf16)
            dst_ref[:, cols] = d_stream
            rows.append(col_sum(d_stream.astype(f32)))
            wait(stream)
            d_normed = d_normed + dot(d_stream, weight[:, cols], NT)
        unit, scale = norm_stats(x_ref[...].astype(f32))
        dx_ref[...] = dres_ref[...] + norm_back(d_normed, p_ref[0:1, :], unit, scale)
        vec_ref[...] = jnp.concatenate(
            [col_sum(d_normed * unit), col_sum(d_normed)] + rows + [jnp.zeros((3, D), f32)], axis=0
        )

    def call(sc, d_short, halo, x, d_res, params, own, rcv, deps, through):
        return run(
            body,
            [((shard_len, 3 * D), bf16), ((shard_len, D), f32), ((8, D), f32)],
            (sc, d_short, halo, x, d_res, params, own, rcv),
            [SMEM] + [VMEM] * 5 + [ANY] * 2,
            [pltpu.VMEM((D, 3 * D), bf16), pltpu.SemaphoreType.DMA((3,))],
            f"in_back_{block}",
            2 * shard_len * D * 3 * D,
            D * 3 * D * 2,
            deps,
            through,
        )

    return call


def weight_grad(name, parts, first_bits, shard_len, shards, count):
    groups = len(first_bits)
    sizes = [0] * groups
    for _, rows, _, cols, splits in parts:
        for group, _, size in splits:
            sizes[group] += size * (cols // HALF)
    shapes, firsts = [], []
    for size, bit in zip(sizes, first_bits):
        firsts.append(len(shapes))
        shapes += [(shards, size, HALF)] if bit is None else [(shards // 2, size, HALF)] * 2

    def body(sc, g_own, g_rcv, a_own, a_rcv, *outs):
        outs[-1][0, 0] = 0.0
        me = sc[2 + NDOCS] * count
        bases = [0] * groups
        for g_start, rows, a_start, cols, splits in parts:
            block = rows // shards
            chunk = 8 * block if block % 32 else 4 * block
            acts = slice(a_start, a_start + cols)
            starts = list(bases)

            @pl.loop(0, rows // chunk)
            def _(step, starts=starts, g_start=g_start, chunk=chunk, block=block, acts=acts, cols=cols, splits=splits):
                here = pl.ds(pl.multiple_of(g_start + step * chunk, 128), chunk)
                full = dot(g_own[:, here], a_own[:, acts], TN) + dot(g_rcv[:, here], a_rcv[:, acts], TN)
                for index in range(chunk // block):
                    device = step * (chunk // block) + index
                    for group, begin, size in splits:
                        bit = first_bits[group]
                        if bit is None:
                            slot = device
                        else:
                            away = device ^ me
                            low = away & ((1 << bit) - 1)
                            slot = ((away >> (bit + 1)) << bit) | low
                            sent = (away >> bit) & 1

                        def store(ref, group=group, begin=begin, size=size, slot=slot, index=index):
                            for part in range(cols // HALF):
                                top = starts[group] + part * size
                                ref[slot, top : top + size, :] = full[
                                    index * block + begin : index * block + begin + size,
                                    part * HALF : (part + 1) * HALF,
                                ].astype(bf16)

                        first = firsts[group]
                        if bit is None:
                            store(outs[first])
                        else:
                            pl.when(sent == 1)(functools.partial(store, outs[first]))
                            pl.when(sent == 0)(functools.partial(store, outs[first + 1]))

            for group, _, size in splits:
                bases[group] += size * (cols // HALF)

    def call(sc, *ins, deps=()):
        flops = sum(4 * shard_len * rows * cols for _, rows, _, cols, _ in parts)
        outs = run(
            body,
            [(shape, bf16) for shape in shapes] + [TICK],
            (sc, *ins),
            [SMEM] + [VMEM] * 4,
            [],
            name,
            flops,
            flops // 256,
            deps,
        )
        return [
            outs[first] if bit is None else outs[first : first + 2]
            for first, bit in zip(firsts, first_bits)
        ], outs[-1]

    return call


def weight_grad_plain(parts, first_bits, shards, me):
    groups = len(first_bits)

    def call(_, g_own, g_rcv, a_own, a_rcv, deps=()):
        gathered = [[] for _ in range(groups)]
        for g_start, rows, a_start, cols, splits in parts:
            block = rows // shards
            full = sum(
                jnp.einsum(
                    "tn,tk->nk",
                    g[:, g_start : g_start + rows],
                    a[:, a_start : a_start + cols],
                    preferred_element_type=f32,
                )
                for g, a in ((g_own, a_own), (g_rcv, a_rcv))
            ).astype(bf16)
            full = full.reshape(shards, block, cols // HALF, HALF).transpose(0, 2, 1, 3)
            for group, begin, size in splits:
                piece = full[:, :, begin : begin + size]
                gathered[group].append(piece.reshape(shards, -1, HALF))
        outs = []
        for group in range(groups):
            whole = jnp.concatenate(gathered[group], axis=1)
            bit = first_bits[group]
            if bit is None:
                outs.append(whole)
                continue
            whole = whole[jnp.arange(shards, dtype=jnp.int32) ^ me]
            whole = whole.reshape((shards >> (bit + 1), 2, 1 << bit) + whole.shape[1:])
            outs.append(
                [whole[:, side].reshape((shards // 2,) + whole.shape[3:]) for side in (1, 0)]
            )
        return outs, jnp.zeros((1, 1), f32)

    return call


def halving(name, groups, count):
    def call(deps, through=None):
        ins, outs, in_specs, out_specs, lists = [], [], [], [], []
        alias = {}
        steps = None
        for group in groups:
            height, sizes = sum(kept.shape[1] for kept, _, _ in group), []
            for kept, got, spot in group:
                blocks, rows, cols = kept.shape
                inner = count << spot
                outer = blocks // (2 * inner)
                steps = outer * inner
                ins += [v.reshape(outer, 2, inner, rows, cols) for v in (kept, got)]
                in_specs += [
                    pl.BlockSpec(
                        (1, 2, 1, rows, cols), lambda i, inner=inner: (i // inner, 0, i % inner, 0, 0)
                    )
                ] * 2
                sizes.append(rows)
            outs += [jax.ShapeDtypeStruct((outer, inner, height, cols), bf16)] * 2
            out_specs += [
                pl.BlockSpec(
                    (1, 1, height, cols), lambda i, inner=inner: (i // inner, i % inner, 0, 0)
                )
            ] * 2
            lists.append(sizes)
        taken = len(ins)
        if through is not None:
            alias = {taken + len(deps): len(outs) + 1}
            deps = [*deps, through]

        def body(*refs):
            out_refs = refs[taken + len(deps) :]
            out_refs[2 * len(groups)][0, 0] = 0.0
            index = 0
            for group, sizes in enumerate(lists):
                begin = 0
                for size in sizes:
                    kept, got = refs[index : index + 2]
                    index += 2
                    for side, ref in ((1, out_refs[2 * group]), (0, out_refs[2 * group + 1])):
                        ref[0, 0, begin : begin + size, :] = (
                            kept[0, side, 0].astype(f32) + got[0, side, 0].astype(f32)
                        ).astype(bf16)
                    begin += size

        values = pl.pallas_call(
            body,
            grid=(steps,),
            out_shape=outs
            + [jax.ShapeDtypeStruct(*TICK)]
            + [jax.ShapeDtypeStruct(through.shape, through.dtype) for _ in alias],
            in_specs=in_specs + [ANY] * len(deps),
            out_specs=out_specs + [SMEM] + [ANY] * len(alias),
            input_output_aliases=alias,
            compiler_params=pltpu.CompilerParams(vmem_limit_bytes=VMEM_LIMIT),
            cost_estimate=pl.CostEstimate(flops=1, bytes_accessed=1, transcendentals=0),
            name=name,
        )(*ins, *deps)
        flat = [v.reshape((-1,) + v.shape[2:]) for v in values[: 2 * len(groups)]]
        pairs_out = [flat[2 * group : 2 * group + 2] for group in range(len(groups))]
        return pairs_out, values[2 * len(groups)], values[-1] if alias else None

    return call


def relay(name, deps):
    def body(tick_ref):
        tick_ref[0, 0] = 0.0

    return run(body, [TICK], [], [], [], name, deps=deps)[0]


def merging(name, sizes, count):
    def call(terms, deps):
        taken, rows = 2 * len(terms), sum(sizes)

        def body(*refs):
            out_ref, tick_ref = refs[taken + len(deps) :]
            tick_ref[0, 0] = 0.0
            begin = 0
            for group, size in enumerate(sizes):
                kept, got = refs[2 * group : 2 * group + 2]
                out_ref[0, begin : begin + size, :] = (
                    kept[0].astype(f32) + got[0].astype(f32)
                ).astype(bf16)
                begin += size

        def block(size):
            return pl.BlockSpec((1, size, HALF), lambda i: (i, 0, 0))

        return pl.pallas_call(
            body,
            grid=(count,),
            out_shape=[
                jax.ShapeDtypeStruct((count, rows, HALF), bf16),
                jax.ShapeDtypeStruct(*TICK),
            ],
            in_specs=[block(size) for size in sizes for _ in range(2)] + [ANY] * len(deps),
            out_specs=[block(rows), SMEM],
            compiler_params=pltpu.CompilerParams(vmem_limit_bytes=VMEM_LIMIT),
            cost_estimate=pl.CostEstimate(flops=1, bytes_accessed=1, transcendentals=0),
            name=name,
        )(*[value for kept, got, _ in terms for value in (kept, got)], *deps)

    return call


def pairs(count, step):
    return [(index, index ^ step) for index in range(count)]


def swap(value):
    return lax.ppermute(value, "section", pairs(2, 1))


def exchange_apart(chunks):
    count = len(chunks)
    return [chunks[0]] + [
        lax.ppermute(chunks[step], "seq", pairs(count, step)) for step in range(1, count)
    ]


def moved(block, chunks):
    return exchange_apart(chunks) if block == 1 else [exchange(chunks[0])]


def exchange(chunks):
    return lax.all_to_all(chunks, "seq", split_axis=0, concat_axis=0, tiled=True)


class Reduction:
    def __init__(self, groups, dp_count, count):
        self.sizes = (dp_count, count)
        self.terms = []
        for (sent, kept), bits in groups:
            self.terms.append((kept, self.over_dp(sent, bits[0]), list(bits[1:])))

    def arrived(self):
        return [got for _, got, _ in self.terms]

    def over_dp(self, value, bit):
        return lax.ppermute(value, "dp", pairs(self.sizes[0], (1 << bit) // self.sizes[1]))

    def plane(self, name, tick, deps=(), through=None):
        handed = through
        for turn in range(len(self.terms[0][2])):
            orders, groups = [], []
            for kept, got, left in self.terms:
                if left not in orders:
                    orders.append(left)
                    groups.append([])
                spot = sum(1 for other in left[1:] if other < left[0])
                groups[orders.index(left)].append((kept, got, spot))
            values, tick, passed = halving(f"{name}_{turn}", groups, self.sizes[1])(
                [tick, *deps], None if turn else through
            )
            handed = handed if passed is None else passed
            self.terms = [
                (keep, self.over_dp(send, left[0]), left[1:])
                for (send, keep), left in zip(values, orders)
            ]
        return tick, handed

    def rest(self, name, deps):
        sizes = [kept.shape[1] for kept, _, _ in self.terms]
        if any(size % 16 for size in sizes):
            parts = [
                (kept.astype(f32) + got.astype(f32)).astype(bf16) for kept, got, _ in self.terms
            ]
            return jnp.concatenate(parts, axis=1), jnp.zeros((1, 1), f32)
        return merging(name, sizes, self.sizes[1])(self.terms, deps)


def joined(parts):
    whole = Reduction([], *parts[0].sizes)
    for part in parts:
        whole.terms += part.terms
    return whole


def line_sum(values):
    return jnp.sum(exchange(values).astype(f32), axis=0)


def scatter(value, axis):
    blocks, rows, cols = value.shape
    value = value.reshape(blocks * rows, cols)
    return lax.psum_scatter(value, axis, scatter_dimension=0, tiled=True).reshape(-1, rows, cols)


def mat(spec, left, right):
    return jnp.einsum(spec, left, right, precision=highest, preferred_element_type=f32)


def filter_state(net, last, decay, pos, window):
    first_w, inner_b, second_w = net[:EMB], net[EMB : EMB + 2], net[EMB + 2 :]
    pre_a = mat("ef,en->fn", first_w, pos) + inner_b[0][:, None]
    hid_a = jnp.sin(pre_a)
    pre_b = mat("gf,gn->fn", second_w, hid_a) + inner_b[1][:, None]
    hid_b = jnp.sin(pre_b)
    taps = mat("fc,fn->cn", last, hid_b) * decay
    blocks = taps.reshape(taps.shape[0], NB, BLK)
    filt = mat("cmn,nk->mck", blocks, window[BLK:])
    behind = mat("cmn,nk->mck", blocks[:, :-1], window[:BLK])
    filt = filt + jnp.pad(behind, ((1, 0), (0, 0), (0, 0)))
    energy = taps * taps
    share = jnp.sum(jnp.sum(energy[:, LONG_LAG:], axis=1) / (jnp.sum(energy, axis=1) + 1e-06))
    return filt, share, (pre_a, hid_a, pre_b, hid_b, second_w)


def split(value):
    high = value.astype(bf16)
    return high, (value - high.astype(f32)).astype(bf16)


def dot_split(left, right, dims):
    total = dot(left[0], right[0], dims)
    if left[1] is not None:
        total = total + dot(left[1], right[0], dims)
    if right[1] is not None:
        total = total + dot(left[0], right[1], dims)
    return total


NN = ((1,), (0,))
POS_ROWS = 40


def net_back(block, chan):
    def body(d_filt, pre_a, hid_a, pre_b, hid_b, second, last, decay, pos, win_hi, win_lo, first_ref, second_ref, last_ref, tick_ref, taps):
        tick_ref[0, 0] = 0.0
        behind = (win_hi[:BLK, :], win_lo[:BLK, :])
        ahead = (win_hi[BLK:, :], win_lo[BLK:, :])
        for m in range(NB):
            d_block = dot_split(split(d_filt[m]), ahead, NT)
            if m + 1 < NB:
                d_block = d_block + dot_split(split(d_filt[m + 1]), behind, NT)
            cols = slice(m * BLK, (m + 1) * BLK)
            taps[:, cols] = d_block * (decay[:, cols] * (1.0 / BLK))
        d_out = split(taps[...])
        ones = jnp.ones((8, SEQ), f32)
        last_ref[...] = dot_split(split(hid_b[...]), d_out, NT)
        d_b = split(dot_split((last[...].astype(bf16), None), d_out, NN) * jnp.cos(pre_b[...]))
        second_ref[...] = dot_split(
            split(jnp.concatenate([hid_a[...], ones], axis=0)), d_b, NT
        )
        d_a = split(dot_split((second[...].astype(bf16), None), d_b, NN) * jnp.cos(pre_a[...]))
        first_ref[...] = dot_split(split(pos[...]), d_a, NT)

    def call(d_filt, state, last, decay, pos, window, deps):
        return run(
            body,
            [((POS_ROWS, FILT), f32), ((FILT + 8, FILT), f32), ((FILT, chan), f32), TICK],
            (d_filt, *state, last, decay, pos, *window),
            [VMEM] * 11,
            [pltpu.VMEM((chan, SEQ), f32)],
            f"net_back_{block}",
            0,
            0,
            deps,
        )

    return call


def local(
    layer_input,
    out_cot,
    doc_lengths,
    norm_gains,
    biases,
    in_weight,
    mix_vecs,
    filt_first,
    filt_inner_bias,
    filt_second,
    filt_last,
    filt_skip,
    out_weight,
    up_weight,
    up_bias,
    down_weight,
):
    count = lax.axis_size("seq")
    dp_count = lax.axis_size("dp")
    section = lax.axis_index("section")
    place = lax.axis_index("seq")
    first = section == 0
    shard_len = layer_input.shape[2]
    chan = D // count
    fwd_hi, fwd_lo, inv_hi, inv_lo, window = block_tables()
    tables = tuple(jnp.asarray(t) for t in (fwd_hi, fwd_lo, inv_hi, inv_lo))
    window = jnp.asarray(window)
    pos = jnp.asarray(position_table())
    pos_ext = jnp.asarray(
        np.concatenate(
            [position_table(), np.ones((1, SEQ)), np.zeros((POS_ROWS - EMB - 1, SEQ))]
        ).astype(np.float32)
    )
    window_split = tuple(jnp.asarray(part) for part in split_table(block_tables()[4].astype(np.float64)))

    def own_micro(value):
        return lax.dynamic_index_in_dim(value, section, 0, keepdims=False)[0]

    x_zero = own_micro(layer_input)
    cot = own_micro(out_cot)
    lengths = own_micro(doc_lengths)
    starts = jnp.cumsum(lengths) - lengths
    sc = jnp.concatenate(
        [jnp.stack([section, place]), starts, lax.axis_index("dp")[None]]
    ).astype(jnp.int32)

    def behind(rows):
        return lax.ppermute(rows, "seq", [(index, index + 1) for index in range(count - 1)])

    def ahead(rows):
        return lax.ppermute(rows, "seq", [(index + 1, index) for index in range(count - 1)])

    halo = behind(x_zero[-HALO:])
    small = jnp.concatenate(
        [
            norm_gains[0],
            biases[0],
            mix_vecs[0].reshape(15, D),
            filt_skip[0],
            up_bias[0].reshape(4, D),
            filt_last[0],
        ],
        axis=0,
    )
    net = jnp.concatenate([filt_first[0], filt_inner_bias[0], filt_second[0]], axis=0)
    small_rcv, net_rcv = swap(small), swap(net)
    rcv_in, rcv_out, rcv_up, rcv_down = (
        swap(in_weight),
        swap(out_weight),
        swap(up_weight),
        swap(down_weight),
    )
    mlp_pairs = (out_weight, rcv_out, up_weight, rcv_up, down_weight, rcv_down)
    params, nets = [], []
    for block in range(2):
        mine = section == block
        params.append(jnp.where(mine, small, small_rcv).astype(f32))
        nets.append(jnp.where(mine, net, net_rcv).astype(f32))
    tokens = [p[:24] for p in params]
    up_biases = [p[22:26].reshape(1, FF) for p in params]
    lasts = [lax.dynamic_slice_in_dim(p[26:90], place * chan, chan, 1) for p in params]
    chan_ids = (jnp.arange(chan, dtype=jnp.int32) + place * chan).astype(f32)
    times = jnp.arange(SEQ, dtype=f32) / SEQ
    decay = jnp.exp(-(3.0 + 12.0 * chan_ids / (D - 1))[:, None] * times[None, :])

    x = x_zero
    kept = []
    results = []
    filters = []
    for block in range(2):
        normed, st, tick, *chunks = in_part(block, shard_len, count)(
            sc, x, halo, tokens[block], in_weight, rcv_in, []
        )
        if block == 0:
            filters.append(filter_state(nets[0] + tick[0, 0], lasts[0], decay, pos, window))
        *chunks, blocks, tick = conv_part(block, shard_len, count)(
            sc, filters[block][0], exchange_apart(chunks), tables, [k[5] for k in kept]
        )
        if block == 0:
            filters.append(filter_state(nets[1] + tick[0, 0], lasts[1], decay, pos, window))
        result, residual, acts, acts_other, slope, cmix = out_part(block, shard_len, count)(
            sc, x, st, normed, tokens[block], up_biases[block], exchange_apart(chunks), mlp_pairs
        )
        kept.append((x, st, blocks, residual, acts, swap(acts_other), slope, cmix))
        results.append(result)
        x = result
        if block == 0:
            halo = behind(result[-HALO:])

    def choose(values):
        return jnp.where(first, values[0], values[1]), jnp.where(first, values[1], values[0])

    def swapped(values):
        mine, other = choose(values)
        got = swap(other)

        def stacked(tick=None):
            pair = jnp.stack([jnp.where(first, mine, got), jnp.where(first, got, mine)])
            return pair if tick is None else pair + tick[0, 0]

        return stacked, [got]

    outputs, got_results = swapped(results)
    shards = dp_count * count
    shard = lax.axis_index("dp") * count + place
    low_bit = count.bit_length() - 1
    up_bits = list(range(low_bit, low_bit + dp_count.bit_length() - 1))
    down_bits = up_bits[::-1]
    rows, wide_rows, ff_rows = D // shards, 3 * D // shards, FF // shards
    split = SPLIT if wide_rows > SPLIT else wide_rows // 2
    top, ff_top = rows - rows // 3, ff_rows - ff_rows // 3
    parts_zero = [
        (GRAD_MLP, D, ACT_HIDDEN, FF // 2, [(0, 0, top), (1, top, rows - top)]),
        (GRAD_BRANCH, D, ACT_GATED, HALF, [(0, 0, top), (1, top, rows - top)]),
        (GRAD_PRE, FF, ACT_TWO, HALF, [(2, 0, ff_top), (3, ff_top, ff_rows - ff_top)]),
    ]
    parts_in = [(0, 3 * D, ACT_NORMED, HALF, [(0, 0, split), (1, split, wide_rows - split)])]
    parts_early = [
        (GRAD_MLP, D, ACT_HIDDEN, FF // 2, [(0, 0, rows)]),
        (GRAD_BRANCH, D, ACT_GATED, HALF, [(0, 0, rows)]),
        (GRAD_PRE, FF, ACT_TWO, HALF, [(0, 0, ff_rows)]),
    ]
    whole_tiles = rows % 16 == 0

    def grads_of(name, parts, first_bits):
        if whole_tiles:
            return weight_grad(name, parts, first_bits, shard_len, shards, count)
        return weight_grad_plain(parts, first_bits, shards, shard - place)

    def back(block, grad, wait_out, wait_conv, wait_short, wait_in, through=()):
        x, st, blocks, residual, acts, acts_got, slope, cmix = kept[block]
        grads, d_res, dg, vec_out, d_up_bias, tick, *chunks = out_back(block, shard_len, count)(
            sc, grad, residual, slope, st, tokens[block], mlp_pairs, wait_out
        )
        state = dict(grads=(grads, swap(grads), acts, acts_got), acts=(acts, acts_got))
        *chunks, d_filt, tick = conv_back(block, shard_len, count)(
            sc, filters[block][0], blocks, moved(block, chunks), tables, wait_conv(state, tick)
        )
        state["d_filt"] = d_filt
        d_short, head, vec_short, tick = short_back(block, shard_len, count)(
            sc, st, dg, cmix, tokens[block], moved(block, chunks), wait_short(state, tick)
        )
        d_st, d_x, vec_in, *state["handed"] = in_back(block, shard_len)(
            sc,
            d_short,
            ahead(head),
            x,
            d_res,
            tokens[block],
            in_weight,
            rcv_in,
            wait_in(state, tick),
            through,
        )
        state["grads_in"] = (d_st, swap(d_st), acts, acts_got)
        state["vecs"] = (vec_in, vec_out, vec_short, d_up_bias)
        return d_x, state

    def grads_split(name, state, key, parts, bits, deps):
        values, end = grads_of(name, parts, [group[0] for group in bits])(
            sc, *state[key], deps=deps
        )
        moving = [Reduction([pair], dp_count, count) for pair in zip(values, bits)]
        return moving, [value[0] for value in values], end

    def early_one(state, tick):
        (value,), _ = grads_of("grad_early_1", parts_early, [None])(
            sc, *state["grads"], deps=[tick]
        )
        state["early"] = value
        return [value]

    def net_grads(block, state, tick):
        first_ext, second_ext, d_last, end = net_back(block, chan)(
            state["d_filt"], filters[block][2], lasts[block], decay, pos_ext, window_split, [tick]
        )
        d_net = jnp.concatenate(
            [first_ext[: EMB + 1], second_ext[FILT : FILT + 1], second_ext[:FILT]], axis=0
        )
        state["net"] = (d_last, d_net)
        return [end]

    d_mid, one = back(
        1,
        cot,
        [],
        lambda state, tick: list(got_results),
        lambda state, tick: early_one(state, tick) + net_grads(1, state, tick),
        lambda state, tick: [],
    )

    def cut(value):
        height, width = value.shape
        return value.reshape(height, shards, width // shards).swapaxes(0, 1).reshape(shards, -1)

    def small_grads(block, state, tick):
        vec_in, vec_out, vec_short, d_up_bias = state["vecs"]
        d_last, d_net = state["net"]
        vec_in, vec_out, vec_short, d_up_bias, d_last, d_net = (
            value + tick[0, 0]
            for value in (vec_in, vec_out, vec_short, d_up_bias, d_last, d_net)
        )
        vecs = jnp.concatenate(
            [
                vec_in[0:1],
                vec_out[0:1],
                vec_in[1:2],
                vec_out[2:3],
                vec_out[1:2],
                vec_out[3:4],
                vec_short[12:13],
            ],
            axis=0,
        )
        mixes = jnp.concatenate([vec_in[2:5], vec_short[0:12]], axis=0).reshape(5, 3 * D)
        last_full = lax.dynamic_update_slice_in_dim(
            jnp.zeros((FILT, D), f32), d_last, place * chan, 1
        )
        return (
            jnp.concatenate(
                [
                    cut(vecs),
                    cut(mixes),
                    cut(d_up_bias[0:1]),
                    cut(last_full),
                    jnp.broadcast_to(d_net.reshape(1, -1), (shards, d_net.size)),
                ],
                axis=1,
            )
        )

    moving, moving_in = [], []

    def wait_conv_zero(state, tick):
        got, sent, _ = grads_split(
            "grad_early_0",
            state,
            "grads",
            parts_zero,
            [up_bits, up_bits, down_bits, down_bits],
            [tick],
        )
        moving.extend(got)
        return sent

    def wait_short_zero(state, tick):
        ends = net_grads(0, state, tick)
        got, sent, _ = grads_split(
            "grad_in_1", one, "grads_in", parts_in, [up_bits, down_bits], ends
        )
        moving_in.extend(got)
        return sent + ends + moving[0].arrived() + moving[2].arrived()

    def wait_in_zero(state, tick):
        one["pack"] = small_grads(1, one, tick)
        arrived = moving[1].arrived() + moving[3].arrived() + joined(moving_in).arrived()
        return arrived + [one["pack"]]

    d_start, zero = back(
        0,
        d_mid,
        [],
        wait_conv_zero,
        wait_short_zero,
        wait_in_zero,
        [scatter(one["early"], "dp")],
    )
    in_grads, got_grads = swapped([d_start, d_mid])
    early = joined(moving)
    tick, _ = early.plane(
        "halve_early",
        zero["vecs"][0],
        got_grads + [zero["grads_in"][1]],
    )
    one["seq"] = scatter(zero["handed"][0], "seq")
    one["all"] = one["seq"][0].astype(f32)
    got, _, tick = grads_split(
        "grad_in_0", zero, "grads_in", parts_in, [up_bits, down_bits], [tick]
    )
    late = joined(moving_in + got)
    late_cuts = [0, split, 2 * split, wide_rows + split, 2 * wide_rows]
    pack_tick = relay("after_in", [tick, one["seq"]] + joined(got).arrived())

    packs = [small_grads(0, zero, pack_tick), one["pack"]]
    penalty = (filters[0][1] + 4.0 * filters[1][1]) / (chan * dp_count)
    penalty_high = penalty.astype(bf16)
    penalty_low = (penalty - penalty_high.astype(f32)).astype(bf16)
    mine, other = choose(packs)
    got = swap(other.astype(bf16))
    early_rest, tick = early.rest("merge_early", [tick, mine, got])
    late.plane("halve_late", tick)
    early_zero = scatter(early_rest, "seq")[0].astype(f32)
    pack = (mine + got.astype(f32) + tick[0, 0]).astype(bf16)
    ends = jnp.broadcast_to(jnp.stack([penalty_high, penalty_low])[None], (shards, 2))
    pack = jnp.concatenate([pack, ends], axis=1)
    width = pack.shape[1]
    pack = jnp.pad(pack, ((0, 0), (0, 1024 - width % 1024))).reshape(shards, -1, 128)
    pack = lax.all_to_all(pack, ("dp", "seq"), split_axis=0, concat_axis=0, tiled=True)
    pack = jnp.sum(pack.astype(f32), axis=0).reshape(-1)

    late_rest, last_tick = late.rest("merge_late", [pack])
    late = line_sum(late_rest)
    late = [
        jnp.concatenate([late[late_cuts[k] : late_cuts[k + 1]] for k in (side, side + 2)], axis=0)
        for side in (1, 0)
    ]
    first_a, second_a = FF // D * top + top, (FF // D + 1) * rows
    cuts = [FF // D * top, first_a, first_a + FF // D * (rows - top), second_a]

    def spread_out(value):
        low = value[: cuts[0]].reshape(-1, top, HALF)
        high = value[cuts[1] : cuts[2]].reshape(-1, rows - top, HALF)
        return jnp.concatenate(
            [
                jnp.concatenate([low, high], axis=1).reshape(-1, HALF),
                value[cuts[0] : cuts[1]],
                value[cuts[2] :],
            ],
            axis=0,
        )

    early_zero = spread_out(early_zero)

    def turned(value):
        return value.swapaxes(-1, -2).reshape(1, -1, value.shape[-2])

    full = swapped([early_zero, one["all"]])[0]()
    full_in = swapped(late)[0]()
    down_rows = rows * (FF // D)
    edges = [down_rows, down_rows + rows]
    down = full[:, : edges[0]].reshape(2, FF // D, rows, HALF)
    taken = [0]

    def part(height, cols):
        begin = taken[0]
        taken[0] += height * cols
        return pack[begin : begin + height * cols].reshape(1, height, cols)

    vecs = part(7, rows)
    mixes = part(5, wide_rows)
    d_up_bias = part(1, ff_rows)
    d_last = part(FILT, rows)
    d_net = part(EMB + 2 + FILT, FILT)
    penalty = jnp.sum(part(1, 2))
    return (
        outputs(last_tick)[None, :, None],
        in_grads(last_tick)[None, :, None],
        vecs[:, 0:2],
        vecs[:, 2:6],
        turned(full_in),
        mixes,
        d_net[:, :EMB],
        d_net[:, EMB : EMB + 2],
        d_net[:, EMB + 2 :],
        d_last,
        vecs[:, 6:7],
        turned(full[:, edges[0] : edges[1]]),
        turned(full[:, edges[1] :]),
        d_up_bias,
        turned(down),
        penalty,
    )


def solution(mesh):
    by_section = P("section")
    shard = P("section", None, ("dp", "seq"))
    tokens = P("section", None, "dp", "seq", None)
    return jax.shard_map(
        local,
        mesh=mesh,
        in_specs=(P(None, "dp", "seq", None), P(None, "dp", "seq", None), P(None, "dp", None))
        + (by_section,) * 13,
        out_specs=(tokens, tokens, shard, shard, shard, shard)
        + (by_section,) * 3
        + (shard,) * 6
        + (P(),),
        check_vma=False,
    )
```

```python
import functools

import jax
import jax.numpy as jnp
import ml_dtypes
import numpy as np
from jax import lax
from jax.experimental import pallas as pl
from jax.experimental.pallas import tpu as pltpu
from jax.sharding import PartitionSpec as P

D = 768
FF = 3072
EMB = 33
FILT = 64
SEQ = 1024
NDOCS = 3
LONG_LAG = 32
BLK = 128
NB = SEQ // BLK
FREQ = 2 * BLK
PIECES = NB + NDOCS - 1
HALO = 16
TILE = 48
FF_TILE = 512

eps = 1e-05
highest = lax.Precision.HIGHEST
f32 = jnp.float32
bf16 = jnp.bfloat16
TICK = ((1, 1), f32)
HALF = D // 2
ACT_HIDDEN = 0
ACT_TWO = FF // 2
ACT_GATED = ACT_TWO + HALF
ACT_NORMED = ACT_GATED + HALF
ACT_COLS = ACT_NORMED + HALF
GRAD_PRE = 0
GRAD_MLP = FF
GRAD_BRANCH = FF + D
GRAD_COLS = FF + 2 * D
SPLIT = 80
VMEM_LIMIT = 56 * 1024 * 1024


def split_table(table):
    high = table.astype(ml_dtypes.bfloat16)
    low = (table - high.astype(np.float64)).astype(ml_dtypes.bfloat16)
    return high, low


def ring_table(offsets):
    theta = 2.0 * np.pi * (np.arange(BLK) + 0.5) / FREQ
    angles = offsets[:, None] * theta[None, :]
    return np.concatenate([np.cos(angles), -np.sin(angles)], axis=1)


def block_tables():
    fwd = ring_table(np.arange(BLK, dtype=np.float64))
    fwd_hi, fwd_lo = split_table(fwd)
    inv_hi, inv_lo = split_table(fwd.T / BLK)
    window = ring_table(np.arange(FREQ, dtype=np.float64) - BLK)
    window[0] = 0.0
    return fwd_hi, fwd_lo, inv_hi, inv_lo, window.astype(np.float32)


def position_table():
    positions = np.arange(SEQ, dtype=np.float32)
    band_count = (EMB - 1) // 2
    band_freq = np.float32(0.0001) + np.arange(band_count, dtype=np.float32) * np.float32(
        (band_count - 1 - 0.0001) / (band_count - 1)
    )
    angles = np.float32(2.0 * np.pi / SEQ) * positions[:, None] * band_freq[None, :]
    return np.concatenate(
        [(positions / SEQ)[:, None], np.cos(angles), np.sin(angles)], axis=1
    ).T.astype(np.float32)


def dot(left, right, dims=((1,), (0,))):
    return lax.dot_general(left, right, (dims, ((), ())), preferred_element_type=f32)


NT = ((1,), (1,))
TN = ((0,), (0,))


def norm_stats(values):
    centre = jnp.mean(values, axis=-1, keepdims=True)
    centred = values - centre
    variance = jnp.mean(centred * centred, axis=-1, keepdims=True)
    scale = lax.rsqrt(variance + eps)
    return centred * scale, scale


def norm_back(grad, gain, unit, scale):
    scaled = grad * gain
    return scale * (
        scaled
        - jnp.mean(scaled, axis=-1, keepdims=True)
        - unit * jnp.mean(scaled * unit, axis=-1, keepdims=True)
    )


def col_sum(values):
    return jnp.sum(values, axis=0, keepdims=True)


def place_masks(sc, rows, shard_len):
    pos = sc[1] * shard_len + lax.broadcasted_iota(jnp.int32, (rows, 1), 0)
    starts = pos == sc[2]
    after = pos == sc[2] + 1
    for doc in range(1, NDOCS):
        starts = starts | (pos == sc[2 + doc])
        after = after | (pos == sc[2 + doc] + 1)
    one = jnp.where(starts, 0.0, 1.0)
    two = jnp.where(starts | after, 0.0, 1.0)
    return one, two


def shifted(stream_ext):
    ext = stream_ext.astype(f32)
    return (
        ext[HALO:],
        pltpu.roll(ext, 1, 0)[HALO:],
        pltpu.roll(ext, 2, 0)[HALO:],
    )


def mix_row(p_ref, which, stream):
    row = 6 + 3 * which + stream
    return p_ref[row : row + 1, :]


def short_conv(st_ref, p_ref, stream, masks):
    zero, one, two = shifted(st_ref[:, stream * D : (stream + 1) * D])
    return (
        mix_row(p_ref, 4, stream)
        + mix_row(p_ref, 1, stream) * zero
        + mix_row(p_ref, 2, stream) * (one * masks[0])
        + mix_row(p_ref, 3, stream) * (two * masks[1])
    )


def fetch(own_first, own, rcv, dst, sem):
    @pl.when(own_first)
    def _():
        pltpu.make_async_copy(own, dst, sem).start()

    @pl.when(jnp.logical_not(own_first))
    def _():
        pltpu.make_async_copy(rcv, dst, sem).start()


def rows_at(start, size):
    return pl.ds(pl.multiple_of(start, 16), size)


def fetch_in(own_first, own, rcv, weight, sems):
    def part(ref, stream):
        return ref.at[0, :, pl.ds(stream * D, D)]

    def dest(stream):
        return weight.at[:, pl.ds(stream * D, D)]

    for stream in range(3):
        fetch(own_first, part(own, stream), part(rcv, stream), dest(stream), sems.at[stream])

    def wait(stream):
        pltpu.make_async_copy(part(own, stream), dest(stream), sems.at[stream]).wait()

    return wait


SMEM = pl.BlockSpec(memory_space=pltpu.SMEM)
VMEM = pl.BlockSpec(memory_space=pltpu.VMEM)
ANY = pl.BlockSpec(memory_space=pl.ANY)


def run(body, outs, ins, specs, scratch, name, flops=0, bytes_accessed=0, deps=(), through=()):
    taken, skipped, results = len(ins), len(deps) + len(through), len(outs)

    def wrapped(*refs):
        last = taken + skipped + results
        body(*refs[:taken], *refs[taken + skipped : last], *refs[last + len(through) :])

    return pl.pallas_call(
        wrapped,
        out_shape=[jax.ShapeDtypeStruct(shape, dtype) for shape, dtype in outs]
        + [jax.ShapeDtypeStruct(value.shape, value.dtype) for value in through],
        in_specs=specs + [ANY] * skipped,
        out_specs=[SMEM if out == TICK else VMEM for out in outs] + [ANY] * len(through),
        input_output_aliases={
            taken + len(deps) + index: results + index for index in range(len(through))
        },
        scratch_shapes=scratch,
        compiler_params=pltpu.CompilerParams(vmem_limit_bytes=VMEM_LIMIT),
        cost_estimate=pl.CostEstimate(
            flops=1, bytes_accessed=1, transcendentals=0
        ),
        name=name,
    )(*ins, *deps, *through)


def in_part(block, shard_len, count):
    chan = D // count

    def body(sc, x_ref, halo_ref, p_ref, own, rcv, normed_ref, st_ref, tick_ref, *rest):
        outs = rest[:count]
        tick_ref[0, 0] = 0.0
        weight, sig_t, sems = rest[count:]
        wait = fetch_in(sc[0] == block, own, rcv, weight, sems)
        ext = jnp.concatenate([halo_ref[...].astype(f32), x_ref[...].astype(f32)], axis=0)
        unit, _ = norm_stats(ext)
        normed = (unit * p_ref[0:1, :] + p_ref[2:3, :]).astype(bf16)
        normed_ref[...] = normed[HALO:]
        for stream in range(3):
            wait(stream)
            cols = slice(stream * D, (stream + 1) * D)
            st_ref[:, cols] = (dot(normed, weight[:, cols]) + mix_row(p_ref, 0, stream)).astype(bf16)
        masks = place_masks(sc, shard_len, shard_len)
        signal = short_conv(st_ref, p_ref, 2, masks) * short_conv(st_ref, p_ref, 1, masks)
        sig_t[...] = signal.T.astype(bf16)
        for step in range(count):
            outs[step][...] = sig_t[rows_at((sc[1] ^ step) * chan, chan), :]

    def call(sc, x, halo, params, own, rcv, deps):
        return run(
            body,
            [((shard_len, D), bf16), ((shard_len + HALO, 3 * D), bf16), TICK]
            + [((chan, shard_len), bf16)] * count,
            (sc, x, halo, params, own, rcv),
            [SMEM, VMEM, VMEM, VMEM, ANY, ANY],
            [
                pltpu.VMEM((D, 3 * D), bf16),
                pltpu.VMEM((D, shard_len), bf16),
                pltpu.SemaphoreType.DMA((3,)),
            ],
            f"in_part_{block}",
            2 * shard_len * D * 3 * D,
            D * 3 * D * 2,
            deps,
        )

    return call


def piece_scalars(sc):
    starts = [sc[2 + doc] for doc in range(NDOCS)] + [SEQ]
    lows, offsets = [], [0]
    for doc in range(NDOCS):
        low, high = starts[doc] // BLK, (starts[doc + 1] - 1) // BLK
        lows.append(low)
        offsets.append(offsets[-1] + high - low + 1)
    pieces = []
    for piece in range(PIECES):
        begin, stop, low, first, last = starts[0], starts[1], lows[0], offsets[0], offsets[1]
        for doc in range(1, NDOCS):
            here = piece >= offsets[doc]
            begin = jnp.where(here, starts[doc], begin)
            stop = jnp.where(here, starts[doc + 1], stop)
            low = jnp.where(here, lows[doc], low)
            first = jnp.where(here, offsets[doc], first)
            last = jnp.where(here, offsets[doc + 1], last)
        live = piece < offsets[NDOCS]
        blk = jnp.minimum(low + piece - first, NB - 1)
        begin = jnp.where(live, begin, 0)
        stop = jnp.where(live, stop, 0)
        first = jnp.where(live, first, piece + 1)
        last = jnp.where(live, last, piece)
        pieces.append((blk, begin, stop, first, last))
    return pieces


def piece_mask(piece):
    pos = piece[0] * BLK + lax.broadcasted_iota(jnp.int32, (1, BLK), 1)
    return (pos >= piece[1]) & (pos < piece[2])


def gather_blocks(sc, ins, blocks, per_shard):
    if isinstance(ins, (list, tuple)):
        for step, ref in enumerate(ins):
            source = sc[1] ^ step
            for part in range(per_shard):
                blocks[source * per_shard + part] = ref[:, part * BLK : (part + 1) * BLK]
        return
    for source in range(NB // per_shard):
        for part in range(per_shard):
            blocks[source * per_shard + part] = ins[source, :, part * BLK : (part + 1) * BLK]


def to_freq(pieces, blocks, masked, freq, tables, chan):
    for index, piece in enumerate(pieces):
        keep = jnp.where(piece_mask(piece), 1.0, 0.0)
        masked[index * chan : (index + 1) * chan, :] = (
            blocks[piece[0]].astype(f32) * keep
        ).astype(bf16)
    values = masked[...]
    freq[...] = dot(values, tables[0][...]) + dot(values, tables[1][...])


def from_freq(pieces, freq, out_blocks, tables, chan):
    values = freq[...]
    high = values.astype(bf16)
    low = (values - high.astype(f32)).astype(bf16)
    back = dot(high, tables[2][...]) + dot(low, tables[2][...]) + dot(high, tables[3][...])
    for index, piece in enumerate(pieces):
        mine = back[index * chan : (index + 1) * chan, :]
        before = out_blocks[piece[0]]
        out_blocks[piece[0]] = jnp.where(piece_mask(piece), mine, before)


def scatter_blocks(sc, outs, out_blocks, per_shard):
    if isinstance(outs, (list, tuple)):
        for step, ref in enumerate(outs):
            target = sc[1] ^ step
            for part in range(per_shard):
                ref[:, part * BLK : (part + 1) * BLK] = out_blocks[
                    target * per_shard + part
                ].astype(bf16)
        return
    for target in range(NB // per_shard):
        for part in range(per_shard):
            outs[target, :, part * BLK : (part + 1) * BLK] = out_blocks[
                target * per_shard + part
            ].astype(bf16)


def conv_part(block, shard_len, count):
    chan = D // count
    per_shard = shard_len // BLK
    tiles = chan // TILE

    def body(sc, filt, *rest):
        ins, tables, rest = rest[:count], rest[count : count + 4], rest[count + 4 :]
        outs, blocks, tick_ref = rest[:count], rest[count], rest[count + 1]
        masked, freq, total, out_blocks = rest[count + 2 :]
        tick_ref[0, 0] = 0.0
        gather_blocks(sc, ins, blocks, per_shard)
        pieces = piece_scalars(sc)
        to_freq(pieces, blocks, masked, freq, tables, chan)
        for index, piece in enumerate(pieces):
            for tile in range(tiles):

                def step(other, carry, index=index, piece=piece, tile=tile):
                    sum_re, sum_im = carry
                    rows = rows_at(other * chan + tile * TILE, TILE)
                    sig_re, sig_im = freq[rows, :BLK], freq[rows, BLK:]
                    lag = index - other
                    here = slice(tile * TILE, (tile + 1) * TILE)
                    fil_re, fil_im = filt[lag, here, :BLK], filt[lag, here, BLK:]
                    return (
                        sum_re + fil_re * sig_re - fil_im * sig_im,
                        sum_im + fil_re * sig_im + fil_im * sig_re,
                    )

                zero = jnp.zeros((TILE, BLK), f32)
                sum_re, sum_im = lax.fori_loop(piece[3], index + 1, step, (zero, zero))
                here = slice(index * chan + tile * TILE, index * chan + (tile + 1) * TILE)
                total[here, :BLK] = sum_re
                total[here, BLK:] = sum_im
        out_blocks[...] = jnp.zeros_like(out_blocks)
        from_freq(pieces, total, out_blocks, tables, chan)
        scatter_blocks(sc, outs, out_blocks, per_shard)

    def call(sc, filt, ins, tables, deps):
        return run(
            body,
            [((chan, shard_len), bf16)] * count + [((NB, chan, BLK), bf16), TICK],
            (sc, filt, *ins, *tables),
            [SMEM] + [VMEM] * (count + 5),
            [
                pltpu.VMEM((PIECES * chan, BLK), bf16),
                pltpu.VMEM((PIECES * chan, FREQ), f32),
                pltpu.VMEM((PIECES * chan, FREQ), f32),
                pltpu.VMEM((NB, chan, BLK), f32),
            ],
            f"conv_part_{block}",
            10 * PIECES * chan * BLK * FREQ,
            NB * chan * FREQ * 4,
            deps,
        )

    return call


def conv_back(block, shard_len, count):
    chan = D // count
    per_shard = shard_len // BLK
    tiles = chan // TILE

    def body(sc, filt, blocks, *rest):
        ins, rest = take(rest, block, count)
        tables, rest = rest[:4], rest[4:]
        outs, rest = take(rest, block, count)
        d_filt, tick_ref = rest[:2]
        d_blocks, masked, freq, d_freq, total, out_blocks = rest[2:]
        tick_ref[0, 0] = 0.0
        gather_blocks(sc, ins, d_blocks, per_shard)
        pieces = piece_scalars(sc)
        to_freq(pieces, blocks, masked, freq, tables, chan)
        to_freq(pieces, d_blocks, masked, d_freq, tables, chan)
        d_filt[...] = jnp.zeros_like(d_filt)
        for index, piece in enumerate(pieces):
            for tile in range(tiles):
                rows = slice(index * chan + tile * TILE, index * chan + (tile + 1) * TILE)
                here = slice(tile * TILE, (tile + 1) * TILE)

                def step(other, carry, index=index, here=here, rows=rows, tile=tile):
                    sum_re, sum_im = carry
                    sig_re, sig_im = freq[rows, :BLK], freq[rows, BLK:]
                    there = rows_at(other * chan + tile * TILE, TILE)
                    der_re, der_im = d_freq[there, :BLK], d_freq[there, BLK:]
                    lag = other - index
                    fil_re, fil_im = filt[lag, here, :BLK], filt[lag, here, BLK:]
                    d_filt[lag, here, :BLK] += sig_re * der_re + sig_im * der_im
                    d_filt[lag, here, BLK:] += sig_re * der_im - sig_im * der_re
                    return (
                        sum_re + fil_re * der_re + fil_im * der_im,
                        sum_im + fil_re * der_im - fil_im * der_re,
                    )

                zero = jnp.zeros((TILE, BLK), f32)
                sum_re, sum_im = lax.fori_loop(index, piece[4], step, (zero, zero))
                total[rows, :BLK] = sum_re
                total[rows, BLK:] = sum_im
        out_blocks[...] = jnp.zeros_like(out_blocks)
        from_freq(pieces, total, out_blocks, tables, chan)
        scatter_blocks(sc, outs, out_blocks, per_shard)

    def call(sc, filt, blocks, ins, tables, deps):
        return run(
            body,
            chunk_shapes(block, count, chan, shard_len) + [((NB, chan, FREQ), f32), TICK],
            (sc, filt, blocks, *ins, *tables),
            [SMEM] + [VMEM] * (6 + len(ins)),
            [
                pltpu.VMEM((NB, chan, BLK), bf16),
                pltpu.VMEM((PIECES * chan, BLK), bf16),
                pltpu.VMEM((PIECES * chan, FREQ), f32),
                pltpu.VMEM((PIECES * chan, FREQ), f32),
                pltpu.VMEM((PIECES * chan, FREQ), f32),
                pltpu.VMEM((NB, chan, BLK), f32),
            ],
            f"conv_back_{block}",
            14 * PIECES * chan * BLK * FREQ,
            NB * chan * FREQ * 8,
            deps,
        )

    return call


def chunk_shapes(block, count, chan, shard_len):
    if block == 1:
        return [((chan, shard_len), bf16)] * count
    return [((count, chan, shard_len), bf16)]


def take(refs, block, count):
    if block == 1:
        return list(refs[:count]), refs[count:]
    return refs[0], refs[1:]


def token_major(ins):
    return ins[...].reshape(D, ins.shape[2]).astype(f32).T


def weight_scratch():
    return [
        pltpu.VMEM((D, D), bf16),
        pltpu.VMEM((D, FF), bf16),
        pltpu.VMEM((FF, D), bf16),
        pltpu.SemaphoreType.DMA((1 + 2 * (FF // FF_TILE),)),
    ]


def fetch_mlp(own_first, pairs, dsts, sems, out_first):
    tiles = FF // FF_TILE
    (out_own, out_rcv), (up_own, up_rcv), (down_own, down_rcv) = pairs
    w_out, w_up, w_down = dsts

    def start_out():
        fetch(own_first, out_own.at[0], out_rcv.at[0], w_out, sems.at[0])

    def start_up(tile):
        cols = pl.ds(tile * FF_TILE, FF_TILE)
        fetch(
            own_first,
            up_own.at[0, :, cols],
            up_rcv.at[0, :, cols],
            w_up.at[:, cols],
            sems.at[1 + tile],
        )

    def start_down(tile):
        rows = pl.ds(tile * FF_TILE, FF_TILE)
        fetch(
            own_first,
            down_own.at[0, rows],
            down_rcv.at[0, rows],
            w_down.at[rows],
            sems.at[1 + tiles + tile],
        )

    if out_first:
        start_out()
    for tile in range(tiles):
        if out_first:
            start_up(tile)
            start_down(tile)
        else:
            start_down(tile)
            start_up(tile)
    if not out_first:
        start_out()

    def wait_out():
        pltpu.make_async_copy(out_own.at[0], w_out, sems.at[0]).wait()

    def wait_up(tile):
        cols = pl.ds(pl.multiple_of(tile * FF_TILE, FF_TILE), FF_TILE)
        pltpu.make_async_copy(up_own.at[0, :, cols], w_up.at[:, cols], sems.at[1 + tile]).wait()
        return cols

    def wait_down(tile):
        rows = pl.ds(pl.multiple_of(tile * FF_TILE, FF_TILE), FF_TILE)
        pltpu.make_async_copy(
            down_own.at[0, rows], w_down.at[rows], sems.at[1 + tiles + tile]
        ).wait()
        return rows

    return wait_out, wait_up, wait_down


GELU_SCALE = 0.7978845608028654
GELU_CUBE = 0.044715


def out_part(block, shard_len, count):
    chan = D // count

    def body(sc, x_ref, st_ref, normed_one, p_ref, bias_ref, *rest):
        ins, rest = rest[:count], rest[count:]
        pairs = (rest[0:2], rest[2:4], rest[4:6])
        result_ref, residual_ref, mine_ref, other_ref, slope_ref, cmix_ref = rest[6:12]
        turned, w_out, w_up, w_down, sems, normed_ref, gated_ref, hidden_ref = rest[12:]

        def keep_halves(ref, start, half):
            for side, target in ((sc[0], mine_ref), (1 - sc[0], other_ref)):
                cols = pl.ds(pl.multiple_of(side * half, half), half)
                target[:, start : start + half] = ref[:, cols]

        wait_out, wait_up, wait_down = fetch_mlp(
            sc[0] == block, pairs, (w_out, w_up, w_down), sems, True
        )
        masks = place_masks(sc, shard_len, shard_len)
        for step, ref in enumerate(ins):
            turned[rows_at((sc[1] ^ step) * chan, chan), :] = ref[...]
        conv = turned[...].astype(f32).T
        signal = short_conv(st_ref, p_ref, 2, masks) * short_conv(st_ref, p_ref, 1, masks)
        cmix = conv + p_ref[21:22, :] * signal
        cmix_ref[...] = cmix
        gated = (cmix * short_conv(st_ref, p_ref, 0, masks)).astype(bf16)
        gated_ref[...] = gated
        wait_out()
        residual = x_ref[...].astype(f32) + dot(gated, w_out[...]) + p_ref[3:4, :]
        residual_ref[...] = residual
        unit, _ = norm_stats(residual)
        normed_ref[...] = (unit * p_ref[1:2, :] + p_ref[4:5, :]).astype(bf16)
        result_ref[...] = residual + p_ref[5:6, :]

        @pl.loop(0, FF // FF_TILE)
        def _(tile):
            cols = wait_up(tile)
            pre = dot(normed_ref[...], w_up[:, cols]) + bias_ref[:, cols]
            square = pre * pre
            bent = jnp.tanh(GELU_SCALE * pre * (1.0 + GELU_CUBE * square))
            half = 0.5 * (1.0 + bent)
            slope = half + (0.5 * GELU_SCALE) * pre * (1.0 - bent * bent) * (
                1.0 + 3.0 * GELU_CUBE * square
            )
            hidden = (pre * half).astype(bf16)
            hidden_ref[:, cols] = hidden
            slope_ref[:, cols] = slope.astype(bf16)
            rows = wait_down(tile)
            result_ref[...] += dot(hidden, w_down[rows, :])

        keep_halves(hidden_ref, ACT_HIDDEN, FF // 2)
        keep_halves(normed_ref, ACT_TWO, HALF)
        keep_halves(gated_ref, ACT_GATED, HALF)
        keep_halves(normed_one, ACT_NORMED, HALF)

    def call(sc, x, st, normed, params, up_bias, ins, weights):
        return run(
            body,
            [
                ((shard_len, D), f32),
                ((shard_len, D), f32),
                ((shard_len, ACT_COLS), bf16),
                ((shard_len, ACT_COLS), bf16),
                ((shard_len, FF), bf16),
                ((shard_len, D), f32),
            ],
            (sc, x, st, normed, params, up_bias, *ins, *weights),
            [SMEM] + [VMEM] * (5 + count) + [ANY] * 6,
            [pltpu.VMEM((D, shard_len), bf16)]
            + weight_scratch()
            + [
                pltpu.VMEM((shard_len, D), bf16),
                pltpu.VMEM((shard_len, D), bf16),
                pltpu.VMEM((shard_len, FF), bf16),
            ],
            f"out_part_{block}",
            2 * shard_len * D * (D + 2 * FF),
            D * (D + 2 * FF) * 2,
        )

    return call


def out_back(block, shard_len, count):
    chan = D // count

    def body(sc, grad_ref, residual_ref, slope_ref, st_ref, p_ref, *rest):
        pairs = (rest[0:2], rest[2:4], rest[4:6])
        grads_ref, dres_ref, dg_ref, vec_ref, dub_ref, tick_ref = rest[6:12]
        outs, rest = take(rest[12:], block, count)
        tick_ref[0, 0] = 0.0
        turned, w_out, w_up, w_down, sems, total = rest
        wait_out, wait_up, wait_down = fetch_mlp(
            sc[0] == block, pairs, (w_out, w_up, w_down), sems, False
        )
        grad = grad_ref[...].astype(f32)
        gm = grad.astype(bf16)
        grads_ref[:, GRAD_MLP : GRAD_MLP + D] = gm
        total[...] = jnp.zeros_like(total)

        @pl.loop(0, FF // FF_TILE)
        def _(tile):
            rows = wait_down(tile)
            d_hidden = dot(grads_ref[:, GRAD_MLP : GRAD_MLP + D], w_down[rows, :], NT)
            d_pre = (d_hidden * slope_ref[:, rows].astype(f32)).astype(bf16)
            grads_ref[:, rows] = d_pre
            dub_ref[:, rows] = jnp.broadcast_to(col_sum(d_pre.astype(f32)), (8, FF_TILE))
            cols = wait_up(tile)
            total[...] += dot(d_pre, w_up[:, cols], NT)

        d_normed = total[...]
        unit, scale = norm_stats(residual_ref[...])
        d_res = grad + norm_back(d_normed, p_ref[1:2, :], unit, scale)
        dres_ref[...] = d_res
        gb = d_res.astype(bf16)
        grads_ref[:, GRAD_BRANCH : GRAD_BRANCH + D] = gb
        wait_out()
        dg = dot(gb, w_out[...], NT).astype(bf16)
        dg_ref[...] = dg
        masks = place_masks(sc, shard_len, shard_len)
        d_conv = dg.astype(f32) * short_conv(st_ref, p_ref, 0, masks)
        turned[...] = d_conv.T.astype(bf16)
        for step in range(count):
            if isinstance(outs, list):
                outs[step][...] = turned[rows_at((sc[1] ^ step) * chan, chan), :]
            else:
                outs[step] = turned[step * chan : (step + 1) * chan, :]
        vec_ref[...] = jnp.concatenate(
            [
                col_sum(d_normed * unit),
                col_sum(d_normed),
                col_sum(gb.astype(f32)),
                col_sum(gm.astype(f32)),
                jnp.zeros((4, D), f32),
            ],
            axis=0,
        )

    def call(sc, grad, residual, slope, st, params, weights, deps):
        return run(
            body,
            [
                ((shard_len, GRAD_COLS), bf16),
                ((shard_len, D), f32),
                ((shard_len, D), bf16),
                ((8, D), f32),
                ((8, FF), f32),
                TICK,
            ]
            + chunk_shapes(block, count, chan, shard_len),
            (sc, grad, residual, slope, st, params, *weights),
            [SMEM] + [VMEM] * 5 + [ANY] * 6,
            [pltpu.VMEM((D, shard_len), bf16)]
            + weight_scratch()
            + [pltpu.VMEM((shard_len, D), f32)],
            f"out_back_{block}",
            2 * shard_len * D * (D + 2 * FF),
            D * (D + 2 * FF) * 2,
            deps,
        )

    return call


def short_back(block, shard_len, count):
    chan = D // count

    def body(sc, st_ref, dg_ref, cmix_ref, p_ref, *rest):
        ins, rest = take(rest, block, count)
        ds_ref, head_ref, vec_ref, tick_ref, turned = rest
        tick_ref[0, 0] = 0.0
        masks = place_masks(sc, shard_len, shard_len)
        if isinstance(ins, list):
            for step, ref in enumerate(ins):
                turned[rows_at((sc[1] ^ step) * chan, chan), :] = ref[...]
            d_signal = turned[...].astype(f32).T
        else:
            d_signal = token_major(ins)
        dg = dg_ref[...].astype(f32)
        d_conv = dg * short_conv(st_ref, p_ref, 0, masks)
        inner = short_conv(st_ref, p_ref, 1, masks)
        value = short_conv(st_ref, p_ref, 2, masks)
        d_signal = d_signal + p_ref[21:22, :] * d_conv
        rows = [None] * 16
        rows[12] = col_sum(d_conv * value * inner)
        for stream, d_short in enumerate((dg * cmix_ref[...], d_signal * value, d_signal * inner)):
            cols = slice(stream * D, (stream + 1) * D)
            ds_ref[:, cols] = d_short
            head_ref[:, cols] = d_short[:HALO]
            zero, one, two = shifted(st_ref[:, cols])
            rows[stream] = col_sum(d_short * zero)
            rows[3 + stream] = col_sum(d_short * (one * masks[0]))
            rows[6 + stream] = col_sum(d_short * (two * masks[1]))
            rows[9 + stream] = col_sum(d_short)
        for index in range(13, 16):
            rows[index] = jnp.zeros((1, D), f32)
        vec_ref[...] = jnp.concatenate(rows, axis=0)

    def call(sc, st, dg, cmix, params, ins, deps):
        return run(
            body,
            [((shard_len, 3 * D), f32), ((HALO, 3 * D), f32), ((16, D), f32), TICK],
            (sc, st, dg, cmix, params, *ins),
            [SMEM] + [VMEM] * (4 + len(ins)),
            [pltpu.VMEM((D, shard_len), bf16)],
            f"short_back_{block}",
            40 * shard_len * D,
            shard_len * D * 20,
            deps,
        )

    return call


def in_back(block, shard_len):
    def body(sc, ds_ref, halo_ref, x_ref, dres_ref, p_ref, own, rcv, dst_ref, dx_ref, vec_ref, weight, sems):
        wait = fetch_in(sc[0] == block, own, rcv, weight, sems)
        long = shard_len + HALO
        one, two = place_masks(sc, long, shard_len)
        d_normed = jnp.zeros((shard_len, D), f32)
        rows = []
        for stream in range(3):
            cols = slice(stream * D, (stream + 1) * D)
            ext = jnp.concatenate([ds_ref[:, cols], halo_ref[:, cols]], axis=0)
            d_stream = (
                mix_row(p_ref, 1, stream) * ext[:shard_len]
                + mix_row(p_ref, 2, stream) * pltpu.roll(ext * one, long - 1, 0)[:shard_len]
                + mix_row(p_ref, 3, stream) * pltpu.roll(ext * two, long - 2, 0)[:shard_len]
            ).astype(bf16)
            dst_ref[:, cols] = d_stream
            rows.append(col_sum(d_stream.astype(f32)))
            wait(stream)
            d_normed = d_normed + dot(d_stream, weight[:, cols], NT)
        unit, scale = norm_stats(x_ref[...].astype(f32))
        dx_ref[...] = dres_ref[...] + norm_back(d_normed, p_ref[0:1, :], unit, scale)
        vec_ref[...] = jnp.concatenate(
            [col_sum(d_normed * unit), col_sum(d_normed)] + rows + [jnp.zeros((3, D), f32)], axis=0
        )

    def call(sc, d_short, halo, x, d_res, params, own, rcv, deps, through):
        return run(
            body,
            [((shard_len, 3 * D), bf16), ((shard_len, D), f32), ((8, D), f32)],
            (sc, d_short, halo, x, d_res, params, own, rcv),
            [SMEM] + [VMEM] * 5 + [ANY] * 2,
            [pltpu.VMEM((D, 3 * D), bf16), pltpu.SemaphoreType.DMA((3,))],
            f"in_back_{block}",
            2 * shard_len * D * 3 * D,
            D * 3 * D * 2,
            deps,
            through,
        )

    return call


def weight_grad(name, parts, first_bits, shard_len, shards, count):
    groups = len(first_bits)
    sizes = [0] * groups
    for _, rows, _, cols, splits in parts:
        for group, _, size in splits:
            sizes[group] += size * (cols // HALF)
    shapes, firsts = [], []
    for size, bit in zip(sizes, first_bits):
        firsts.append(len(shapes))
        shapes += [(shards, size, HALF)] if bit is None else [(shards // 2, size, HALF)] * 2

    def body(sc, g_own, g_rcv, a_own, a_rcv, *outs):
        outs[-1][0, 0] = 0.0
        me = sc[2 + NDOCS] * count
        bases = [0] * groups
        for g_start, rows, a_start, cols, splits in parts:
            block = rows // shards
            chunk = 8 * block if block % 32 else 4 * block
            acts = slice(a_start, a_start + cols)
            starts = list(bases)

            @pl.loop(0, rows // chunk)
            def _(step, starts=starts, g_start=g_start, chunk=chunk, block=block, acts=acts, cols=cols, splits=splits):
                here = pl.ds(pl.multiple_of(g_start + step * chunk, 128), chunk)
                full = dot(g_own[:, here], a_own[:, acts], TN) + dot(g_rcv[:, here], a_rcv[:, acts], TN)
                for index in range(chunk // block):
                    device = step * (chunk // block) + index
                    for group, begin, size in splits:
                        bit = first_bits[group]
                        if bit is None:
                            slot = device
                        else:
                            away = device ^ me
                            low = away & ((1 << bit) - 1)
                            slot = ((away >> (bit + 1)) << bit) | low
                            sent = (away >> bit) & 1

                        def store(ref, group=group, begin=begin, size=size, slot=slot, index=index):
                            for part in range(cols // HALF):
                                top = starts[group] + part * size
                                ref[slot, top : top + size, :] = full[
                                    index * block + begin : index * block + begin + size,
                                    part * HALF : (part + 1) * HALF,
                                ].astype(bf16)

                        first = firsts[group]
                        if bit is None:
                            store(outs[first])
                        else:
                            pl.when(sent == 1)(functools.partial(store, outs[first]))
                            pl.when(sent == 0)(functools.partial(store, outs[first + 1]))

            for group, _, size in splits:
                bases[group] += size * (cols // HALF)

    def call(sc, *ins, deps=()):
        flops = sum(4 * shard_len * rows * cols for _, rows, _, cols, _ in parts)
        outs = run(
            body,
            [(shape, bf16) for shape in shapes] + [TICK],
            (sc, *ins),
            [SMEM] + [VMEM] * 4,
            [],
            name,
            flops,
            flops // 256,
            deps,
        )
        return [
            outs[first] if bit is None else outs[first : first + 2]
            for first, bit in zip(firsts, first_bits)
        ], outs[-1]

    return call


def weight_grad_plain(parts, first_bits, shards, me):
    groups = len(first_bits)

    def call(_, g_own, g_rcv, a_own, a_rcv, deps=()):
        gathered = [[] for _ in range(groups)]
        for g_start, rows, a_start, cols, splits in parts:
            block = rows // shards
            full = sum(
                jnp.einsum(
                    "tn,tk->nk",
                    g[:, g_start : g_start + rows],
                    a[:, a_start : a_start + cols],
                    preferred_element_type=f32,
                )
                for g, a in ((g_own, a_own), (g_rcv, a_rcv))
            ).astype(bf16)
            full = full.reshape(shards, block, cols // HALF, HALF).transpose(0, 2, 1, 3)
            for group, begin, size in splits:
                piece = full[:, :, begin : begin + size]
                gathered[group].append(piece.reshape(shards, -1, HALF))
        outs = []
        for group in range(groups):
            whole = jnp.concatenate(gathered[group], axis=1)
            bit = first_bits[group]
            if bit is None:
                outs.append(whole)
                continue
            whole = whole[jnp.arange(shards, dtype=jnp.int32) ^ me]
            whole = whole.reshape((shards >> (bit + 1), 2, 1 << bit) + whole.shape[1:])
            outs.append(
                [whole[:, side].reshape((shards // 2,) + whole.shape[3:]) for side in (1, 0)]
            )
        return outs, jnp.zeros((1, 1), f32)

    return call


def halving(name, groups, count):
    def call(deps, through=None):
        ins, outs, in_specs, out_specs, lists = [], [], [], [], []
        alias = {}
        steps = None
        for group in groups:
            height, sizes = sum(kept.shape[1] for kept, _, _ in group), []
            for kept, got, spot in group:
                blocks, rows, cols = kept.shape
                inner = count << spot
                outer = blocks // (2 * inner)
                steps = outer * inner
                ins += [v.reshape(outer, 2, inner, rows, cols) for v in (kept, got)]
                in_specs += [
                    pl.BlockSpec(
                        (1, 2, 1, rows, cols), lambda i, inner=inner: (i // inner, 0, i % inner, 0, 0)
                    )
                ] * 2
                sizes.append(rows)
            outs += [jax.ShapeDtypeStruct((outer, inner, height, cols), bf16)] * 2
            out_specs += [
                pl.BlockSpec(
                    (1, 1, height, cols), lambda i, inner=inner: (i // inner, i % inner, 0, 0)
                )
            ] * 2
            lists.append(sizes)
        taken = len(ins)
        if through is not None:
            alias = {taken + len(deps): len(outs) + 1}
            deps = [*deps, through]

        def body(*refs):
            out_refs = refs[taken + len(deps) :]
            out_refs[2 * len(groups)][0, 0] = 0.0
            index = 0
            for group, sizes in enumerate(lists):
                begin = 0
                for size in sizes:
                    kept, got = refs[index : index + 2]
                    index += 2
                    for side, ref in ((1, out_refs[2 * group]), (0, out_refs[2 * group + 1])):
                        ref[0, 0, begin : begin + size, :] = (
                            kept[0, side, 0].astype(f32) + got[0, side, 0].astype(f32)
                        ).astype(bf16)
                    begin += size

        values = pl.pallas_call(
            body,
            grid=(steps,),
            out_shape=outs
            + [jax.ShapeDtypeStruct(*TICK)]
            + [jax.ShapeDtypeStruct(through.shape, through.dtype) for _ in alias],
            in_specs=in_specs + [ANY] * len(deps),
            out_specs=out_specs + [SMEM] + [ANY] * len(alias),
            input_output_aliases=alias,
            compiler_params=pltpu.CompilerParams(vmem_limit_bytes=VMEM_LIMIT),
            cost_estimate=pl.CostEstimate(flops=1, bytes_accessed=1, transcendentals=0),
            name=name,
        )(*ins, *deps)
        flat = [v.reshape((-1,) + v.shape[2:]) for v in values[: 2 * len(groups)]]
        pairs_out = [flat[2 * group : 2 * group + 2] for group in range(len(groups))]
        return pairs_out, values[2 * len(groups)], values[-1] if alias else None

    return call


def relay(name, deps):
    def body(tick_ref):
        tick_ref[0, 0] = 0.0

    return run(body, [TICK], [], [], [], name, deps=deps)[0]


def merging(name, sizes, count):
    def call(terms, deps):
        taken, rows = 2 * len(terms), sum(sizes)

        def body(*refs):
            out_ref, tick_ref = refs[taken + len(deps) :]
            tick_ref[0, 0] = 0.0
            begin = 0
            for group, size in enumerate(sizes):
                kept, got = refs[2 * group : 2 * group + 2]
                out_ref[0, begin : begin + size, :] = (
                    kept[0].astype(f32) + got[0].astype(f32)
                ).astype(bf16)
                begin += size

        def block(size):
            return pl.BlockSpec((1, size, HALF), lambda i: (i, 0, 0))

        return pl.pallas_call(
            body,
            grid=(count,),
            out_shape=[
                jax.ShapeDtypeStruct((count, rows, HALF), bf16),
                jax.ShapeDtypeStruct(*TICK),
            ],
            in_specs=[block(size) for size in sizes for _ in range(2)] + [ANY] * len(deps),
            out_specs=[block(rows), SMEM],
            compiler_params=pltpu.CompilerParams(vmem_limit_bytes=VMEM_LIMIT),
            cost_estimate=pl.CostEstimate(flops=1, bytes_accessed=1, transcendentals=0),
            name=name,
        )(*[value for kept, got, _ in terms for value in (kept, got)], *deps)

    return call


def pairs(count, step):
    return [(index, index ^ step) for index in range(count)]


def swap(value):
    return lax.ppermute(value, "section", pairs(2, 1))


def exchange_apart(chunks):
    count = len(chunks)
    return [chunks[0]] + [
        lax.ppermute(chunks[step], "seq", pairs(count, step)) for step in range(1, count)
    ]


def moved(block, chunks):
    return exchange_apart(chunks) if block == 1 else [exchange(chunks[0])]


def exchange(chunks):
    return lax.all_to_all(chunks, "seq", split_axis=0, concat_axis=0, tiled=True)


class Reduction:
    def __init__(self, groups, dp_count, count):
        self.sizes = (dp_count, count)
        self.terms = []
        for (sent, kept), bits in groups:
            self.terms.append((kept, self.over_dp(sent, bits[0]), list(bits[1:])))

    def arrived(self):
        return [got for _, got, _ in self.terms]

    def over_dp(self, value, bit):
        return lax.ppermute(value, "dp", pairs(self.sizes[0], (1 << bit) // self.sizes[1]))

    def plane(self, name, tick, deps=(), through=None):
        handed = through
        for turn in range(len(self.terms[0][2])):
            orders, groups = [], []
            for kept, got, left in self.terms:
                if left not in orders:
                    orders.append(left)
                    groups.append([])
                spot = sum(1 for other in left[1:] if other < left[0])
                groups[orders.index(left)].append((kept, got, spot))
            values, tick, passed = halving(f"{name}_{turn}", groups, self.sizes[1])(
                [tick, *deps], None if turn else through
            )
            handed = handed if passed is None else passed
            self.terms = [
                (keep, self.over_dp(send, left[0]), left[1:])
                for (send, keep), left in zip(values, orders)
            ]
        return tick, handed

    def rest(self, name, deps):
        sizes = [kept.shape[1] for kept, _, _ in self.terms]
        if any(size % 16 for size in sizes):
            parts = [
                (kept.astype(f32) + got.astype(f32)).astype(bf16) for kept, got, _ in self.terms
            ]
            return jnp.concatenate(parts, axis=1), jnp.zeros((1, 1), f32)
        return merging(name, sizes, self.sizes[1])(self.terms, deps)


def joined(parts):
    whole = Reduction([], *parts[0].sizes)
    for part in parts:
        whole.terms += part.terms
    return whole


def line_sum(values):
    return jnp.sum(exchange(values).astype(f32), axis=0)


def scatter(value, axis):
    blocks, rows, cols = value.shape
    value = value.reshape(blocks * rows, cols)
    return lax.psum_scatter(value, axis, scatter_dimension=0, tiled=True).reshape(-1, rows, cols)


def mat(spec, left, right):
    return jnp.einsum(spec, left, right, precision=highest, preferred_element_type=f32)


def filter_state(net, last, decay, pos, window):
    first_w, inner_b, second_w = net[:EMB], net[EMB : EMB + 2], net[EMB + 2 :]
    pre_a = mat("ef,en->fn", first_w, pos) + inner_b[0][:, None]
    hid_a = jnp.sin(pre_a)
    pre_b = mat("gf,gn->fn", second_w, hid_a) + inner_b[1][:, None]
    hid_b = jnp.sin(pre_b)
    taps = mat("fc,fn->cn", last, hid_b) * decay
    blocks = taps.reshape(taps.shape[0], NB, BLK)
    filt = mat("cmn,nk->mck", blocks, window[BLK:])
    behind = mat("cmn,nk->mck", blocks[:, :-1], window[:BLK])
    filt = filt + jnp.pad(behind, ((1, 0), (0, 0), (0, 0)))
    energy = taps * taps
    share = jnp.sum(jnp.sum(energy[:, LONG_LAG:], axis=1) / (jnp.sum(energy, axis=1) + 1e-06))
    return filt, share, (pre_a, hid_a, pre_b, hid_b, second_w)


def split(value):
    high = value.astype(bf16)
    return high, (value - high.astype(f32)).astype(bf16)


def dot_split(left, right, dims):
    total = dot(left[0], right[0], dims)
    if left[1] is not None:
        total = total + dot(left[1], right[0], dims)
    if right[1] is not None:
        total = total + dot(left[0], right[1], dims)
    return total


NN = ((1,), (0,))
POS_ROWS = 40


def net_back(block, chan):
    def body(d_filt, pre_a, hid_a, pre_b, hid_b, second, last, decay, pos, win_hi, win_lo, first_ref, second_ref, last_ref, tick_ref, taps):
        tick_ref[0, 0] = 0.0
        behind = (win_hi[:BLK, :], win_lo[:BLK, :])
        ahead = (win_hi[BLK:, :], win_lo[BLK:, :])
        for m in range(NB):
            d_block = dot_split(split(d_filt[m]), ahead, NT)
            if m + 1 < NB:
                d_block = d_block + dot_split(split(d_filt[m + 1]), behind, NT)
            cols = slice(m * BLK, (m + 1) * BLK)
            taps[:, cols] = d_block * (decay[:, cols] * (1.0 / BLK))
        d_out = split(taps[...])
        ones = jnp.ones((8, SEQ), f32)
        last_ref[...] = dot_split(split(hid_b[...]), d_out, NT)
        d_b = split(dot_split((last[...].astype(bf16), None), d_out, NN) * jnp.cos(pre_b[...]))
        second_ref[...] = dot_split(
            split(jnp.concatenate([hid_a[...], ones], axis=0)), d_b, NT
        )
        d_a = split(dot_split((second[...].astype(bf16), None), d_b, NN) * jnp.cos(pre_a[...]))
        first_ref[...] = dot_split(split(pos[...]), d_a, NT)

    def call(d_filt, state, last, decay, pos, window, deps):
        return run(
            body,
            [((POS_ROWS, FILT), f32), ((FILT + 8, FILT), f32), ((FILT, chan), f32), TICK],
            (d_filt, *state, last, decay, pos, *window),
            [VMEM] * 11,
            [pltpu.VMEM((chan, SEQ), f32)],
            f"net_back_{block}",
            0,
            0,
            deps,
        )

    return call


def local(
    layer_input,
    out_cot,
    doc_lengths,
    norm_gains,
    biases,
    in_weight,
    mix_vecs,
    filt_first,
    filt_inner_bias,
    filt_second,
    filt_last,
    filt_skip,
    out_weight,
    up_weight,
    up_bias,
    down_weight,
):
    count = lax.axis_size("seq")
    dp_count = lax.axis_size("dp")
    section = lax.axis_index("section")
    place = lax.axis_index("seq")
    first = section == 0
    shard_len = layer_input.shape[2]
    chan = D // count
    fwd_hi, fwd_lo, inv_hi, inv_lo, window = block_tables()
    tables = tuple(jnp.asarray(t) for t in (fwd_hi, fwd_lo, inv_hi, inv_lo))
    window = jnp.asarray(window)
    pos = jnp.asarray(position_table())
    pos_ext = jnp.asarray(
        np.concatenate(
            [position_table(), np.ones((1, SEQ)), np.zeros((POS_ROWS - EMB - 1, SEQ))]
        ).astype(np.float32)
    )
    window_split = tuple(jnp.asarray(part) for part in split_table(block_tables()[4].astype(np.float64)))

    def own_micro(value):
        return lax.dynamic_index_in_dim(value, section, 0, keepdims=False)[0]

    x_zero = own_micro(layer_input)
    cot = own_micro(out_cot)
    lengths = own_micro(doc_lengths)
    starts = jnp.cumsum(lengths) - lengths
    sc = jnp.concatenate(
        [jnp.stack([section, place]), starts, lax.axis_index("dp")[None]]
    ).astype(jnp.int32)

    def behind(rows):
        return lax.ppermute(rows, "seq", [(index, index + 1) for index in range(count - 1)])

    def ahead(rows):
        return lax.ppermute(rows, "seq", [(index + 1, index) for index in range(count - 1)])

    halo = behind(x_zero[-HALO:])
    small = jnp.concatenate(
        [
            norm_gains[0],
            biases[0],
            mix_vecs[0].reshape(15, D),
            filt_skip[0],
            up_bias[0].reshape(4, D),
            filt_last[0],
        ],
        axis=0,
    )
    net = jnp.concatenate([filt_first[0], filt_inner_bias[0], filt_second[0]], axis=0)
    small_rcv, net_rcv = swap(small), swap(net)
    rcv_in, rcv_out, rcv_up, rcv_down = (
        swap(in_weight),
        swap(out_weight),
        swap(up_weight),
        swap(down_weight),
    )
    mlp_pairs = (out_weight, rcv_out, up_weight, rcv_up, down_weight, rcv_down)
    params, nets = [], []
    for block in range(2):
        mine = section == block
        params.append(jnp.where(mine, small, small_rcv).astype(f32))
        nets.append(jnp.where(mine, net, net_rcv).astype(f32))
    tokens = [p[:24] for p in params]
    up_biases = [p[22:26].reshape(1, FF) for p in params]
    lasts = [lax.dynamic_slice_in_dim(p[26:90], place * chan, chan, 1) for p in params]
    chan_ids = (jnp.arange(chan, dtype=jnp.int32) + place * chan).astype(f32)
    times = jnp.arange(SEQ, dtype=f32) / SEQ
    decay = jnp.exp(-(3.0 + 12.0 * chan_ids / (D - 1))[:, None] * times[None, :])

    x = x_zero
    kept = []
    results = []
    filters = []
    for block in range(2):
        normed, st, tick, *chunks = in_part(block, shard_len, count)(
            sc, x, halo, tokens[block], in_weight, rcv_in, []
        )
        if block == 0:
            filters.append(filter_state(nets[0] + tick[0, 0], lasts[0], decay, pos, window))
        *chunks, blocks, tick = conv_part(block, shard_len, count)(
            sc, filters[block][0], exchange_apart(chunks), tables, [k[5] for k in kept]
        )
        if block == 0:
            filters.append(filter_state(nets[1] + tick[0, 0], lasts[1], decay, pos, window))
        result, residual, acts, acts_other, slope, cmix = out_part(block, shard_len, count)(
            sc, x, st, normed, tokens[block], up_biases[block], exchange_apart(chunks), mlp_pairs
        )
        kept.append((x, st, blocks, residual, acts, swap(acts_other), slope, cmix))
        results.append(result)
        x = result
        if block == 0:
            halo = behind(result[-HALO:])

    def choose(values):
        return jnp.where(first, values[0], values[1]), jnp.where(first, values[1], values[0])

    def swapped(values):
        mine, other = choose(values)
        got = swap(other)

        def stacked(tick=None):
            pair = jnp.stack([jnp.where(first, mine, got), jnp.where(first, got, mine)])
            return pair if tick is None else pair + tick[0, 0]

        return stacked, [got]

    outputs, got_results = swapped(results)
    shards = dp_count * count
    shard = lax.axis_index("dp") * count + place
    low_bit = count.bit_length() - 1
    up_bits = list(range(low_bit, low_bit + dp_count.bit_length() - 1))
    down_bits = up_bits[::-1]
    rows, wide_rows, ff_rows = D // shards, 3 * D // shards, FF // shards
    split = SPLIT if wide_rows > SPLIT else wide_rows // 2
    top, ff_top = rows - rows // 3, ff_rows - ff_rows // 3
    parts_zero = [
        (GRAD_MLP, D, ACT_HIDDEN, FF // 2, [(0, 0, top), (1, top, rows - top)]),
        (GRAD_BRANCH, D, ACT_GATED, HALF, [(0, 0, top), (1, top, rows - top)]),
        (GRAD_PRE, FF, ACT_TWO, HALF, [(2, 0, ff_top), (3, ff_top, ff_rows - ff_top)]),
    ]
    parts_in = [(0, 3 * D, ACT_NORMED, HALF, [(0, 0, split), (1, split, wide_rows - split)])]
    parts_early = [
        (GRAD_MLP, D, ACT_HIDDEN, FF // 2, [(0, 0, rows)]),
        (GRAD_BRANCH, D, ACT_GATED, HALF, [(0, 0, rows)]),
        (GRAD_PRE, FF, ACT_TWO, HALF, [(0, 0, ff_rows)]),
    ]
    whole_tiles = rows % 16 == 0

    def grads_of(name, parts, first_bits):
        if whole_tiles:
            return weight_grad(name, parts, first_bits, shard_len, shards, count)
        return weight_grad_plain(parts, first_bits, shards, shard - place)

    def back(block, grad, wait_out, wait_conv, wait_short, wait_in, through=()):
        x, st, blocks, residual, acts, acts_got, slope, cmix = kept[block]
        grads, d_res, dg, vec_out, d_up_bias, tick, *chunks = out_back(block, shard_len, count)(
            sc, grad, residual, slope, st, tokens[block], mlp_pairs, wait_out
        )
        state = dict(grads=(grads, swap(grads), acts, acts_got), acts=(acts, acts_got))
        *chunks, d_filt, tick = conv_back(block, shard_len, count)(
            sc, filters[block][0], blocks, moved(block, chunks), tables, wait_conv(state, tick)
        )
        state["d_filt"] = d_filt
        state["moved"] = moved(block, chunks)
        d_short, head, vec_short, tick = short_back(block, shard_len, count)(
            sc, st, dg, cmix, tokens[block], state["moved"], wait_short(state, tick)
        )
        d_st, d_x, vec_in, *state["handed"] = in_back(block, shard_len)(
            sc,
            d_short,
            ahead(head),
            x,
            d_res,
            tokens[block],
            in_weight,
            rcv_in,
            wait_in(state, tick),
            through,
        )
        state["grads_in"] = (d_st, swap(d_st), acts, acts_got)
        state["vecs"] = (vec_in, vec_out, vec_short, d_up_bias)
        return d_x, state

    def grads_split(name, state, key, parts, bits, deps):
        values, end = grads_of(name, parts, [group[0] for group in bits])(
            sc, *state[key], deps=deps
        )
        moving = [Reduction([pair], dp_count, count) for pair in zip(values, bits)]
        return moving, [value[0] for value in values], end

    def early_one(state, tick):
        (value,), _ = grads_of("grad_early_1", parts_early, [None])(
            sc, *state["grads"], deps=net_grads(1, state, tick) + state["moved"][1:]
        )
        state["early"] = value
        return [value]

    def net_grads(block, state, tick):
        first_ext, second_ext, d_last, end = net_back(block, chan)(
            state["d_filt"], filters[block][2], lasts[block], decay, pos_ext, window_split, [tick]
        )
        d_net = jnp.concatenate(
            [first_ext[: EMB + 1], second_ext[FILT : FILT + 1], second_ext[:FILT]], axis=0
        )
        state["net"] = (d_last, d_net)
        return [end]

    d_mid, one = back(
        1,
        cot,
        [],
        lambda state, tick: list(got_results),
        early_one,
        lambda state, tick: [],
    )

    def cut(value):
        height, width = value.shape
        return value.reshape(height, shards, width // shards).swapaxes(0, 1).reshape(shards, -1)

    def small_grads(block, state, tick):
        vec_in, vec_out, vec_short, d_up_bias = state["vecs"]
        d_last, d_net = state["net"]
        vec_in, vec_out, vec_short, d_up_bias, d_last, d_net = (
            value + tick[0, 0]
            for value in (vec_in, vec_out, vec_short, d_up_bias, d_last, d_net)
        )
        vecs = jnp.concatenate(
            [
                vec_in[0:1],
                vec_out[0:1],
                vec_in[1:2],
                vec_out[2:3],
                vec_out[1:2],
                vec_out[3:4],
                vec_short[12:13],
            ],
            axis=0,
        )
        mixes = jnp.concatenate([vec_in[2:5], vec_short[0:12]], axis=0).reshape(5, 3 * D)
        last_full = lax.dynamic_update_slice_in_dim(
            jnp.zeros((FILT, D), f32), d_last, place * chan, 1
        )
        return (
            jnp.concatenate(
                [
                    cut(vecs),
                    cut(mixes),
                    cut(d_up_bias[0:1]),
                    cut(last_full),
                    jnp.broadcast_to(d_net.reshape(1, -1), (shards, d_net.size)),
                ],
                axis=1,
            )
        )

    moving, moving_in = [], []

    def wait_conv_zero(state, tick):
        got, sent, _ = grads_split(
            "grad_early_0",
            state,
            "grads",
            parts_zero,
            [up_bits, up_bits, down_bits, down_bits],
            [tick],
        )
        moving.extend(got)
        return sent

    def wait_short_zero(state, tick):
        ends = net_grads(0, state, tick)
        got, sent, _ = grads_split(
            "grad_in_1", one, "grads_in", parts_in, [up_bits, down_bits], ends
        )
        moving_in.extend(got)
        return sent + ends + moving[0].arrived() + moving[2].arrived()

    def wait_in_zero(state, tick):
        one["pack"] = small_grads(1, one, tick)
        arrived = moving[1].arrived() + moving[3].arrived() + joined(moving_in).arrived()
        return arrived + [one["pack"]]

    d_start, zero = back(
        0,
        d_mid,
        [],
        wait_conv_zero,
        wait_short_zero,
        wait_in_zero,
        [scatter(one["early"], "dp")],
    )
    in_grads, got_grads = swapped([d_start, d_mid])
    early = joined(moving)
    tick, _ = early.plane(
        "halve_early",
        zero["vecs"][0],
        got_grads + [zero["grads_in"][1]],
    )
    one["seq"] = scatter(zero["handed"][0], "seq")
    one["all"] = one["seq"][0].astype(f32)
    got, _, tick = grads_split(
        "grad_in_0", zero, "grads_in", parts_in, [up_bits, down_bits], [tick]
    )
    late = joined(moving_in + got)
    late_cuts = [0, split, 2 * split, wide_rows + split, 2 * wide_rows]
    pack_tick = relay("after_in", [tick, one["seq"]] + joined(got).arrived())

    packs = [small_grads(0, zero, pack_tick), one["pack"]]
    penalty = (filters[0][1] + 4.0 * filters[1][1]) / (chan * dp_count)
    penalty_high = penalty.astype(bf16)
    penalty_low = (penalty - penalty_high.astype(f32)).astype(bf16)
    mine, other = choose(packs)
    got = swap(other.astype(bf16))
    early_rest, tick = early.rest("merge_early", [tick, mine, got])
    late.plane("halve_late", tick)
    early_zero = scatter(early_rest, "seq")[0].astype(f32)
    pack = (mine + got.astype(f32) + tick[0, 0]).astype(bf16)
    ends = jnp.broadcast_to(jnp.stack([penalty_high, penalty_low])[None], (shards, 2))
    pack = jnp.concatenate([pack, ends], axis=1)
    width = pack.shape[1]
    pack = jnp.pad(pack, ((0, 0), (0, 1024 - width % 1024))).reshape(shards, -1, 128)
    pack = lax.all_to_all(pack, ("dp", "seq"), split_axis=0, concat_axis=0, tiled=True)
    pack = jnp.sum(pack.astype(f32), axis=0).reshape(-1)

    late_rest, last_tick = late.rest("merge_late", [pack])
    late = line_sum(late_rest)
    late = [
        jnp.concatenate([late[late_cuts[k] : late_cuts[k + 1]] for k in (side, side + 2)], axis=0)
        for side in (1, 0)
    ]
    first_a, second_a = FF // D * top + top, (FF // D + 1) * rows
    cuts = [FF // D * top, first_a, first_a + FF // D * (rows - top), second_a]

    def spread_out(value):
        low = value[: cuts[0]].reshape(-1, top, HALF)
        high = value[cuts[1] : cuts[2]].reshape(-1, rows - top, HALF)
        return jnp.concatenate(
            [
                jnp.concatenate([low, high], axis=1).reshape(-1, HALF),
                value[cuts[0] : cuts[1]],
                value[cuts[2] :],
            ],
            axis=0,
        )

    early_zero = spread_out(early_zero)

    def turned(value):
        return value.swapaxes(-1, -2).reshape(1, -1, value.shape[-2])

    full = swapped([early_zero, one["all"]])[0]()
    full_in = swapped(late)[0]()
    down_rows = rows * (FF // D)
    edges = [down_rows, down_rows + rows]
    down = full[:, : edges[0]].reshape(2, FF // D, rows, HALF)
    taken = [0]

    def part(height, cols):
        begin = taken[0]
        taken[0] += height * cols
        return pack[begin : begin + height * cols].reshape(1, height, cols)

    vecs = part(7, rows)
    mixes = part(5, wide_rows)
    d_up_bias = part(1, ff_rows)
    d_last = part(FILT, rows)
    d_net = part(EMB + 2 + FILT, FILT)
    penalty = jnp.sum(part(1, 2))
    return (
        outputs(last_tick)[None, :, None],
        in_grads(last_tick)[None, :, None],
        vecs[:, 0:2],
        vecs[:, 2:6],
        turned(full_in),
        mixes,
        d_net[:, :EMB],
        d_net[:, EMB : EMB + 2],
        d_net[:, EMB + 2 :],
        d_last,
        vecs[:, 6:7],
        turned(full[:, edges[0] : edges[1]]),
        turned(full[:, edges[1] :]),
        d_up_bias,
        turned(down),
        penalty,
    )


def solution(mesh):
    by_section = P("section")
    shard = P("section", None, ("dp", "seq"))
    tokens = P("section", None, "dp", "seq", None)
    return jax.shard_map(
        local,
        mesh=mesh,
        in_specs=(P(None, "dp", "seq", None), P(None, "dp", "seq", None), P(None, "dp", None))
        + (by_section,) * 13,
        out_specs=(tokens, tokens, shard, shard, shard, shard)
        + (by_section,) * 3
        + (shard,) * 6
        + (P(),),
        check_vma=False,
    )
```
